32 devices in a mesh: dp: 16 (over z, y, x), tensor: 2 (over core).
Axes of the slice: x: 2, y: 2, z: 4, core: 2. Of those that a mesh axis runs over, the one named last changes fastest.
Arguments:
- frames: bfloat16 [16, 1536, 768], P('dp'), may hold values from -6 to 6
- lengths: int32 [16], P('dp'), may hold values from 192 to 1536, as said below
- cotangent: bfloat16 [16, 1536, 768], P('dp'), may hold values from -6 to 6
- norm1_gain: float32 [768], replicated, may hold values from 0.1 to 1.9
- norm1_bias: float32 [768], replicated, may hold values from -3 to 3
- query_weight: bfloat16 [768, 768], P(None, 'tensor'), may hold values from -0.21875 to 0.21875
- query_bias: float32 [768], P('tensor'), may hold values from -3 to 3
- key_weight: bfloat16 [768, 768], P(None, 'tensor'), may hold values from -0.21875 to 0.21875
- value_weight: bfloat16 [768, 768], P(None, 'tensor'), may hold values from -0.21875 to 0.21875
- value_bias: float32 [768], P('tensor'), may hold values from -3 to 3
- output_weight: bfloat16 [768, 768], P('tensor'), may hold values from -0.875 to 0.875
- output_bias: float32 [768], replicated, may hold values from -3 to 3
- norm2_gain: float32 [768], replicated, may hold values from 0.1 to 1.9
- norm2_bias: float32 [768], replicated, may hold values from -3 to 3
- hidden_weight: bfloat16 [768, 3072], P(None, 'tensor'), may hold values from -0.21875 to 0.21875
- hidden_bias: float32 [3072], P('tensor'), may hold values from -3 to 3
- proj_weight: bfloat16 [3072, 768], P('tensor'), may hold values from -0.15625 to 0.15625
- proj_bias: float32 [768], replicated, may hold values from -3 to 3
Outputs:
- block_out: bfloat16 [16, 1536, 768], P('dp')
- input_grad: bfloat16 [16, 1536, 768], P('dp')
- grad_norm1_gain: float32 [768], replicated
- grad_norm1_bias: float32 [768], replicated
- grad_query_weight: float32 [768, 768], P(None, 'tensor')
- grad_query_bias: float32 [768], P('tensor')
- grad_key_weight: float32 [768, 768], P(None, 'tensor')
- grad_value_weight: float32 [768, 768], P(None, 'tensor')
- grad_value_bias: float32 [768], P('tensor')
- grad_output_weight: float32 [768, 768], P('tensor')
- grad_output_bias: float32 [768], replicated
- grad_norm2_gain: float32 [768], replicated
- grad_norm2_bias: float32 [768], replicated
- grad_hidden_weight: float32 [768, 3072], P(None, 'tensor')
- grad_hidden_bias: float32 [3072], P('tensor')
- grad_proj_weight: float32 [3072, 768], P('tensor')
- grad_proj_bias: float32 [768], replicated
The draws below stay inside these ranges and needn't reach their ends.
Inputs may be any that keep to these rules, and one draw needn't show every extreme that they name: `lengths`: valid frames of each clip; positions at or beyond it are padding that no key attention reads and that carry no loss; some clip has exactly 1536.
All inputs are finite; a program needn't handle non-finite values.
Results may differ from the reference program's by a relative error of at most 0.013.
The reference program's roundings to bfloat16 on the way count: a program that leaves them out, or rounds other values in their place, can miss the bound.
Values sent between devices are 32-bit elements; how exact they have to be, the bound alone decides.
A program may use at most 192 MiB of HBM per device.

```python
import math
import jax
import jax.numpy as jnp
from jax import lax

D = 768
FF = 3072
HD = 64
LEN = 1536
CLIPS = 16


def draw_lengths(key, part):
    key = jax.random.fold_in(key, 11)
    first_key, second_key, chosen_key = jax.random.split(key, 3)
    first = jax.random.randint(first_key, (CLIPS,), 0, LEN + 1)
    second = jax.random.randint(second_key, (CLIPS,), 0, LEN + 1)
    shortest = jnp.maximum(jnp.minimum(first, second), max(1, LEN // 8))
    chosen = jax.random.randint(chosen_key, (), 0, CLIPS)
    return jnp.where(jnp.arange(CLIPS) == chosen, LEN, shortest).astype(jnp.int32)


def level_of(own_key, extent, cuts, smallest, largest):
    gain = 1.0
    for axis_at, shards_of in cuts:
        heights = jax.random.uniform(jax.random.fold_in(jax.random.fold_in(own_key, 6), axis_at), (shards_of,), jnp.float32, smallest / len(cuts), largest / len(cuts))
        gain = gain * jnp.repeat(jnp.exp(heights), extent[axis_at] // shards_of).reshape((-1,) + (1,) * (len(extent) - 1 - axis_at))
    return gain


def normal_values(own_key, dims, spread, reach, cuts=(), kind=jnp.bfloat16):
    loudness = level_of(own_key, dims, cuts, -0.22, 0.18) if cuts else 1.0
    array = jax.random.normal(own_key, dims, jnp.float32) * spread * loudness
    return jnp.minimum(jnp.maximum(array, -reach), reach).astype(kind)


def setup_inputs(seed: int = 0) -> dict:
    streams_of = jax.random.split(jax.random.key(seed), 19)
    frames = normal_values(streams_of[0], (CLIPS, LEN, D), 1.0, 6.0, ((0, 16),))
    lengths = draw_lengths(jax.random.fold_in(streams_of[18], 71), 0)
    cotangent = normal_values(streams_of[2], (CLIPS, LEN, D), 1.0, 6.0, ((0, 16),))
    norm1_gain = jnp.clip(1.0 + 0.18 * jax.random.normal(streams_of[3], (D,), jnp.float32), 0.1, 1.9)
    norm1_bias = normal_values(streams_of[4], (D,), 0.5, 3.0, (), jnp.float32)
    query_weight = normal_values(streams_of[5], (D, D), D ** -0.5, 0.21875, ((1, 2),))
    query_bias = normal_values(streams_of[6], (D,), 0.5, 3.0, ((0, 2),), jnp.float32)
    key_weight = normal_values(streams_of[7], (D, D), D ** -0.5, 0.21875, ((1, 2),))
    value_weight = normal_values(streams_of[8], (D, D), D ** -0.5, 0.21875, ((1, 2),))
    value_bias = normal_values(streams_of[9], (D,), 0.5, 3.0, ((0, 2),), jnp.float32)
    output_weight = normal_values(streams_of[10], (D, D), (D // 16) ** -0.5, 0.875, ((0, 2),))
    output_bias = normal_values(streams_of[11], (D,), 0.5, 3.0, (), jnp.float32)
    norm2_gain = jnp.clip(1.0 + 0.18 * jax.random.normal(streams_of[12], (D,), jnp.float32), 0.1, 1.9)
    norm2_bias = normal_values(streams_of[13], (D,), 0.5, 3.0, (), jnp.float32)
    hidden_weight = normal_values(streams_of[14], (D, FF), D ** -0.5, 0.21875, ((1, 2),))
    hidden_bias = normal_values(streams_of[15], (FF,), 0.5, 3.0, ((0, 2),), jnp.float32)
    proj_weight = normal_values(streams_of[16], (FF, D), (FF // 2) ** -0.5, 0.15625, ((0, 2),))
    proj_bias = normal_values(streams_of[17], (D,), 0.5, 3.0, (), jnp.float32)
    return {"frames": frames, "lengths": lengths, "cotangent": cotangent, "norm1_gain": norm1_gain, "norm1_bias": norm1_bias, "query_weight": query_weight, "query_bias": query_bias, "key_weight": key_weight, "value_weight": value_weight, "value_bias": value_bias, "output_weight": output_weight, "output_bias": output_bias, "norm2_gain": norm2_gain, "norm2_bias": norm2_bias, "hidden_weight": hidden_weight, "hidden_bias": hidden_bias, "proj_weight": proj_weight, "proj_bias": proj_bias}


eps = 1e-05
score_scale = 0.125
masked_value = -1e+30

def contract(form, left, right):
    return jnp.einsum(form, left.astype(jnp.float32), right.astype(jnp.float32))

def layer_norm(values_in, norm_gain, norm_shift):
    center = values_in - lax.optimization_barrier(jnp.mean(values_in, axis=-1, keepdims=True))
    inverse = lax.rsqrt(lax.optimization_barrier(jnp.mean(center * center, axis=-1, keepdims=True)) + eps)
    unit_rows = center * inverse
    return (unit_rows * norm_gain + norm_shift, unit_rows, inverse)

def norm_back(grad_rows, unit_rows, inverse, norm_gain):
    scaled = grad_rows * norm_gain
    return inverse * (scaled - lax.optimization_barrier(jnp.mean(scaled, axis=-1, keepdims=True)) - unit_rows * lax.optimization_barrier(jnp.mean(scaled * unit_rows, axis=-1, keepdims=True)))

def gelu_parts(before):
    normal_cdf = 0.5 * (1.0 + jax.scipy.special.erf(before * (1.0 / math.sqrt(2.0))))
    return (before * normal_cdf, normal_cdf + before * jnp.exp(-0.5 * before * before) * (1.0 / math.sqrt(2.0 * math.pi)))

def attend_forward(queries, keys_in, values_in, clip_length):
    total_rows, head_count, head_size = queries.shape
    block_rows = min(512, total_rows)
    live_keys = jnp.arange(total_rows) < clip_length

    def per_block(query_block):
        scores = contract('qhd,khd->hqk', query_block, keys_in)
        scores = jnp.where(live_keys[None, None, :], scores, masked_value)
        maxima = lax.optimization_barrier(jnp.max(scores, axis=-1, keepdims=True))
        exponent = jnp.exp(scores - maxima)
        totals = lax.optimization_barrier(jnp.sum(exponent, axis=-1, keepdims=True))
        weights = (exponent / totals).astype(jnp.bfloat16)
        mixture = contract('hqk,khd->qhd', weights, values_in).astype(jnp.bfloat16)
        return (mixture, (maxima + jnp.log(totals))[..., 0])
    mixture, log_sums = lax.map(per_block, queries.reshape(total_rows // block_rows, block_rows, head_count, head_size))
    return (mixture.reshape(total_rows, head_count, head_size), log_sums)

def attend_backward(queries, keys_in, values_in, attended, grad_attended, log_sums, clip_length):
    total_rows, head_count, head_size = queries.shape
    block_rows = min(512, total_rows)
    blocks = total_rows // block_rows
    live_keys = jnp.arange(total_rows) < clip_length
    deltas = lax.optimization_barrier(jnp.sum(grad_attended.astype(jnp.float32) * attended.astype(jnp.float32), axis=-1))

    def per_block(carry, inputs):
        query_block, grad_block, delta_block, log_block = inputs
        scores = contract('qhd,khd->hqk', query_block, keys_in)
        scores = jnp.where(live_keys[None, None, :], scores, masked_value)
        probs = jnp.exp(scores - log_block[..., None])
        grad_probs = contract('qhd,khd->hqk', grad_block, values_in)
        grad_scores = (probs * (grad_probs - jnp.transpose(delta_block)[..., None])).astype(jnp.bfloat16)
        grad_query = contract('hqk,khd->qhd', grad_scores, keys_in) * score_scale
        grad_keys = carry[0] + contract('hqk,qhd->khd', grad_scores, query_block)
        grad_values = carry[1] + contract('hqk,qhd->khd', probs.astype(jnp.bfloat16), grad_block)
        return ((grad_keys, grad_values), grad_query)
    start = jnp.zeros((total_rows, head_count, head_size), jnp.float32)
    (grad_keys, grad_values), grad_query = lax.scan(per_block, (start, start), (queries.reshape(blocks, block_rows, head_count, head_size), grad_attended.reshape(blocks, block_rows, head_count, head_size), deltas.reshape(blocks, block_rows, head_count), log_sums))
    return (grad_query.reshape(total_rows, head_count, head_size), grad_keys, grad_values)

def mat_dot(left, right):
    return jnp.dot(left, right, preferred_element_type=jnp.float32)

def clip_pass(params, frame_clip, grad_raw, clip_length):
    norm1_gain, norm1_bias, query_weight, query_bias, key_weight, value_weight, value_bias, output_weight, output_bias, norm2_gain, norm2_bias, hidden_weight, hidden_bias, proj_weight, proj_bias = params
    total_rows = frame_clip.shape[0]
    head_count = query_weight.shape[1] // HD
    inputs_f = frame_clip.astype(jnp.float32)
    normed_one, unit_one, inverse_one = layer_norm(inputs_f, norm1_gain, norm1_bias)
    first_in = normed_one.astype(jnp.bfloat16)
    queries = ((mat_dot(first_in, query_weight) + query_bias) * score_scale).astype(jnp.bfloat16)
    keys_in = mat_dot(first_in, key_weight).astype(jnp.bfloat16)
    values_in = (mat_dot(first_in, value_weight) + value_bias).astype(jnp.bfloat16)
    head_shape = (total_rows, head_count, HD)
    attended, log_sums = attend_forward(queries.reshape(head_shape), keys_in.reshape(head_shape), values_in.reshape(head_shape), clip_length)
    attended_flat = attended.reshape(total_rows, head_count * HD)
    resid = inputs_f + mat_dot(attended_flat, output_weight) + output_bias
    normed_two, unit_two, inverse_two = layer_norm(resid, norm2_gain, norm2_bias)
    second_in = normed_two.astype(jnp.bfloat16)
    before = mat_dot(second_in, hidden_weight) + hidden_bias
    active_f, slope = gelu_parts(before)
    active = active_f.astype(jnp.bfloat16)
    block_out = (resid + mat_dot(active, proj_weight) + proj_bias).astype(jnp.bfloat16)
    live_rows = (jnp.arange(total_rows) < clip_length)[:, None]
    grad_clip = jnp.where(live_rows, grad_raw, jnp.zeros_like(grad_raw))
    grad_f = grad_clip.astype(jnp.float32)
    g_proj_b = lax.optimization_barrier(jnp.sum(grad_f, axis=0))
    g_proj_w = mat_dot(active.T, grad_clip)
    grad_pre = mat_dot(grad_clip, proj_weight.T) * slope
    g_hidden_b = lax.optimization_barrier(jnp.sum(grad_pre, axis=0))
    grad_pre_b = grad_pre.astype(jnp.bfloat16)
    g_hidden_w = mat_dot(second_in.T, grad_pre_b)
    grad_two = mat_dot(grad_pre_b, hidden_weight.T)
    g_norm2_gain = lax.optimization_barrier(jnp.sum(grad_two * unit_two, axis=0))
    g_norm2_bias = lax.optimization_barrier(jnp.sum(grad_two, axis=0))
    grad_resid = grad_f + norm_back(grad_two, unit_two, inverse_two, norm2_gain)
    g_output_b = lax.optimization_barrier(jnp.sum(grad_resid, axis=0))
    grad_resid_b = grad_resid.astype(jnp.bfloat16)
    g_output_w = mat_dot(attended_flat.T, grad_resid_b)
    grad_attended = mat_dot(grad_resid_b, output_weight.T).astype(jnp.bfloat16)
    grad_query, grad_key, grad_value = attend_backward(queries.reshape(head_shape), keys_in.reshape(head_shape), values_in.reshape(head_shape), attended, grad_attended.reshape(head_shape), log_sums, clip_length)
    grad_query = grad_query.reshape(total_rows, head_count * HD)
    grad_key = grad_key.reshape(total_rows, head_count * HD)
    grad_value = grad_value.reshape(total_rows, head_count * HD)
    g_query_b = lax.optimization_barrier(jnp.sum(grad_query, axis=0))
    g_value_b = lax.optimization_barrier(jnp.sum(grad_value, axis=0))
    query_g_b = grad_query.astype(jnp.bfloat16)
    key_g_b = grad_key.astype(jnp.bfloat16)
    value_g_b = grad_value.astype(jnp.bfloat16)
    g_query_w = mat_dot(first_in.T, query_g_b)
    g_key_w = mat_dot(first_in.T, key_g_b)
    g_value_w = mat_dot(first_in.T, value_g_b)
    grad_one = mat_dot(query_g_b, query_weight.T) + mat_dot(key_g_b, key_weight.T) + mat_dot(value_g_b, value_weight.T)
    g_norm1_gain = lax.optimization_barrier(jnp.sum(grad_one * unit_one, axis=0))
    g_norm1_bias = lax.optimization_barrier(jnp.sum(grad_one, axis=0))
    input_grad = (grad_resid + norm_back(grad_one, unit_one, inverse_one, norm1_gain)).astype(jnp.bfloat16)
    grads = (g_norm1_gain, g_norm1_bias, g_query_w, g_query_b, g_key_w, g_value_w, g_value_b, g_output_w, g_output_b, g_norm2_gain, g_norm2_bias, g_hidden_w, g_hidden_b, g_proj_w, g_proj_b)
    return (block_out, input_grad, grads)

def reference(frames, lengths, cotangent, norm1_gain, norm1_bias, query_weight, query_bias, key_weight, value_weight, value_bias, output_weight, output_bias, norm2_gain, norm2_bias, hidden_weight, hidden_bias, proj_weight, proj_bias):
    params = (norm1_gain, norm1_bias, query_weight, query_bias, key_weight, value_weight, value_bias, output_weight, output_bias, norm2_gain, norm2_bias, hidden_weight, hidden_bias, proj_weight, proj_bias)
    zero_grads = jax.tree.map(lambda weight: jnp.zeros(weight.shape, jnp.float32), params)

    def per_clip(carry, inputs):
        frame_clip, grad_clip, clip_length = inputs
        block_out, input_grad, grads = clip_pass(params, frame_clip, grad_clip, clip_length)
        return (jax.tree.map(jnp.add, carry, grads), (block_out, input_grad))
    totals, (block_out, input_grad) = lax.scan(per_clip, zero_grads, (frames, cotangent, lengths.astype(jnp.int32)))
    g_norm1_gain, g_norm1_bias, g_query_w, g_query_b, g_key_w, g_value_w, g_value_b, g_output_w, g_output_b, g_norm2_gain, g_norm2_bias, g_hidden_w, g_hidden_b, g_proj_w, g_proj_b = totals
    return (block_out, input_grad, g_norm1_gain, g_norm1_bias, g_query_w, g_query_b, g_key_w, g_value_w, g_value_b, g_output_w, g_output_b, g_norm2_gain, g_norm2_bias, g_hidden_w, g_hidden_b, g_proj_w, g_proj_b)
```

```python
import functools
import math

import jax
import jax.numpy as jnp
from jax import lax
from jax.experimental import pallas as pl
from jax.experimental.pallas import tpu as pltpu
from jax.sharding import PartitionSpec as P

HD = 64


eps = 1e-05
score_scale = 0.125
masked_value = -1e30


def contract(form, left, right):
    return jnp.einsum(form, left, right, preferred_element_type=jnp.float32)


def mat_dot(left, right):
    return jnp.dot(left, right, preferred_element_type=jnp.float32)


def layer_norm(values_in, norm_gain, norm_shift):
    center = values_in - jnp.mean(values_in, axis=-1, keepdims=True)
    inverse = lax.rsqrt(jnp.mean(center * center, axis=-1, keepdims=True) + eps)
    unit_rows = center * inverse
    return (unit_rows * norm_gain + norm_shift, unit_rows, inverse)


def norm_back(grad_rows, unit_rows, inverse, norm_gain):
    scaled = grad_rows * norm_gain
    return inverse * (
        scaled
        - jnp.mean(scaled, axis=-1, keepdims=True)
        - unit_rows * jnp.mean(scaled * unit_rows, axis=-1, keepdims=True)
    )


def gelu_parts(before):
    normal_cdf = 0.5 * (1.0 + jax.scipy.special.erf(before * (1.0 / math.sqrt(2.0))))
    return (
        before * normal_cdf,
        normal_cdf + before * jnp.exp(-0.5 * before * before) * (1.0 / math.sqrt(2.0 * math.pi)),
    )


def attend_forward(queries, keys_in, values_in, clip_length):
    total_rows, head_count, head_size = queries.shape
    block_rows = min(512, total_rows)
    live_keys = jnp.arange(total_rows) < clip_length

    def per_block(query_block):
        scores = contract("qhd,khd->hqk", query_block, keys_in)
        scores = jnp.where(live_keys[None, None, :], scores, masked_value)
        maxima = jnp.max(scores, axis=-1, keepdims=True)
        exponent = jnp.exp(scores - maxima)
        totals = jnp.sum(exponent, axis=-1, keepdims=True)
        weights = (exponent / totals).astype(jnp.bfloat16)
        mixture = contract("hqk,khd->qhd", weights, values_in).astype(jnp.bfloat16)
        return (mixture, (maxima + jnp.log(totals))[..., 0])

    mixture, log_sums = lax.map(
        per_block, queries.reshape(total_rows // block_rows, block_rows, head_count, head_size)
    )
    return (mixture.reshape(total_rows, head_count, head_size), log_sums)


def attend_backward(queries, keys_in, values_in, attended, grad_attended, log_sums, clip_length):
    total_rows, head_count, head_size = queries.shape
    block_rows = min(512, total_rows)
    blocks = total_rows // block_rows
    live_keys = jnp.arange(total_rows) < clip_length
    deltas = jnp.sum(grad_attended.astype(jnp.float32) * attended.astype(jnp.float32), axis=-1)

    def per_block(carry, inputs):
        query_block, grad_block, delta_block, log_block = inputs
        scores = contract("qhd,khd->hqk", query_block, keys_in)
        scores = jnp.where(live_keys[None, None, :], scores, masked_value)
        probs = jnp.exp(scores - log_block[..., None])
        grad_probs = contract("qhd,khd->hqk", grad_block, values_in)
        grad_scores = (probs * (grad_probs - jnp.transpose(delta_block)[..., None])).astype(
            jnp.bfloat16
        )
        grad_query = contract("hqk,khd->qhd", grad_scores, keys_in) * score_scale
        grad_keys = carry[0] + contract("hqk,qhd->khd", grad_scores, query_block)
        grad_values = carry[1] + contract("hqk,qhd->khd", probs.astype(jnp.bfloat16), grad_block)
        return ((grad_keys, grad_values), grad_query)

    start = jnp.zeros((total_rows, head_count, head_size), jnp.float32)
    (grad_keys, grad_values), grad_query = lax.scan(
        per_block,
        (start, start),
        (
            queries.reshape(blocks, block_rows, head_count, head_size),
            grad_attended.reshape(blocks, block_rows, head_count, head_size),
            deltas.reshape(blocks, block_rows, head_count),
            log_sums,
        ),
    )
    return (grad_query.reshape(total_rows, head_count, head_size), grad_keys, grad_values)


MESH_ID = pl.DeviceIdType.MESH


def bit_of(index, bit):
    return (index // bit) % 2


def partner_of(index, bit):
    return index + bit - 2 * bit * bit_of(index, bit)


class Unit:
    def __init__(self, buffer, total, place, order, extra, landing, sems, me, core):
        row, rows, col, cols = place
        send_sem, recv_sems, own_sem = sems
        self.buffer, self.total, self.landing = buffer, total, landing
        self.columns = pl.ds(col, cols)
        self.rows = rows
        self.order, self.extra = order, extra
        self.send_sem, self.recv_sems, self.own_sem = send_sem, recv_sems, own_sem
        self.me, self.core = me, core
        self.last = None
        self.offsets = [row]
        self.lands = [0]
        for step, bit in enumerate(order):
            self.offsets.append(self.offsets[-1] + bit_of(me, bit) * (rows >> (step + 1)))
            self.lands.append(self.lands[-1] + (rows >> (step + 1)))
        self.stages = 2 * len(order) + len(extra)

    def part(self, array, offset, length):
        return array.at[pl.ds(pl.multiple_of(offset, 8), length), self.columns]

    def own_copy(self):
        length = self.rows >> len(self.order)
        return pltpu.make_async_copy(
            self.part(self.buffer, self.offsets[-1], length),
            self.part(self.total, self.offsets[-1], length),
            self.own_sem,
        )

    def copy(self, stage):
        halvings = len(self.order)
        doublings = len(self.extra)
        if stage < halvings:
            bit = self.order[stage]
            length = self.rows >> (stage + 1)
            source = self.part(self.buffer, self.offsets[stage] + (1 - bit_of(self.me, bit)) * length, length)
            target = self.landing.at[pl.ds(self.lands[stage], length), :]
        elif stage < halvings + doublings:
            bit = self.extra[stage - halvings]
            length = self.rows >> halvings
            source = self.part(self.buffer, self.offsets[-1], length)
            target = self.landing.at[pl.ds(self.lands[-1] + (stage - halvings) * length, length), :]
        else:
            step = 2 * halvings + doublings - 1 - stage
            bit = self.order[step]
            length = self.rows >> (step + 1)
            target = self.part(self.total, self.offsets[step + 1], length)
            source = target
            if step == halvings - 1:
                source = self.part(self.buffer, self.offsets[step + 1], length)
        return pltpu.make_async_remote_copy(
            src_ref=source,
            dst_ref=target,
            send_sem=self.send_sem,
            recv_sem=self.recv_sems.at[stage],
            device_id=(partner_of(self.me, bit), self.core),
            device_id_type=MESH_ID,
        )

    def advance(self, stage):
        halvings = len(self.order)
        doublings = len(self.extra)
        if stage > 0:
            self.last.wait()
            if stage <= halvings + doublings:
                step = min(stage, halvings)
                length = self.rows >> step
                if stage <= halvings:
                    land = self.lands[stage - 1]
                else:
                    land = self.lands[-1] + (stage - 1 - halvings) * length
                index = (pl.ds(pl.multiple_of(self.offsets[step], 8), length), self.columns)
                self.buffer[index] = self.buffer[index] + self.landing[pl.ds(land, length), :]
            if stage == halvings + doublings:
                self.own_copy().start()
            if stage == halvings + doublings + 1:
                self.own_copy().wait()
        if stage < self.stages:
            self.last = self.copy(stage)
            self.last.start()


def dp_bits(size):
    return [1 << power for power in range(size.bit_length() - 1)]


def orders_of(size):
    bits = dp_bits(size)
    a, b, c, d = bits[:4]
    return [[a, b, c, d], [b, a, c, d], [c, a, b, d], [c, b, a, d]], bits[4:]


def landing_rows(rows, extra):
    return rows - (rows >> 4) + len(extra) * (rows >> 4)


def gradient_places():
    waves = []
    for j in range(3):
        waves.append([(4, (512 * j, 512, 256 * c, 256), 0) for c in range(3)])
        waves.append([(5, (256 * c, 256, 512 * j, 512), 1) for c in range(3)])
    for j in range(3):
        waves.append([(j, (256 * c, 256, 0, 384), 2) for c in range(3)])
    waves.append([(3, (0, 384, 256 * c, 256), 3) for c in range(3)])
    return waves


def sum_kernel(size, *refs):
    sources, totals = refs[:7], refs[7:14]
    landings, (send_sems, recv_sems, own_sems) = refs[14:19], refs[19:22]
    held = refs[22:]
    me, core = lax.axis_index("dp"), lax.axis_index("tensor")
    barrier = pltpu.get_barrier_semaphore()
    bits = dp_bits(size)
    for bit in bits:
        pl.semaphore_signal(
            barrier, inc=1, device_id=(partner_of(me, bit), core), device_id_type=MESH_ID
        )
    pl.semaphore_wait(barrier, len(bits))
    orders, spare = orders_of(size)
    for at, source in enumerate(sources):
        pltpu.make_async_copy(source, held[at], own_sems.at[at]).start()
    for at, source in enumerate(sources):
        pltpu.make_async_copy(source, held[at], own_sems.at[at]).wait()
    used = [0] * 5
    waves = []
    number = 0
    for at, places in enumerate(gradient_places() + [[(6, (0, 128, 0, 128), 4)]]):
        wave = []
        for kind, (which, place, shelf) in enumerate(places):
            order = orders[kind] if kind < 2 else orders[2 + at % 2]
            landing = landings[shelf].at[used[shelf]]
            used[shelf] += 1
            wave.append(
                Unit(
                    held[which], totals[which], place, order, spare, landing,
                    (send_sems.at[number], recv_sems.at[number], own_sems.at[number]), me, core,
                )
            )
            number += 1
        waves.append(wave)
    last = waves[0][0].stages
    for tick in range(len(waves) + last):
        for at, wave in enumerate(waves):
            if 0 <= tick - at <= last:
                for unit in wave:
                    unit.advance(tick - at)


def sum_over_dp(size, arrays):
    spare = orders_of(size)[1]
    stages = 8 + len(spare)
    shelves = [(9, 512, 256), (9, 256, 512), (9, 256, 384), (3, 384, 256), (1, 128, 128)]
    return pl.pallas_call(
        functools.partial(sum_kernel, size),
        out_shape=[jax.ShapeDtypeStruct(array.shape, jnp.float32) for array in arrays],
        in_specs=[pl.BlockSpec(memory_space=pl.ANY)] * 7,
        out_specs=[pl.BlockSpec(memory_space=pl.ANY)] * 7,
        scratch_shapes=[
            pltpu.VMEM((count, landing_rows(rows, spare), cols), jnp.float32)
            for count, rows, cols in shelves
        ]
        + [
            pltpu.SemaphoreType.DMA((31,)),
            pltpu.SemaphoreType.DMA((31, stages)),
            pltpu.SemaphoreType.DMA((31,)),
        ]
        + [pltpu.VMEM(array.shape, jnp.float32) for array in arrays],
        compiler_params=pltpu.CompilerParams(
            collective_id=0, has_side_effects=True, vmem_limit_bytes=60 * 2**20
        ),
        name="sum_over_dp",
    )(*arrays)


SMALL_ROWS, SMALL_COLS = 128, 128


def pack_small(vectors):
    flat = jnp.concatenate(vectors)
    flat = jnp.pad(flat, (0, SMALL_ROWS * SMALL_COLS - flat.shape[0]))
    return flat.reshape(SMALL_ROWS, SMALL_COLS)


def unpack_small(packed, vectors):
    flat = packed.reshape(-1)
    out, at = [], 0
    for vector in vectors:
        out.append(lax.slice(flat, (at,), (at + vector.shape[0],)))
        at += vector.shape[0]
    return out


def on_device(
    size,
    frames,
    lengths,
    cotangent,
    norm1_gain,
    norm1_bias,
    query_weight,
    query_bias,
    key_weight,
    value_weight,
    value_bias,
    output_weight,
    output_bias,
    norm2_gain,
    norm2_bias,
    hidden_weight,
    hidden_bias,
    proj_weight,
    proj_bias,
):
    clip_length = lengths[0]
    total_rows = frames.shape[1]
    head_count = query_weight.shape[1] // HD
    head_shape = (total_rows, head_count, HD)
    inputs_f = frames[0].astype(jnp.float32)
    normed_one, unit_one, inverse_one = layer_norm(inputs_f, norm1_gain, norm1_bias)
    first_in = normed_one.astype(jnp.bfloat16)
    queries = ((mat_dot(first_in, query_weight) + query_bias) * score_scale).astype(jnp.bfloat16)
    keys_in = mat_dot(first_in, key_weight).astype(jnp.bfloat16)
    values_in = (mat_dot(first_in, value_weight) + value_bias).astype(jnp.bfloat16)
    attended, log_sums = attend_forward(
        queries.reshape(head_shape),
        keys_in.reshape(head_shape),
        values_in.reshape(head_shape),
        clip_length,
    )
    attended_flat = attended.reshape(total_rows, head_count * HD)
    attn_total = lax.psum(mat_dot(attended_flat, output_weight), "tensor")
    resid = inputs_f + attn_total + output_bias
    normed_two, unit_two, inverse_two = layer_norm(resid, norm2_gain, norm2_bias)
    second_in = normed_two.astype(jnp.bfloat16)
    before = mat_dot(second_in, hidden_weight) + hidden_bias
    active_f, slope = gelu_parts(before)
    active = active_f.astype(jnp.bfloat16)
    mlp_total = lax.psum(mat_dot(active, proj_weight), "tensor")
    block_out = (resid + mlp_total + proj_bias).astype(jnp.bfloat16)
    live_rows = (jnp.arange(total_rows) < clip_length)[:, None]
    grad_raw = cotangent[0]
    grad_clip = jnp.where(live_rows, grad_raw, jnp.zeros_like(grad_raw))
    grad_f = grad_clip.astype(jnp.float32)
    g_proj_b = jnp.sum(grad_f, axis=0)
    g_proj_w = mat_dot(active.T, grad_clip)
    grad_pre = mat_dot(grad_clip, proj_weight.T) * slope
    g_hidden_b = jnp.sum(grad_pre, axis=0)
    grad_pre_b = grad_pre.astype(jnp.bfloat16)
    g_hidden_w = mat_dot(second_in.T, grad_pre_b)
    grad_two = lax.psum(mat_dot(grad_pre_b, hidden_weight.T), "tensor")
    g_norm2_gain = jnp.sum(grad_two * unit_two, axis=0)
    g_norm2_bias = jnp.sum(grad_two, axis=0)
    grad_resid = grad_f + norm_back(grad_two, unit_two, inverse_two, norm2_gain)
    g_output_b = jnp.sum(grad_resid, axis=0)
    grad_resid_b = grad_resid.astype(jnp.bfloat16)
    g_output_w = mat_dot(attended_flat.T, grad_resid_b)
    grad_attended = mat_dot(grad_resid_b, output_weight.T).astype(jnp.bfloat16)
    grad_query, grad_key, grad_value = attend_backward(
        queries.reshape(head_shape),
        keys_in.reshape(head_shape),
        values_in.reshape(head_shape),
        attended,
        grad_attended.reshape(head_shape),
        log_sums,
        clip_length,
    )
    grad_query = grad_query.reshape(total_rows, head_count * HD)
    grad_key = grad_key.reshape(total_rows, head_count * HD)
    grad_value = grad_value.reshape(total_rows, head_count * HD)
    g_query_b = jnp.sum(grad_query, axis=0)
    g_value_b = jnp.sum(grad_value, axis=0)
    query_g_b = grad_query.astype(jnp.bfloat16)
    key_g_b = grad_key.astype(jnp.bfloat16)
    value_g_b = grad_value.astype(jnp.bfloat16)
    g_query_w = mat_dot(first_in.T, query_g_b)
    g_key_w = mat_dot(first_in.T, key_g_b)
    g_value_w = mat_dot(first_in.T, value_g_b)
    partial_one = (
        mat_dot(query_g_b, query_weight.T)
        + mat_dot(key_g_b, key_weight.T)
        + mat_dot(value_g_b, value_weight.T)
    )
    grad_one = lax.psum(partial_one, "tensor")
    g_norm1_gain = jnp.sum(grad_one * unit_one, axis=0)
    g_norm1_bias = jnp.sum(grad_one, axis=0)
    input_grad = (grad_resid + norm_back(grad_one, unit_one, inverse_one, norm1_gain)).astype(
        jnp.bfloat16
    )
    small = [
        g_norm1_gain, g_norm1_bias, g_query_b, g_value_b, g_output_b,
        g_norm2_gain, g_norm2_bias, g_hidden_b, g_proj_b,
    ]
    summed = sum_over_dp(
        size, [g_query_w, g_key_w, g_value_w, g_output_w, g_proj_w, g_hidden_w, pack_small(small)]
    )
    s_query_w, s_key_w, s_value_w, s_output_w, s_proj_w, s_hidden_w, packed = summed
    (
        s_norm1_gain, s_norm1_bias, s_query_b, s_value_b, s_output_b,
        s_norm2_gain, s_norm2_bias, s_hidden_b, s_proj_b,
    ) = unpack_small(packed, small)
    return (
        block_out[None],
        input_grad[None],
        s_norm1_gain,
        s_norm1_bias,
        s_query_w,
        s_query_b,
        s_key_w,
        s_value_w,
        s_value_b,
        s_output_w,
        s_output_b,
        s_norm2_gain,
        s_norm2_bias,
        s_hidden_w,
        s_hidden_b,
        s_proj_w,
        s_proj_b,
    )


def solution(mesh):
    placed = (
        P("dp", None, None),
        P("dp"),
        P("dp", None, None),
        P(),
        P(),
        P(None, "tensor"),
        P("tensor"),
        P(None, "tensor"),
        P(None, "tensor"),
        P("tensor"),
        P("tensor", None),
        P(),
        P(),
        P(),
        P(None, "tensor"),
        P("tensor"),
        P("tensor", None),
        P(),
    )
    return jax.shard_map(
        functools.partial(on_device, mesh.shape["dp"]),
        mesh=mesh,
        in_specs=placed,
        out_specs=(
            P("dp", None, None),
            P("dp", None, None),
            P(),
            P(),
            P(None, "tensor"),
            P("tensor"),
            P(None, "tensor"),
            P(None, "tensor"),
            P("tensor"),
            P("tensor", None),
            P(),
            P(),
            P(),
            P(None, "tensor"),
            P("tensor"),
            P("tensor", None),
            P(),
        ),
        check_vma=False,
    )
```

```python
import functools
import heapq
import math

import jax
import jax.numpy as jnp
from jax import lax
from jax.experimental import pallas as pl
from jax.experimental.pallas import tpu as pltpu
from jax.sharding import PartitionSpec as P

HD = 64
PAIR = 2 * HD
CHUNK = 512
BLOCK = 512
PIECE = 256

eps = 1e-05
score_scale = 0.125
masked_value = -1e30

MESH_ID = pl.DeviceIdType.MESH
NN = (((1,), (0,)), ((), ()))
NT = (((1,), (1,)), ((), ()))
TN = (((0,), (0,)), ((), ()))


def dot(left, right, form=NN):
    return lax.dot_general(left, right, form, preferred_element_type=jnp.float32)


def bit_of(index, bit):
    return (index // bit) % 2


def partner_of(index, bit):
    return index + bit - 2 * bit * bit_of(index, bit)


def dp_bits(size):
    return [1 << power for power in range(size.bit_length() - 1)]


def orders_of(size):
    bits = dp_bits(size)
    a, b, c, d = bits[:4]
    return [[a, b, c, d], [b, a, c, d], [c, a, b, d], [c, b, a, d]], bits[4:]


def landing_rows(rows, extra):
    return rows - (rows >> 4) + len(extra) * (rows >> 4)


class Unit:
    def __init__(self, buffer, total, place, shape, order, extra, landing, sems, me, core):
        (self.row, self.col), (self.total_row, self.total_col) = place
        self.rows, self.cols = shape
        self.buffer, self.total, self.landing = buffer, total, landing
        self.order, self.extra = order, extra
        self.send_sem, self.recv_sems, self.own_sem = sems
        self.me, self.core = me, core
        self.offsets = [0]
        self.lands = [0]
        for step, bit in enumerate(order):
            self.offsets.append(self.offsets[-1] + bit_of(me, bit) * (self.rows >> (step + 1)))
            self.lands.append(self.lands[-1] + (self.rows >> (step + 1)))
        self.stages = 2 * len(order) + len(extra)

    def held(self, offset, length):
        return (pl.ds(pl.multiple_of(self.row + offset, 8), length), pl.ds(self.col, self.cols))

    def final(self, offset, length):
        index = (pl.ds(pl.multiple_of(self.total_row + offset, 8), length), pl.ds(self.total_col, self.cols))
        return self.total.at[index]

    def landed(self, start, length):
        return (pl.ds(start, length), pl.ds(0, self.cols))

    def own_copy(self):
        length = self.rows >> len(self.order)
        return pltpu.make_async_copy(
            self.buffer.at[self.held(self.offsets[-1], length)],
            self.final(self.offsets[-1], length),
            self.own_sem,
        )

    def copy(self, stage):
        halvings = len(self.order)
        doublings = len(self.extra)
        if stage < halvings:
            bit = self.order[stage]
            length = self.rows >> (stage + 1)
            away = self.offsets[stage] + (1 - bit_of(self.me, bit)) * length
            source = self.buffer.at[self.held(away, length)]
            target = self.landing.at[self.landed(self.lands[stage], length)]
        elif stage < halvings + doublings:
            bit = self.extra[stage - halvings]
            length = self.rows >> halvings
            source = self.buffer.at[self.held(self.offsets[-1], length)]
            target = self.landing.at[self.landed(self.lands[-1] + (stage - halvings) * length, length)]
        else:
            step = 2 * halvings + doublings - 1 - stage
            bit = self.order[step]
            length = self.rows >> (step + 1)
            target = self.final(self.offsets[step + 1], length)
            source = target
            if step == halvings - 1:
                source = self.buffer.at[self.held(self.offsets[step + 1], length)]
        return pltpu.make_async_remote_copy(
            src_ref=source,
            dst_ref=target,
            send_sem=self.send_sem,
            recv_sem=self.recv_sems.at[stage],
            device_id=(partner_of(self.me, bit), self.core),
            device_id_type=MESH_ID,
        )

    def advance(self, stage):
        halvings = len(self.order)
        doublings = len(self.extra)
        if stage > 0:
            self.copy(stage - 1).wait()
            if stage <= halvings + doublings:
                step = min(stage, halvings)
                length = self.rows >> step
                if stage <= halvings:
                    land = self.lands[stage - 1]
                else:
                    land = self.lands[-1] + (stage - 1 - halvings) * length
                index = self.held(self.offsets[step], length)
                self.buffer[index] = self.buffer[index] + self.landing[self.landed(land, length)]
            if stage == halvings + doublings:
                self.own_copy().start()
            if stage == halvings + doublings + 1:
                self.own_copy().wait()
        if stage < self.stages:
            self.copy(stage).start()


def unit_table():
    table = []
    for j in range(3):
        for c in range(3):
            place = (CHUNK * j, 256 * c)
            table.append(("proj", place, place, (CHUNK, 256), c, ("hidden", j)))
        for c in range(3):
            place = (256 * c, CHUNK * j)
            table.append(("hidden", place, place, (256, CHUNK), c, ("hidden", j)))
    for c in range(3):
        table.append(("output", (0, 256 * c), (0, 256 * c), (384, 256), c, ("output", 0)))
    for name, col in (("query", 0), ("key", 384), ("value", 0)):
        for c in range(3):
            table.append((name, (256 * c, col), (256 * c, 0), (256, 384), c, ("attend", 0)))
    table.append(("small", (0, 0), (0, 0), (128, 128), 0, ("small", 0)))
    return table


def order_kind(number, kind):
    return kind if kind < 2 else 2 + (number // 3) % 2


def plan_units(size, ticks, table, freed):
    orders, extra = orders_of(size)
    bits = dp_bits(size)
    rate, delay, step_cost = 45e3, 2.5, 0.25
    free = {bit: 0.0 for bit in bits}

    def send(number, stage, now):
        _, _, _, (rows, cols), kind, _ = table[number]
        order = orders[order_kind(number, kind)]
        down = len(order)
        if stage < down:
            bit, length = order[stage], rows >> (stage + 1)
        elif stage < down + len(extra):
            bit, length = extra[stage - down], rows >> down
        else:
            step = 2 * down + len(extra) - 1 - stage
            bit, length = order[step], rows >> (step + 1)
        takes = length * cols * 4 / rate
        if bit == bits[3]:
            takes = 2 * takes
        free[bit] = max(free[bit], now) + takes
        if bit == bits[3]:
            free[bits[2]] = max(free[bits[2]], now) + takes / 2
        return free[bit] + delay

    stages = 8 + len(extra)
    waiting = []
    by_tick = {}
    for name, now in ticks:
        steps = []
        for number, entry in enumerate(table):
            if entry[5] == name:
                heapq.heappush(waiting, (now, number, 0))
        if name == ("free", 0):
            for item in sorted(waiting):
                ready, number, stage = item
                if number in freed and stage <= 5 + len(extra):
                    waiting.remove(item)
                    while stage <= 5 + len(extra):
                        now = max(now, ready) + step_cost
                        steps.append((number, stage))
                        ready = send(number, stage, now)
                        stage += 1
                    waiting.append((ready, number, stage))
            heapq.heapify(waiting)
        while waiting and waiting[0][0] <= now:
            _, number, stage = heapq.heappop(waiting)
            steps.append((number, stage))
            now += step_cost
            if stage < stages:
                heapq.heappush(waiting, (send(number, stage, now), number, stage + 1))
        by_tick[name] = steps
    left = []
    while waiting:
        ready, number, stage = heapq.heappop(waiting)
        now = max(now, ready) + step_cost
        left.append((number, stage))
        if stage < stages:
            heapq.heappush(waiting, (send(number, stage, now), number, stage + 1))
    return by_tick, left, now


def center_of(rows):
    center = rows - jnp.mean(rows, axis=-1, keepdims=True)
    inverse = lax.rsqrt(jnp.mean(center * center, axis=-1, keepdims=True) + eps)
    return center * inverse, inverse


def norm_back(grad_rows, unit_rows, inverse, norm_gain):
    scaled = grad_rows * norm_gain
    return inverse * (
        scaled
        - jnp.mean(scaled, axis=-1, keepdims=True)
        - unit_rows * jnp.mean(scaled * unit_rows, axis=-1, keepdims=True)
    )


def gelu_parts(before):
    normal_cdf = 0.5 * (1.0 + lax.erf(before * (1.0 / math.sqrt(2.0))))
    slope = normal_cdf + before * jnp.exp(-0.5 * before * before) * (1.0 / math.sqrt(2.0 * math.pi))
    return before * normal_cdf, slope


def column_sum(rows):
    return jnp.sum(rows, axis=0, keepdims=True)


def minus_in_three(column, first):
    lane = lax.broadcasted_iota(jnp.int32, (column.shape[0], PAIR), 1)
    high = (-column).astype(jnp.bfloat16).astype(jnp.float32)
    rest = -column - high
    middle = rest.astype(jnp.bfloat16).astype(jnp.float32)
    low = rest - middle
    zero = jnp.zeros((column.shape[0], PAIR), jnp.float32)
    tail = jnp.where(lane == 1, high, jnp.where(lane == 2, middle, jnp.where(lane == 3, low, zero)))
    return jnp.where(lane == 0, first, tail).astype(jnp.bfloat16)


SMALL = (("norm1_gain", 0, 768), ("norm1_bias", 1, 768), ("query_bias", 2, 384), ("value_bias", 3, 384),
         ("output_bias", 4, 768), ("norm2_gain", 5, 768), ("norm2_bias", 6, 768), ("hidden_bias", 7, 1536),
         ("proj_bias", 8, 768))
ROW_OF = {name: row for name, row, _ in SMALL}


def layer_kernel(size, length_ref, *refs):
    (
        frames_in, cotangent_in, hidden_weight_in, proj_weight_in,
        gain_one, shift_one, query_bias, value_bias, output_bias, gain_two, shift_two, hidden_bias, proj_bias,
        query_weight, key_weight, value_weight, output_weight,
    ) = refs[:17]
    (
        block_out, input_grad, query_sum, key_sum, value_sum, output_sum, proj_sum, hidden_sum, small_sum,
        peer_mlp, peer_two, peer_one,
    ) = refs[17:29]
    (
        left, right, resid, second, masked, hidden_w, proj_w, queries, keys, values, lse_terms, attended, key_terms,
        grad_proj, grad_hidden, land_proj, land_hidden, land_attend, land_output, land_small,
        fetched, staged, small, packed,
        load_sems, fetch_sem, stage_sem, peer_send, peer_recv, unit_send, unit_recv, unit_own,
    ) = refs[29:]
    me, core = lax.axis_index("dp"), lax.axis_index("tensor")
    total_rows = frames_in.shape[0]
    blocks, pieces = total_rows // BLOCK, total_rows // PIECE
    length = length_ref[0]
    orders, extra = orders_of(size)
    table = unit_table()

    loads = [
        pltpu.make_async_copy(source, target, load_sems.at[at])
        for at, (source, target) in enumerate(
            ((frames_in, second), (cotangent_in, masked), (hidden_weight_in, hidden_w), (proj_weight_in, proj_w))
        )
    ]
    for load in loads:
        load.start()
    barrier = pltpu.get_barrier_semaphore()
    for bit in dp_bits(size):
        pl.semaphore_signal(barrier, inc=1, device_id=(partner_of(me, bit), core), device_id_type=MESH_ID)
    pl.semaphore_signal(barrier, inc=1, device_id=(me, 1 - core), device_id_type=MESH_ID)

    held = {
        "proj": (grad_proj, proj_sum), "hidden": (grad_hidden, hidden_sum), "output": (resid, output_sum),
        "query": (grad_proj, query_sum), "key": (grad_proj, key_sum),
        "value": (grad_hidden, value_sum), "small": (packed, small_sum),
    }
    lands = {"proj": land_proj, "hidden": land_hidden, "output": land_output, "small": land_small}
    used = {}
    units = []
    for number, (name, place, total_place, shape, kind, _) in enumerate(table):
        shelf = lands.get(name, land_attend)
        key = name if name in lands else "attend"
        slot = used.get(key, 0)
        used[key] = slot + 1
        buffer, total = held[name]
        units.append(
            Unit(
                buffer, total, (place, total_place), shape, orders[order_kind(number, kind)], extra, shelf.at[slot],
                (unit_send.at[number], unit_recv.at[number], unit_own.at[number]), me, core,
            )
        )
    ticks, moment = [], 0.0
    for step in range(3 * blocks):
        moment += FFN_US
        ticks.append((("hidden", step // blocks) if step % blocks == blocks - 1 else ("ffn", step), moment))
    for step in range(pieces):
        moment += BACK_US
        ticks.append((("back", step), moment))
    moment += OUTPUT_US
    ticks.append((("output", 0), moment))
    for step in range(3 * pieces):
        moment += ATTEND_US
        ticks.append((("attn", step), moment))
    ticks.append((("free", 0), moment))
    for step in range(pieces):
        moment += FIRST_US
        ticks.append((("first", step) if step < pieces - 1 else ("attend", 0), moment))
    for step in range(pieces):
        moment += LAST_US
        ticks.append((("last", step) if step < pieces - 1 else ("small", 0), moment))
    freed = [
        at
        for at, (name, (row, col), _, _, _, _) in enumerate(table)
        if (name == "proj" and row < frames_in.shape[1]) or (name == "hidden" and col < 384)
    ]
    by_tick, remaining, _ = plan_units(size, ticks, table, freed)

    def run(steps):
        for number, stage in steps:
            units[number].advance(stage)

    def tick(step, count, name_of):
        for at in range(count):
            steps = by_tick[name_of(at)]
            if steps:
                @pl.when(step == at)
                def _(steps=steps):
                    run(steps)

    def to_peer(source, target, at):
        return pltpu.make_async_remote_copy(
            src_ref=source, dst_ref=target, send_sem=peer_send.at[at], recv_sem=peer_recv.at[at],
            device_id=(me, 1 - core), device_id_type=MESH_ID,
        )

    def rows_at(step, count):
        return pl.ds(pl.multiple_of(step * count, count), count)

    lane = lax.broadcasted_iota(jnp.int32, (1, PAIR), 1)
    heads = (lane < HD, lane >= HD)
    small[...] = jnp.zeros_like(small)
    packed[...] = jnp.zeros_like(packed)

    def add_small(name, value, at=0):
        row = ROW_OF[name]
        index = (slice(row, row + 1), pl.ds(at, value.shape[1]))
        small[index] = small[index] + value

    place = lax.broadcasted_iota(jnp.int32, (total_rows, PAIR), 0)
    column = lax.broadcasted_iota(jnp.int32, (total_rows, PAIR), 1)
    key_terms[...] = jnp.where(
        column == 0, jnp.where(place >= length, masked_value, 0.0), jnp.where(column < 4, 1.0, 0.0)
    ).astype(jnp.bfloat16)
    loads[0].wait()

    @pl.loop(0, blocks)
    def _(step):
        rows = rows_at(step, BLOCK)
        unit_rows, _ = center_of(second[rows, :].astype(jnp.float32))
        first_in = (unit_rows * gain_one[...] + shift_one[...]).astype(jnp.bfloat16)
        queries[rows, :] = ((dot(first_in, query_weight[...]) + query_bias[...]) * score_scale).astype(jnp.bfloat16)
        keys[rows, :] = dot(first_in, key_weight[...]).astype(jnp.bfloat16)
        values[rows, :] = (dot(first_in, value_weight[...]) + value_bias[...]).astype(jnp.bfloat16)

    first_term = jnp.where(lax.broadcasted_iota(jnp.int32, (BLOCK, PAIR), 1) == 0, 1.0, 0.0).astype(jnp.bfloat16)
    ones = jnp.ones((total_rows, PAIR), jnp.bfloat16)
    pl.semaphore_wait(barrier, len(dp_bits(size)) + 1)

    @pl.loop(0, blocks)
    def _(step):
        rows = rows_at(step, BLOCK)

        @pl.loop(0, 3)
        def _(pair):
            cols = pl.ds(pl.multiple_of(pair * PAIR, PAIR), PAIR)
            query_pair = queries[rows, cols]
            key_all = jnp.concatenate([keys[:, cols], key_terms[...]], axis=1)
            value_all = jnp.concatenate([values[:, cols], ones], axis=1)
            mixed = []
            for head in range(2):
                query_one = jnp.where(heads[head], query_pair, jnp.zeros_like(query_pair))
                scores = dot(jnp.concatenate([query_one, first_term], axis=1), key_all, NT)
                maxima = jnp.max(scores, axis=1, keepdims=True)
                weights = jnp.exp(scores - maxima).astype(jnp.bfloat16)
                mixture = dot(weights, value_all)
                totals = mixture[:, PAIR:]
                mixed.append(mixture[:, :PAIR] / totals)
                terms = minus_in_three(maxima + jnp.log(totals), 1.0)
                lse_terms[rows, pl.ds(pl.multiple_of((2 * pair + head) * PAIR, PAIR), PAIR)] = terms
            attended[rows, cols] = jnp.where(heads[0], mixed[0], mixed[1]).astype(jnp.bfloat16)

        right[rows, :] = dot(attended[rows, :], output_weight[...])
        to_peer(right.at[rows, :], left.at[rows, :], step).start()

    loads[1].wait()
    loads[2].wait()
    loads[3].wait()

    @pl.loop(0, 3 * blocks)
    def _(step):
        chunk, block = step // blocks, step % blocks
        rows = rows_at(block, BLOCK)
        units_of = rows_at(chunk, CHUNK)

        @pl.when(chunk == 0)
        def _():
            to_peer(right.at[rows, :], left.at[rows, :], block).wait()
            for half in range(BLOCK // PIECE):
                part = pl.ds(pl.multiple_of(block * BLOCK + half * PIECE, PIECE), PIECE)
                total = second[part, :].astype(jnp.float32) + (right[part, :] + left[part, :]) + output_bias[...]
                resid[part, :] = total
                unit_rows, _ = center_of(total)
                second[part, :] = (unit_rows * gain_two[...] + shift_two[...]).astype(jnp.bfloat16)
                live = lax.broadcasted_iota(jnp.int32, (PIECE, 1), 0) + (block * BLOCK + half * PIECE) < length
                grad_raw = masked[part, :]
                grad_f = jnp.where(live, grad_raw.astype(jnp.float32), 0.0)
                masked[part, :] = grad_f.astype(jnp.bfloat16)
                add_small("proj_bias", column_sum(grad_f))

        rows_in = second[rows, :]
        grad_in = masked[rows, :]
        up, down = hidden_w[:, units_of], proj_w[units_of, :]
        active_f, slope = gelu_parts(dot(rows_in, up) + hidden_bias[:, units_of])
        active = active_f.astype(jnp.bfloat16)
        grad_pre = dot(grad_in, down, NT) * slope
        grad_pre_b = grad_pre.astype(jnp.bfloat16)
        bias_at = (slice(ROW_OF["hidden_bias"], ROW_OF["hidden_bias"] + 1), units_of)
        small[bias_at] = small[bias_at] + column_sum(grad_pre)

        @pl.when(chunk == 0)
        def _():
            left[rows, :] = dot(active, down)
            right[rows, :] = dot(grad_pre_b, up, NT)

        @pl.when(chunk > 0)
        def _():
            left[rows, :] = left[rows, :] + dot(active, down)
            right[rows, :] = right[rows, :] + dot(grad_pre_b, up, NT)

        @pl.when(block == 0)
        def _():
            grad_proj[units_of, :] = dot(active, grad_in, TN)
            grad_hidden[:, units_of] = dot(rows_in, grad_pre_b, TN)

        @pl.when(block > 0)
        def _():
            grad_proj[units_of, :] = grad_proj[units_of, :] + dot(active, grad_in, TN)
            grad_hidden[:, units_of] = grad_hidden[:, units_of] + dot(rows_in, grad_pre_b, TN)

        @pl.when(chunk == 2)
        def _():
            for half in range(BLOCK // PIECE):
                piece = block * (BLOCK // PIECE) + half
                part = rows_at(piece, PIECE)
                to_peer(right.at[part, :], peer_two.at[part, :], blocks + piece).start()
                to_peer(left.at[part, :], peer_mlp.at[part, :], blocks + pieces + piece).start()

        tick(step, 3 * blocks, lambda at: ("hidden", at // blocks) if at % blocks == blocks - 1 else ("ffn", at))

    def fetch(source, part, at):
        return pltpu.make_async_copy(source.at[part, :], fetched.at[at], fetch_sem.at[at])

    def store(value, target, part):
        staged[...] = value.astype(jnp.bfloat16)
        copy = pltpu.make_async_copy(staged, target.at[part, :], stage_sem)
        copy.start()
        copy.wait()

    @pl.loop(0, pieces)
    def _(piece):
        part = rows_at(piece, PIECE)
        to_peer(right.at[part, :], peer_two.at[part, :], blocks + piece).wait()
        fetch(peer_two, part, 0).start()
        to_peer(left.at[part, :], peer_mlp.at[part, :], blocks + pieces + piece).wait()
        fetch(peer_mlp, part, 1).start()
        rows_f = resid[part, :]
        unit_rows, inverse = center_of(rows_f)
        fetch(peer_two, part, 0).wait()
        grad_two = right[part, :] + fetched[0]
        grad_rows = masked[part, :].astype(jnp.float32) + norm_back(grad_two, unit_rows, inverse, gain_two[...])
        add_small("norm2_gain", column_sum(grad_two * unit_rows))
        add_small("norm2_bias", column_sum(grad_two))
        add_small("output_bias", column_sum(grad_rows))
        right[part, :] = grad_rows
        grad_b = grad_rows.astype(jnp.bfloat16)
        masked[part, :] = grad_b
        proj_w[part, 0:384] = dot(grad_b, output_weight[...], NT).astype(jnp.bfloat16)
        fetch(peer_mlp, part, 1).wait()
        store(rows_f + (left[part, :] + fetched[1]) + proj_bias[...], block_out, part)
        tick(piece, pieces, lambda at: ("back", at))

    resid[0:384, :] = dot(attended[...], masked[...], TN)
    run(by_tick[("output", 0)])

    again = pltpu.make_async_copy(frames_in, masked, load_sems.at[4])
    again.start()
    for pair in range(3):
        hidden_w[pair * PAIR : (pair + 1) * PAIR, :] = keys[:, pair * PAIR : (pair + 1) * PAIR].T
    top = lax.broadcasted_iota(jnp.int32, (PAIR, 1), 0) < HD

    @pl.loop(0, 3 * pieces)
    def _(step):
        pair, piece = step // pieces, step % pieces
        part = rows_at(piece, PIECE)
        cols = pl.ds(pl.multiple_of(pair * PAIR, PAIR), PAIR)
        query_pair = queries[part, cols]
        grad_pair = proj_w[part, cols]
        product = grad_pair.astype(jnp.float32) * attended[part, cols].astype(jnp.float32)
        key_all = jnp.concatenate([keys[:, cols], key_terms[...]], axis=1)
        value_all = jnp.concatenate([values[:, cols], ones], axis=1)
        key_rows = hidden_w[cols, :]
        grad_values, grad_keys, grad_queries = 0.0, 0.0, []
        for head in range(2):
            mine = heads[head]
            query_one = jnp.where(mine, query_pair, jnp.zeros_like(query_pair))
            grad_one = jnp.where(mine, grad_pair, jnp.zeros_like(grad_pair))
            delta = jnp.sum(jnp.where(mine, product, 0.0), axis=1, keepdims=True)
            terms = lse_terms[part, pl.ds(pl.multiple_of((2 * pair + head) * PAIR, PAIR), PAIR)]
            probs = jnp.exp(dot(key_all, jnp.concatenate([query_one, terms], axis=1), NT))
            shifted = dot(value_all, jnp.concatenate([grad_one, minus_in_three(delta, 0.0)], axis=1), NT)
            grad_scores = (probs * shifted).astype(jnp.bfloat16)
            grad_values = grad_values + dot(probs.astype(jnp.bfloat16), grad_one)
            grad_keys = grad_keys + dot(grad_scores, query_one)
            grad_queries.append(dot(key_rows, grad_scores))
        grad_query = (jnp.where(top, grad_queries[0], grad_queries[1]) * score_scale).T
        second[part, cols] = grad_query.astype(jnp.bfloat16)
        bias_at = (slice(ROW_OF["query_bias"], ROW_OF["query_bias"] + 1), cols)
        small[bias_at] = small[bias_at] + column_sum(grad_query)

        @pl.when(piece == 0)
        def _():
            left[:, 0:PAIR] = grad_values
            left[:, PAIR : 2 * PAIR] = grad_keys

        @pl.when(piece > 0)
        def _():
            left[:, 0:PAIR] = left[:, 0:PAIR] + grad_values
            left[:, PAIR : 2 * PAIR] = left[:, PAIR : 2 * PAIR] + grad_keys

        @pl.when(piece == pieces - 1)
        def _():
            grad_all = left[:, 0:PAIR]
            bias_at = (slice(ROW_OF["value_bias"], ROW_OF["value_bias"] + 1), cols)
            small[bias_at] = column_sum(grad_all)
            proj_w[:, pl.ds(pl.multiple_of(384 + pair * PAIR, PAIR), PAIR)] = grad_all.astype(jnp.bfloat16)
            second[:, pl.ds(pl.multiple_of(384 + pair * PAIR, PAIR), PAIR)] = left[:, PAIR : 2 * PAIR].astype(
                jnp.bfloat16
            )

        tick(step, 3 * pieces, lambda at: ("attn", at))

    again.wait()
    run(by_tick[("free", 0)])

    @pl.loop(0, pieces)
    def _(piece):
        part = rows_at(piece, PIECE)
        unit_rows, _ = center_of(masked[part, :].astype(jnp.float32))
        first_in = (unit_rows * gain_one[...] + shift_one[...]).astype(jnp.bfloat16)
        grad_query, grad_key = second[part, 0:384], second[part, 384:768]
        grad_value = proj_w[part, 384:768]
        left[part, :] = (
            dot(grad_query, query_weight[...], NT)
            + dot(grad_key, key_weight[...], NT)
            + dot(grad_value, value_weight[...], NT)
        )
        to_peer(left.at[part, :], peer_one.at[part, :], blocks + 2 * pieces + piece).start()
        terms = [dot(first_in, grad, TN) for grad in (grad_query, grad_key, grad_value)]
        width = frames_in.shape[1]
        targets = (
            (grad_proj, (slice(0, width), slice(0, 384))),
            (grad_proj, (slice(0, width), slice(384, 768))),
            (grad_hidden, (slice(0, width), slice(0, 384))),
        )

        @pl.when(piece == 0)
        def _():
            for (ref, index), term in zip(targets, terms):
                ref[index] = term

        @pl.when(piece > 0)
        def _():
            for (ref, index), term in zip(targets, terms):
                ref[index] = ref[index] + term

        tick(piece, pieces, lambda at: ("first", at) if at < pieces - 1 else ("attend", 0))

    @pl.loop(0, pieces)
    def _(piece):
        part = rows_at(piece, PIECE)
        to_peer(left.at[part, :], peer_one.at[part, :], blocks + 2 * pieces + piece).wait()
        fetch(peer_one, part, 0).start()
        unit_rows, inverse = center_of(masked[part, :].astype(jnp.float32))
        fetch(peer_one, part, 0).wait()
        grad_one = left[part, :] + fetched[0]
        add_small("norm1_gain", column_sum(grad_one * unit_rows))
        add_small("norm1_bias", column_sum(grad_one))
        store(right[part, :] + norm_back(grad_one, unit_rows, inverse, gain_one[...]), input_grad, part)

        @pl.when(piece == pieces - 1)
        def _():
            at = 0
            for _, row, count in SMALL:
                for start in range(0, count, 128):
                    packed[at : at + 1, :] = small[row : row + 1, start : start + 128]
                    at += 1

        tick(piece, pieces, lambda at: ("last", at) if at < pieces - 1 else ("small", 0))

    run(remaining)


VMEM_BYTES = 64 * 2**20
FFN_US, BACK_US, OUTPUT_US, ATTEND_US, FIRST_US, LAST_US = 3.3, 2.0, 1.5, 2.8, 1.5, 1.5


def on_device(
    size,
    frames,
    lengths,
    cotangent,
    norm1_gain,
    norm1_bias,
    query_weight,
    query_bias,
    key_weight,
    value_weight,
    value_bias,
    output_weight,
    output_bias,
    norm2_gain,
    norm2_bias,
    hidden_weight,
    hidden_bias,
    proj_weight,
    proj_bias,
):
    rows, width = frames.shape[1:]
    part = query_weight.shape[1]
    hidden = hidden_weight.shape[1]
    extra = orders_of(size)[1]
    units = len(unit_table())
    stages = 8 + len(extra)
    pieces = rows // PIECE
    f32, bf16 = jnp.float32, jnp.bfloat16
    shape = jax.ShapeDtypeStruct
    anywhere = pl.BlockSpec(memory_space=pl.ANY)
    inside = pl.BlockSpec(memory_space=pltpu.VMEM)
    dma = pltpu.SemaphoreType.DMA
    results = pl.pallas_call(
        functools.partial(layer_kernel, size),
        out_shape=[
            shape((rows, width), bf16), shape((rows, width), bf16),
            shape((width, part), f32), shape((width, part), f32), shape((width, part), f32), shape((part, width), f32),
            shape((hidden, width), f32), shape((width, hidden), f32), shape((128, 128), f32),
            shape((rows, width), f32), shape((rows, width), f32), shape((rows, width), f32),
        ],
        in_specs=[pl.BlockSpec(memory_space=pltpu.SMEM)] + [anywhere] * 4 + [inside] * 13,
        out_specs=[anywhere] * 12,
        scratch_shapes=[
            pltpu.VMEM((rows, width), f32), pltpu.VMEM((rows, width), f32), pltpu.VMEM((rows, width), f32),
            pltpu.VMEM((rows, width), bf16), pltpu.VMEM((rows, width), bf16),
            pltpu.VMEM((width, hidden), bf16), pltpu.VMEM((hidden, width), bf16),
            pltpu.VMEM((rows, part), bf16), pltpu.VMEM((rows, part), bf16), pltpu.VMEM((rows, part), bf16),
            pltpu.VMEM((rows, 2 * part), bf16), pltpu.VMEM((rows, part), bf16), pltpu.VMEM((rows, PAIR), bf16),
            pltpu.VMEM((hidden, width), f32), pltpu.VMEM((width, hidden), f32),
            pltpu.VMEM((9, landing_rows(CHUNK, extra), 256), f32),
            pltpu.VMEM((9, landing_rows(256, extra), CHUNK), f32),
            pltpu.VMEM((9, landing_rows(256, extra), 384), f32),
            pltpu.VMEM((3, landing_rows(384, extra), 256), f32),
            pltpu.VMEM((1, landing_rows(128, extra), 128), f32),
            pltpu.VMEM((2, PIECE, width), f32), pltpu.VMEM((PIECE, width), bf16),
            pltpu.VMEM((16, hidden), f32), pltpu.VMEM((128, 128), f32),
            dma((5,)), dma((2,)), dma, dma((3 * pieces + rows // BLOCK,)), dma((3 * pieces + rows // BLOCK,)),
            dma((units,)), dma((units, stages)), dma((units,)),
        ],
        compiler_params=pltpu.CompilerParams(
            collective_id=0, has_side_effects=True, vmem_limit_bytes=VMEM_BYTES
        ),
        name="layer",
    )(
        lengths, frames[0], cotangent[0], hidden_weight, proj_weight,
        norm1_gain[None], norm1_bias[None], query_bias[None], value_bias[None], output_bias[None],
        norm2_gain[None], norm2_bias[None], hidden_bias[None], proj_bias[None],
        query_weight, key_weight, value_weight, output_weight,
    )
    block_out, input_grad, query_w, key_w, value_w, output_w, proj_w, hidden_w, packed = results[:9]
    flat = packed.reshape(-1)
    small, at = {}, 0
    for name, _, count in SMALL:
        small[name] = lax.slice(flat, (at,), (at + count,))
        at += count
    return (
        block_out[None], input_grad[None],
        small["norm1_gain"], small["norm1_bias"],
        query_w, small["query_bias"], key_w, value_w, small["value_bias"],
        output_w, small["output_bias"], small["norm2_gain"], small["norm2_bias"],
        hidden_w, small["hidden_bias"], proj_w, small["proj_bias"],
    )


def solution(mesh):
    placed = (
        P("dp", None, None),
        P("dp"),
        P("dp", None, None),
        P(),
        P(),
        P(None, "tensor"),
        P("tensor"),
        P(None, "tensor"),
        P(None, "tensor"),
        P("tensor"),
        P("tensor", None),
        P(),
        P(),
        P(),
        P(None, "tensor"),
        P("tensor"),
        P("tensor", None),
        P(),
    )
    return jax.shard_map(
        functools.partial(on_device, mesh.shape["dp"]),
        mesh=mesh,
        in_specs=placed,
        out_specs=(
            P("dp", None, None),
            P("dp", None, None),
            P(),
            P(),
            P(None, "tensor"),
            P("tensor"),
            P(None, "tensor"),
            P(None, "tensor"),
            P("tensor"),
            P("tensor", None),
            P(),
            P(),
            P(),
            P(None, "tensor"),
            P("tensor"),
            P("tensor", None),
            P(),
        ),
        check_vma=False,
    )
```

```python
import functools
import math

import jax
import jax.numpy as jnp
from jax import lax
from jax.experimental import pallas as pl
from jax.experimental.pallas import tpu as pltpu
from jax.sharding import PartitionSpec as P

HD = 64
PAIR = 2 * HD
CHUNKS = ((256, 6),)
BLOCK = 512
PIECE = 256

eps = 1e-05
score_scale = 0.125
masked_value = -1e30

MESH_ID = pl.DeviceIdType.MESH
NN = (((1,), (0,)), ((), ()))
NT = (((1,), (1,)), ((), ()))
TN = (((0,), (0,)), ((), ()))


def dot(left, right, form=NN):
    return lax.dot_general(left, right, form, preferred_element_type=jnp.float32)


def bit_of(index, bit):
    return (index // bit) % 2


def partner_of(index, bit):
    return index + bit - 2 * bit * bit_of(index, bit)


def dp_bits(size):
    return [1 << power for power in range(size.bit_length() - 1)]


def orders_of(size):
    bits = dp_bits(size)
    a, b, c, d = bits[:4]
    return [[a, b, c, d], [b, a, c, d], [c, a, b, d], [c, b, a, d]], bits[4:]


def landing_rows(rows, extra):
    return rows - (rows >> 4) + len(extra) * (rows >> 4)


class Unit:
    def __init__(self, buffer, total, place, shape, order, extra, landing, sems, me, core):
        (self.row, self.col), (self.total_row, self.total_col) = place
        self.rows, self.cols = shape
        self.buffer, self.total, self.landing = buffer, total, landing
        self.order, self.extra = order, extra
        self.send_sem, self.recv_sems, self.own_sem = sems
        self.me, self.core = me, core
        self.offsets = [0]
        self.lands = [0]
        for step, bit in enumerate(order):
            self.offsets.append(self.offsets[-1] + bit_of(me, bit) * (self.rows >> (step + 1)))
            self.lands.append(self.lands[-1] + (self.rows >> (step + 1)))
        self.stages = 2 * len(order) + len(extra)

    def held(self, offset, length):
        return (pl.ds(pl.multiple_of(self.row + offset, 8), length), pl.ds(self.col, self.cols))

    def final(self, offset, length):
        index = (pl.ds(pl.multiple_of(self.total_row + offset, 8), length), pl.ds(self.total_col, self.cols))
        return self.total.at[index]

    def landed(self, start, length):
        return (pl.ds(start, length), pl.ds(0, self.cols))

    def own_copy(self):
        length = self.rows >> len(self.order)
        return pltpu.make_async_copy(
            self.buffer.at[self.held(self.offsets[-1], length)],
            self.final(self.offsets[-1], length),
            self.own_sem,
        )

    def copy(self, stage):
        halvings = len(self.order)
        doublings = len(self.extra)
        if stage < halvings:
            bit = self.order[stage]
            length = self.rows >> (stage + 1)
            away = self.offsets[stage] + (1 - bit_of(self.me, bit)) * length
            source = self.buffer.at[self.held(away, length)]
            target = self.landing.at[self.landed(self.lands[stage], length)]
        elif stage < halvings + doublings:
            bit = self.extra[stage - halvings]
            length = self.rows >> halvings
            source = self.buffer.at[self.held(self.offsets[-1], length)]
            target = self.landing.at[self.landed(self.lands[-1] + (stage - halvings) * length, length)]
        else:
            step = 2 * halvings + doublings - 1 - stage
            bit = self.order[step]
            length = self.rows >> (step + 1)
            target = self.final(self.offsets[step + 1], length)
            source = target
            if step == halvings - 1:
                source = self.buffer.at[self.held(self.offsets[step + 1], length)]
        return pltpu.make_async_remote_copy(
            src_ref=source,
            dst_ref=target,
            send_sem=self.send_sem,
            recv_sem=self.recv_sems.at[stage],
            device_id=(partner_of(self.me, bit), self.core),
            device_id_type=MESH_ID,
        )

    def advance(self, stage):
        halvings = len(self.order)
        doublings = len(self.extra)
        if stage > 0:
            self.copy(stage - 1).wait()
            if stage <= halvings + doublings:
                step = min(stage, halvings)
                length = self.rows >> step
                if stage <= halvings:
                    land = self.lands[stage - 1]
                else:
                    land = self.lands[-1] + (stage - 1 - halvings) * length
                index = self.held(self.offsets[step], length)
                self.buffer[index] = self.buffer[index] + self.landing[self.landed(land, length)]
            if stage == halvings + doublings:
                self.own_copy().start()
            if stage == halvings + doublings + 1:
                self.own_copy().wait()
        if stage < self.stages:
            self.copy(stage).start()


def chunk_list():
    out, base = [], 0
    for group, (width, count) in enumerate(CHUNKS):
        for at in range(count):
            out.append((group, at, base, width))
            base += width
    return out


def unit_table():
    table = []
    for number, (group, _, base, width) in enumerate(chunk_list()):
        for c in range(3):
            place = (base, 256 * c)
            table.append((("proj", group), place, place, (width, 256), c, ("hidden", number)))
        for c in range(3):
            place = (256 * c, base)
            table.append((("hidden", group), place, place, (256, width), c, ("hidden", number)))
    for c in range(3):
        table.append(("output", (0, 256 * c), (0, 256 * c), (384, 256), c, ("output", 0)))
    for name, col in (("query", 0), ("key", 384), ("value", 0)):
        for c in range(3):
            table.append((name, (256 * c, col), (256 * c, 0), (256, 384), c, ("attend", 0)))
    table.append(("small", (0, 0), (0, 0), (128, 128), 0, ("small", 0)))
    return table


def order_kind(number, kind):
    return kind if kind < 2 else 2 + (number // 3) % 2


def plan_units(size, ticks, table, freed, start):
    orders, extra = orders_of(size)
    bits = dp_bits(size)
    rate, delay, step_cost, add_rate = RATES
    spots = range(4)
    busy = {}

    def messages(number):
        _, _, _, (rows, cols), kind, _ = table[number]
        order = orders[order_kind(number, kind)]
        down = [(bit, (rows >> (step + 1)) * cols * 4) for step, bit in enumerate(order)]
        across = [(bit, (rows >> len(order)) * cols * 4) for bit in extra]
        return down + across + down[::-1], len(down) + len(across)

    def arrival(message, now):
        bit, length = message
        takes, latest = length / rate, now
        for spot in spots:
            if bit == bits[2]:
                path = [(min(spot, spot ^ 1), spot % 2)]
            elif bit == bits[3]:
                path = [(at, 0) for at in range(spot, spot + 2)] if spot < 2 else [
                    (at, 1) for at in range(spot - 1, spot - 3, -1)
                ]
            else:
                path = [(bit, spot)]
            begin = now
            for link in path:
                key = (len(path) == 1 and bit != bits[2], link)
                begin = max(busy.get(key, 0.0), begin)
                busy[key] = begin + takes
                latest = max(latest, begin + takes)
        return latest + delay

    plans = [messages(number) for number in range(len(table))]
    waiting = []

    def take(item, now, steps):
        waiting.remove(item)
        _, number, stage = item
        sent, downs = plans[number]
        now += step_cost
        if 0 < stage <= downs:
            now += sent[stage - 1][1] / add_rate
        steps.append((number, stage))
        if stage < len(sent):
            waiting.append((arrival(sent[stage], now), number, stage + 1))
        return now

    def run_ready(now, steps):
        while True:
            ready = [item for item in waiting if item[0] <= now]
            if not ready:
                return now
            now = take(min(ready, key=urgency), now, steps)

    by_tick = {}
    now = start
    for name, takes in ticks:
        steps = by_tick[name] = []
        now += takes
        waiting.extend((now, number, 0) for number, entry in enumerate(table) if entry[5] == name)
        if name == ("free", 0):
            for item in sorted(waiting):
                while item[1] in freed and item[2] <= 5 + len(extra):
                    now = take(item, max(now, item[0]), steps)
                    item = waiting[-1]
        now = run_ready(now, steps)
    left = []
    while waiting:
        now = run_ready(max(now, min(waiting)[0]), left)
    return by_tick, left, now


def center_of(rows):
    center = rows - jnp.mean(rows, axis=-1, keepdims=True)
    inverse = lax.rsqrt(jnp.mean(center * center, axis=-1, keepdims=True) + eps)
    return center * inverse, inverse


def norm_back(grad_rows, unit_rows, inverse, norm_gain):
    scaled = grad_rows * norm_gain
    return inverse * (
        scaled
        - jnp.mean(scaled, axis=-1, keepdims=True)
        - unit_rows * jnp.mean(scaled * unit_rows, axis=-1, keepdims=True)
    )


def gelu_parts(before):
    normal_cdf = 0.5 * (1.0 + lax.erf(before * (1.0 / math.sqrt(2.0))))
    slope = normal_cdf + before * jnp.exp(-0.5 * before * before) * (1.0 / math.sqrt(2.0 * math.pi))
    return before * normal_cdf, slope


def column_sum(rows):
    return jnp.sum(rows, axis=0, keepdims=True)


def minus_in_three(column, first):
    lane = lax.broadcasted_iota(jnp.int32, (column.shape[0], PAIR), 1)
    high = (-column).astype(jnp.bfloat16).astype(jnp.float32)
    rest = -column - high
    middle = rest.astype(jnp.bfloat16).astype(jnp.float32)
    low = rest - middle
    zero = jnp.zeros((column.shape[0], PAIR), jnp.float32)
    tail = jnp.where(lane == 1, high, jnp.where(lane == 2, middle, jnp.where(lane == 3, low, zero)))
    return jnp.where(lane == 0, first, tail).astype(jnp.bfloat16)


class Row:
    def __init__(self, ref):
        self.ref = ref

    def __getitem__(self, _):
        return self.ref[...].reshape(1, self.ref.shape[0])


SMALL = (("norm1_gain", 0, 768), ("norm1_bias", 1, 768), ("query_bias", 2, 384), ("value_bias", 3, 384),
         ("output_bias", 4, 768), ("norm2_gain", 5, 768), ("norm2_bias", 6, 768), ("hidden_bias", 7, 1536),
         ("proj_bias", 8, 768))
ROW_OF = {name: row for name, row, _ in SMALL}


def unpack_kernel(packed, *vectors):
    at = 0
    for (_, _, count), vector in zip(SMALL, vectors):
        rows = count // 128
        vector[...] = packed[at : at + rows, :].reshape(count)
        at += rows


def layer_kernel(size, length_ref, *refs):
    (
        frames_in, cotangent_in, hidden_weight_in, proj_weight_in,
        gain_one, shift_one, query_bias, value_bias, output_bias, gain_two, shift_two, hidden_bias, proj_bias,
        query_weight_in, key_weight_in, value_weight_in, output_weight_in,
    ) = refs[:17]
    (
        block_out, input_grad, query_sum, key_sum, value_sum, output_sum, proj_sum, hidden_sum, small_sum,
        peer_mlp, peer_two, peer_one,
    ) = refs[17:29]
    gain_one, shift_one, query_bias, value_bias, output_bias, gain_two, shift_two, proj_bias = (
        Row(ref) for ref in (gain_one, shift_one, query_bias, value_bias, output_bias, gain_two, shift_two, proj_bias)
    )
    (
        left, right, resid, second, masked, hidden_w, proj_w, queries, keys, values, lse_terms, attended, key_terms,
        grad_proj, grad_hidden, *land_hidden, land_attend, land_output, land_small,
        fetched, staged, small, packed, query_weight, key_weight, value_weight, output_weight,
        load_sems, fetch_sem, stage_sem, peer_send, peer_recv, unit_send, unit_recv, unit_own,
    ) = refs[29:]
    me, core = lax.axis_index("dp"), lax.axis_index("tensor")
    total_rows = frames_in.shape[0]
    blocks, pieces = total_rows // BLOCK, total_rows // PIECE
    length = length_ref[0]
    orders, extra = orders_of(size)
    chunks = chunk_list()
    table = unit_table()

    pairs = [
        (frames_in.at[pl.ds(block * BLOCK, BLOCK), :], second.at[pl.ds(block * BLOCK, BLOCK), :])
        for block in range(blocks)
    ]
    pairs += [
        (query_weight_in, query_weight), (key_weight_in, key_weight), (value_weight_in, value_weight),
        (output_weight_in, output_weight), (cotangent_in, masked), (hidden_weight_in, hidden_w),
        (proj_weight_in, proj_w), (frames_in, masked),
    ]
    loads = [
        pltpu.make_async_copy(source, target, load_sems.at[at]) for at, (source, target) in enumerate(pairs)
    ]
    first_loads, weight_loads, later_loads = loads[:blocks], loads[blocks : blocks + 3], loads[blocks + 3 : -1]
    for load in first_loads + weight_loads:
        load.start()
    barrier = pltpu.get_barrier_semaphore()
    for bit in dp_bits(size):
        pl.semaphore_signal(barrier, inc=1, device_id=(partner_of(me, bit), core), device_id_type=MESH_ID)
    pl.semaphore_signal(barrier, inc=1, device_id=(me, 1 - core), device_id_type=MESH_ID)

    held = {
        "output": (resid, output_sum),
        "query": (grad_proj, query_sum), "key": (grad_proj, key_sum),
        "value": (grad_hidden, value_sum), "small": (packed, small_sum),
    }
    lands = {"output": land_output, "small": land_small}
    for group in range(len(CHUNKS)):
        held["proj", group], held["hidden", group] = (grad_proj, proj_sum), (grad_hidden, hidden_sum)
        lands["proj", group], lands["hidden", group] = land_hidden[2 * group : 2 * group + 2]
    used = {}
    units = []
    for number, (name, place, total_place, shape, kind, _) in enumerate(table):
        shelf = lands.get(name, land_attend)
        key = name if name in lands else "attend"
        slot = used.get(key, 0)
        used[key] = slot + 1
        buffer, total = held[name]
        units.append(
            Unit(
                buffer, total, (place, total_place), shape, orders[order_kind(number, kind)], extra, shelf.at[slot],
                (unit_send.at[number], unit_recv.at[number], unit_own.at[number]), me, core,
            )
        )
    ticks = []
    for number, (_, _, _, width) in enumerate(chunks):
        for block in range(blocks):
            name = ("hidden", number) if block == blocks - 1 else ("ffn", (number, block))
            ticks.append((name, FFN_US * width / 512))
    ticks += [(("back", step), BACK_US) for step in range(pieces)] + [(("output", 0), OUTPUT_US)]
    ticks += [(("attn", step), ATTEND_US) for step in range(3 * pieces)] + [(("free", 0), 0.0)]
    ticks += [(("first", step) if step < pieces - 1 else ("attend", 0), FIRST_US) for step in range(pieces)]
    ticks += [(("last", step) if step < pieces - 1 else ("small", 0), LAST_US) for step in range(pieces)]
    freed = [
        at
        for at, (name, (row, col), _, _, _, _) in enumerate(table)
        if (name[0] == "proj" and row < frames_in.shape[1]) or (name[0] == "hidden" and col < 384)
    ]
    by_tick, remaining, _ = plan_units(size, ticks, table, freed, 0.0)

    def run(steps):
        for number, stage in steps:
            units[number].advance(stage)

    def tick(step, count, name_of):
        for at in range(count):
            steps = by_tick[name_of(at)]
            if steps:
                @pl.when(step == at)
                def _(steps=steps):
                    run(steps)

    def to_peer(source, target, at):
        return pltpu.make_async_remote_copy(
            src_ref=source, dst_ref=target, send_sem=peer_send.at[at], recv_sem=peer_recv.at[at],
            device_id=(me, 1 - core), device_id_type=MESH_ID,
        )

    def rows_at(step, count):
        return pl.ds(pl.multiple_of(step * count, count), count)

    lane = lax.broadcasted_iota(jnp.int32, (1, PAIR), 1)
    heads = (lane < HD, lane >= HD)
    small[...] = jnp.zeros_like(small)
    packed[...] = jnp.zeros_like(packed)

    def add_small(name, value, at=0):
        row = ROW_OF[name]
        index = (slice(row, row + 1), pl.ds(at, value.shape[1]))
        small[index] = small[index] + value

    place = lax.broadcasted_iota(jnp.int32, (total_rows, PAIR), 0)
    column = lax.broadcasted_iota(jnp.int32, (total_rows, PAIR), 1)
    key_terms[...] = jnp.where(
        column == 0, jnp.where(place >= length, masked_value, 0.0), jnp.where(column < 4, 1.0, 0.0)
    ).astype(jnp.bfloat16)
    for step in range(blocks):
        first_loads[step].wait()
        rows = pl.ds(step * BLOCK, BLOCK)
        unit_rows, _ = center_of(second[rows, :].astype(jnp.float32))
        first_in = (unit_rows * gain_one[...] + shift_one[...]).astype(jnp.bfloat16)
        if step == 0:
            for load in weight_loads:
                load.wait()
            for load in later_loads:
                load.start()
        queries[rows, :] = ((dot(first_in, query_weight[...]) + query_bias[...]) * score_scale).astype(jnp.bfloat16)
        keys[rows, :] = dot(first_in, key_weight[...]).astype(jnp.bfloat16)
        values[rows, :] = (dot(first_in, value_weight[...]) + value_bias[...]).astype(jnp.bfloat16)

    first_term = jnp.where(lax.broadcasted_iota(jnp.int32, (BLOCK, PAIR), 1) == 0, 1.0, 0.0).astype(jnp.bfloat16)
    ones = jnp.ones((total_rows, PAIR), jnp.bfloat16)
    later_loads[0].wait()
    pl.semaphore_wait(barrier, len(dp_bits(size)) + 1)

    @pl.loop(0, blocks)
    def _(step):
        rows = rows_at(step, BLOCK)

        for pair in range(3):
            cols = pl.ds(pair * PAIR, PAIR)
            query_pair = queries[rows, cols]
            key_all = jnp.concatenate([keys[:, cols], key_terms[...]], axis=1)
            value_all = jnp.concatenate([values[:, cols], ones], axis=1)
            mixed = []
            for head in range(2):
                query_one = jnp.where(heads[head], query_pair, jnp.zeros_like(query_pair))
                scores = dot(jnp.concatenate([query_one, first_term], axis=1), key_all, NT)
                maxima = jnp.max(scores, axis=1, keepdims=True)
                weights = jnp.exp(scores - maxima).astype(jnp.bfloat16)
                mixture = dot(weights, value_all)
                totals = mixture[:, PAIR:]
                mixed.append(mixture[:, :PAIR] / totals)
                terms = minus_in_three(maxima + jnp.log(totals), 1.0)
                lse_terms[rows, pl.ds((2 * pair + head) * PAIR, PAIR)] = terms
            attended[rows, cols] = jnp.where(heads[0], mixed[0], mixed[1]).astype(jnp.bfloat16)

        right[rows, :] = dot(attended[rows, :], output_weight[...])
        to_peer(right.at[rows, :], left.at[rows, :], step).start()

    for load in later_loads[1:]:
        load.wait()

    def feed_forward(group, step):
        width, count = CHUNKS[group]
        first = sum(chunk_count for _, chunk_count in CHUNKS[:group])
        base = chunks[first][2]
        chunk, block = first + step // blocks, step % blocks
        rows = rows_at(block, BLOCK)
        units_of = pl.ds(pl.multiple_of(base + (step // blocks) * width, 256), width)

        @pl.when(chunk == 0)
        def _():
            to_peer(right.at[rows, :], left.at[rows, :], block).wait()
            for half in range(BLOCK // PIECE):
                part = pl.ds(pl.multiple_of(block * BLOCK + half * PIECE, PIECE), PIECE)
                total = second[part, :].astype(jnp.float32) + (right[part, :] + left[part, :]) + output_bias[...]
                resid[part, :] = total
                unit_rows, _ = center_of(total)
                second[part, :] = (unit_rows * gain_two[...] + shift_two[...]).astype(jnp.bfloat16)
                live = lax.broadcasted_iota(jnp.int32, (PIECE, 1), 0) + (block * BLOCK + half * PIECE) < length
                grad_raw = masked[part, :]
                grad_f = jnp.where(live, grad_raw.astype(jnp.float32), 0.0)
                masked[part, :] = grad_f.astype(jnp.bfloat16)
                add_small("proj_bias", column_sum(grad_f))

        rows_in = second[rows, :]
        grad_in = masked[rows, :]
        up, down = hidden_w[:, units_of], proj_w[units_of, :]
        active_f, slope = gelu_parts(dot(rows_in, up) + hidden_bias[units_of].reshape(1, width))
        active = active_f.astype(jnp.bfloat16)
        grad_pre = dot(grad_in, down, NT) * slope
        grad_pre_b = grad_pre.astype(jnp.bfloat16)
        bias_at = (slice(ROW_OF["hidden_bias"], ROW_OF["hidden_bias"] + 1), units_of)
        small[bias_at] = small[bias_at] + column_sum(grad_pre)

        @pl.when(chunk == 0)
        def _():
            left[rows, :] = dot(active, down)
            right[rows, :] = dot(grad_pre_b, up, NT)

        @pl.when(chunk > 0)
        def _():
            left[rows, :] = left[rows, :] + dot(active, down)
            right[rows, :] = right[rows, :] + dot(grad_pre_b, up, NT)

        @pl.when(block == 0)
        def _():
            grad_proj[units_of, :] = dot(active, grad_in, TN)
            grad_hidden[:, units_of] = dot(rows_in, grad_pre_b, TN)

        @pl.when(block > 0)
        def _():
            grad_proj[units_of, :] = grad_proj[units_of, :] + dot(active, grad_in, TN)
            grad_hidden[:, units_of] = grad_hidden[:, units_of] + dot(rows_in, grad_pre_b, TN)

        @pl.when(chunk == len(chunks) - 1)
        def _():
            for half in range(BLOCK // PIECE):
                piece = block * (BLOCK // PIECE) + half
                part = rows_at(piece, PIECE)
                to_peer(right.at[part, :], peer_two.at[part, :], blocks + piece).start()
                to_peer(left.at[part, :], peer_mlp.at[part, :], blocks + pieces + piece).start()

        def name_of(at):
            number = first + at // blocks
            return ("hidden", number) if at % blocks == blocks - 1 else ("ffn", (number, at % blocks))

        tick(step, count * blocks, name_of)

    for group, (_, count) in enumerate(CHUNKS):
        pl.loop(0, count * blocks)(functools.partial(feed_forward, group))

    def fetch(source, part, at):
        return pltpu.make_async_copy(source.at[part, :], fetched.at[at], fetch_sem.at[at])

    def store(value, target, part):
        staged[...] = value.astype(jnp.bfloat16)
        copy = pltpu.make_async_copy(staged, target.at[part, :], stage_sem)
        copy.start()
        copy.wait()

    @pl.loop(0, pieces)
    def _(piece):
        part = rows_at(piece, PIECE)
        to_peer(right.at[part, :], peer_two.at[part, :], blocks + piece).wait()
        fetch(peer_two, part, 0).start()
        to_peer(left.at[part, :], peer_mlp.at[part, :], blocks + pieces + piece).wait()
        fetch(peer_mlp, part, 1).start()
        rows_f = resid[part, :]
        unit_rows, inverse = center_of(rows_f)
        fetch(peer_two, part, 0).wait()
        grad_two = right[part, :] + fetched[0]
        grad_rows = masked[part, :].astype(jnp.float32) + norm_back(grad_two, unit_rows, inverse, gain_two[...])
        add_small("norm2_gain", column_sum(grad_two * unit_rows))
        add_small("norm2_bias", column_sum(grad_two))
        add_small("output_bias", column_sum(grad_rows))
        right[part, :] = grad_rows
        grad_b = grad_rows.astype(jnp.bfloat16)
        masked[part, :] = grad_b
        proj_w[part, 0:384] = dot(grad_b, output_weight[...], NT).astype(jnp.bfloat16)
        fetch(peer_mlp, part, 1).wait()
        store(rows_f + (left[part, :] + fetched[1]) + proj_bias[...], block_out, part)
        tick(piece, pieces, lambda at: ("back", at))

    resid[0:384, :] = dot(attended[...], masked[...], TN)
    run(by_tick[("output", 0)])

    again = loads[-1]
    again.start()
    for pair in range(3):
        hidden_w[pair * PAIR : (pair + 1) * PAIR, :] = keys[:, pair * PAIR : (pair + 1) * PAIR].T
    top = lax.broadcasted_iota(jnp.int32, (PAIR, 1), 0) < HD

    @pl.loop(0, 3 * pieces)
    def _(step):
        pair, piece = step // pieces, step % pieces
        part = rows_at(piece, PIECE)
        cols = pl.ds(pl.multiple_of(pair * PAIR, PAIR), PAIR)
        query_pair = queries[part, cols]
        grad_pair = proj_w[part, cols]
        product = grad_pair.astype(jnp.float32) * attended[part, cols].astype(jnp.float32)
        key_all = jnp.concatenate([keys[:, cols], key_terms[...]], axis=1)
        value_all = jnp.concatenate([values[:, cols], ones], axis=1)
        key_rows = hidden_w[cols, :]
        grad_values, grad_keys, grad_queries = 0.0, 0.0, []
        for head in range(2):
            mine = heads[head]
            query_one = jnp.where(mine, query_pair, jnp.zeros_like(query_pair))
            grad_one = jnp.where(mine, grad_pair, jnp.zeros_like(grad_pair))
            delta = jnp.sum(jnp.where(mine, product, 0.0), axis=1, keepdims=True)
            terms = lse_terms[part, pl.ds(pl.multiple_of((2 * pair + head) * PAIR, PAIR), PAIR)]
            probs = jnp.exp(dot(key_all, jnp.concatenate([query_one, terms], axis=1), NT))
            shifted = dot(value_all, jnp.concatenate([grad_one, minus_in_three(delta, 0.0)], axis=1), NT)
            grad_scores = (probs * shifted).astype(jnp.bfloat16)
            grad_values = grad_values + dot(probs.astype(jnp.bfloat16), grad_one)
            grad_keys = grad_keys + dot(grad_scores, query_one)
            grad_queries.append(dot(key_rows, grad_scores))
        grad_query = (jnp.where(top, grad_queries[0], grad_queries[1]) * score_scale).T
        second[part, cols] = grad_query.astype(jnp.bfloat16)
        bias_at = (slice(ROW_OF["query_bias"], ROW_OF["query_bias"] + 1), cols)
        small[bias_at] = small[bias_at] + column_sum(grad_query)

        @pl.when(piece == 0)
        def _():
            left[:, 0:PAIR] = grad_values
            left[:, PAIR : 2 * PAIR] = grad_keys

        @pl.when(piece > 0)
        def _():
            left[:, 0:PAIR] = left[:, 0:PAIR] + grad_values
            left[:, PAIR : 2 * PAIR] = left[:, PAIR : 2 * PAIR] + grad_keys

        @pl.when(piece == pieces - 1)
        def _():
            grad_all = left[:, 0:PAIR]
            bias_at = (slice(ROW_OF["value_bias"], ROW_OF["value_bias"] + 1), cols)
            small[bias_at] = column_sum(grad_all)
            proj_w[:, pl.ds(pl.multiple_of(384 + pair * PAIR, PAIR), PAIR)] = grad_all.astype(jnp.bfloat16)
            second[:, pl.ds(pl.multiple_of(384 + pair * PAIR, PAIR), PAIR)] = left[:, PAIR : 2 * PAIR].astype(
                jnp.bfloat16
            )

        tick(step, 3 * pieces, lambda at: ("attn", at))

    again.wait()
    run(by_tick[("free", 0)])

    @pl.loop(0, pieces)
    def _(piece):
        part = rows_at(piece, PIECE)
        unit_rows, _ = center_of(masked[part, :].astype(jnp.float32))
        first_in = (unit_rows * gain_one[...] + shift_one[...]).astype(jnp.bfloat16)
        grad_query, grad_key = second[part, 0:384], second[part, 384:768]
        grad_value = proj_w[part, 384:768]
        left[part, :] = (
            dot(grad_query, query_weight[...], NT)
            + dot(grad_key, key_weight[...], NT)
            + dot(grad_value, value_weight[...], NT)
        )
        to_peer(left.at[part, :], peer_one.at[part, :], blocks + 2 * pieces + piece).start()
        terms = [dot(first_in, grad, TN) for grad in (grad_query, grad_key, grad_value)]
        width = frames_in.shape[1]
        targets = (
            (grad_proj, (slice(0, width), slice(0, 384))),
            (grad_proj, (slice(0, width), slice(384, 768))),
            (grad_hidden, (slice(0, width), slice(0, 384))),
        )

        @pl.when(piece == 0)
        def _():
            for (ref, index), term in zip(targets, terms):
                ref[index] = term

        @pl.when(piece > 0)
        def _():
            for (ref, index), term in zip(targets, terms):
                ref[index] = ref[index] + term

        tick(piece, pieces, lambda at: ("first", at) if at < pieces - 1 else ("attend", 0))

    @pl.loop(0, pieces)
    def _(piece):
        part = rows_at(piece, PIECE)
        to_peer(left.at[part, :], peer_one.at[part, :], blocks + 2 * pieces + piece).wait()
        fetch(peer_one, part, 0).start()
        unit_rows, inverse = center_of(masked[part, :].astype(jnp.float32))
        fetch(peer_one, part, 0).wait()
        grad_one = left[part, :] + fetched[0]
        add_small("norm1_gain", column_sum(grad_one * unit_rows))
        add_small("norm1_bias", column_sum(grad_one))
        store(right[part, :] + norm_back(grad_one, unit_rows, inverse, gain_one[...]), input_grad, part)

        @pl.when(piece == pieces - 1)
        def _():
            at = 0
            for _, row, count in SMALL:
                for start in range(0, count, 128):
                    packed[at : at + 1, :] = small[row : row + 1, start : start + 128]
                    at += 1

        tick(piece, pieces, lambda at: ("last", at) if at < pieces - 1 else ("small", 0))

    run(remaining)


VMEM_BYTES = 64 * 2**20
FFN_US, BACK_US, OUTPUT_US, ATTEND_US, FIRST_US, LAST_US = 4.0, 1.4, 1.0, 2.5, 2.0, 2.0
RATES = (46e3, 1.0, 0.05, 2e6)


def urgency(item):
    return (item[1], item[0])


def on_device(
    size,
    frames,
    lengths,
    cotangent,
    norm1_gain,
    norm1_bias,
    query_weight,
    query_bias,
    key_weight,
    value_weight,
    value_bias,
    output_weight,
    output_bias,
    norm2_gain,
    norm2_bias,
    hidden_weight,
    hidden_bias,
    proj_weight,
    proj_bias,
):
    rows, width = frames.shape[1:]
    part = query_weight.shape[1]
    hidden = hidden_weight.shape[1]
    f32, bf16 = jnp.float32, jnp.bfloat16
    extra = orders_of(size)[1]
    units = len(unit_table())
    chunk_lands = []
    for chunk, count in CHUNKS:
        chunk_lands.append(pltpu.VMEM((3 * count, landing_rows(chunk, extra), 256), f32))
        chunk_lands.append(pltpu.VMEM((3 * count, landing_rows(256, extra), chunk), f32))
    stages = 8 + len(extra)
    pieces = rows // PIECE
    shape = jax.ShapeDtypeStruct
    anywhere = pl.BlockSpec(memory_space=pl.ANY)
    inside = pl.BlockSpec(memory_space=pltpu.VMEM)
    dma = pltpu.SemaphoreType.DMA
    results = pl.pallas_call(
        functools.partial(layer_kernel, size),
        out_shape=[
            shape((rows, width), bf16), shape((rows, width), bf16),
            shape((width, part), f32), shape((width, part), f32), shape((width, part), f32), shape((part, width), f32),
            shape((hidden, width), f32), shape((width, hidden), f32), shape((128, 128), f32),
            shape((rows, width), f32), shape((rows, width), f32), shape((rows, width), f32),
        ],
        in_specs=[pl.BlockSpec(memory_space=pltpu.SMEM)] + [anywhere] * 4 + [inside] * 9 + [anywhere] * 4,
        out_specs=[anywhere] * 12,
        scratch_shapes=[
            pltpu.VMEM((rows, width), f32), pltpu.VMEM((rows, width), f32), pltpu.VMEM((rows, width), f32),
            pltpu.VMEM((rows, width), bf16), pltpu.VMEM((rows, width), bf16),
            pltpu.VMEM((width, hidden), bf16), pltpu.VMEM((hidden, width), bf16),
            pltpu.VMEM((rows, part), bf16), pltpu.VMEM((rows, part), bf16), pltpu.VMEM((rows, part), bf16),
            pltpu.VMEM((rows, 2 * part), bf16), pltpu.VMEM((rows, part), bf16), pltpu.VMEM((rows, PAIR), bf16),
            pltpu.VMEM((hidden, width), f32), pltpu.VMEM((width, hidden), f32),
            *chunk_lands,
            pltpu.VMEM((9, landing_rows(256, extra), 384), f32),
            pltpu.VMEM((3, landing_rows(384, extra), 256), f32),
            pltpu.VMEM((1, landing_rows(128, extra), 128), f32),
            pltpu.VMEM((2, PIECE, width), f32), pltpu.VMEM((PIECE, width), bf16),
            pltpu.VMEM((16, hidden), f32), pltpu.VMEM((128, 128), f32),
            *[pltpu.VMEM((width, part), bf16)] * 3, pltpu.VMEM((part, width), bf16),
            dma((rows // BLOCK + 8,)), dma((2,)), dma, dma((3 * pieces + rows // BLOCK,)), dma((3 * pieces + rows // BLOCK,)),
            dma((units,)), dma((units, stages)), dma((units,)),
        ],
        compiler_params=pltpu.CompilerParams(
            collective_id=0, has_side_effects=True, vmem_limit_bytes=VMEM_BYTES
        ),
        name="layer",
    )(
        lengths, frames[0], cotangent[0], hidden_weight, proj_weight,
        norm1_gain, norm1_bias, query_bias, value_bias, output_bias,
        norm2_gain, norm2_bias, hidden_bias, proj_bias,
        query_weight, key_weight, value_weight, output_weight,
    )
    block_out, input_grad, query_w, key_w, value_w, output_w, proj_w, hidden_w, packed = results[:9]
    vectors = pl.pallas_call(
        unpack_kernel, out_shape=[shape((count,), f32) for _, _, count in SMALL], name="unpack"
    )(packed)
    small = {name: vector for (name, _, _), vector in zip(SMALL, vectors)}
    return (
        block_out[None], input_grad[None],
        small["norm1_gain"], small["norm1_bias"],
        query_w, small["query_bias"], key_w, value_w, small["value_bias"],
        output_w, small["output_bias"], small["norm2_gain"], small["norm2_bias"],
        hidden_w, small["hidden_bias"], proj_w, small["proj_bias"],
    )


def solution(mesh):
    placed = (
        P("dp", None, None),
        P("dp"),
        P("dp", None, None),
        P(),
        P(),
        P(None, "tensor"),
        P("tensor"),
        P(None, "tensor"),
        P(None, "tensor"),
        P("tensor"),
        P("tensor", None),
        P(),
        P(),
        P(),
        P(None, "tensor"),
        P("tensor"),
        P("tensor", None),
        P(),
    )
    return jax.shard_map(
        functools.partial(on_device, mesh.shape["dp"]),
        mesh=mesh,
        in_specs=placed,
        out_specs=(
            P("dp", None, None),
            P("dp", None, None),
            P(),
            P(),
            P(None, "tensor"),
            P("tensor"),
            P(None, "tensor"),
            P(None, "tensor"),
            P("tensor"),
            P("tensor", None),
            P(),
            P(),
            P(),
            P(None, "tensor"),
            P("tensor"),
            P("tensor", None),
            P(),
        ),
        check_vma=False,
    )
```

```python
import functools
import math

import jax
import jax.numpy as jnp
from jax import lax
from jax.experimental import pallas as pl
from jax.experimental.pallas import tpu as pltpu
from jax.sharding import PartitionSpec as P

HD = 64
PAIR = 2 * HD
CHUNKS = ((256, 6),)
BLOCK = 512
PIECE = 256

eps = 1e-05
score_scale = 0.125
masked_value = -1e30

MESH_ID = pl.DeviceIdType.MESH
NN = (((1,), (0,)), ((), ()))
NT = (((1,), (1,)), ((), ()))
TN = (((0,), (0,)), ((), ()))


def dot(left, right, form=NN):
    return lax.dot_general(left, right, form, preferred_element_type=jnp.float32)


def bit_of(index, bit):
    return (index // bit) % 2


def partner_of(index, bit):
    return index + bit - 2 * bit * bit_of(index, bit)


def dp_bits(size):
    return [1 << power for power in range(size.bit_length() - 1)]


def orders_of(size):
    bits = dp_bits(size)
    a, b, c, d = bits[:4]
    return [[a, b, c, d], [b, a, c, d], [c, a, b, d], [c, b, a, d]], bits[4:]


def landing_rows(rows, extra):
    return rows - (rows >> 4) + len(extra) * (rows >> 4)


class Unit:
    def __init__(self, buffer, total, place, shape, order, extra, landing, sems, me, core):
        (self.row, self.col), (self.total_row, self.total_col) = place
        self.rows, self.cols = shape
        self.buffer, self.total, self.landing = buffer, total, landing
        self.order, self.extra = order, extra
        self.send_sem, self.recv_sems, self.own_sem = sems
        self.me, self.core = me, core
        self.offsets = [0]
        self.lands = [0]
        for step, bit in enumerate(order):
            self.offsets.append(self.offsets[-1] + bit_of(me, bit) * (self.rows >> (step + 1)))
            self.lands.append(self.lands[-1] + (self.rows >> (step + 1)))
        self.stages = 2 * len(order) + len(extra)

    def held(self, offset, length):
        return (pl.ds(pl.multiple_of(self.row + offset, 8), length), pl.ds(self.col, self.cols))

    def final(self, offset, length):
        index = (pl.ds(pl.multiple_of(self.total_row + offset, 8), length), pl.ds(self.total_col, self.cols))
        return self.total.at[index]

    def landed(self, start, length):
        return (pl.ds(start, length), pl.ds(0, self.cols))

    def own_copy(self):
        length = self.rows >> len(self.order)
        return pltpu.make_async_copy(
            self.buffer.at[self.held(self.offsets[-1], length)],
            self.final(self.offsets[-1], length),
            self.own_sem,
        )

    def copy(self, stage):
        halvings = len(self.order)
        doublings = len(self.extra)
        if stage < halvings:
            bit = self.order[stage]
            length = self.rows >> (stage + 1)
            away = self.offsets[stage] + (1 - bit_of(self.me, bit)) * length
            source = self.buffer.at[self.held(away, length)]
            target = self.landing.at[self.landed(self.lands[stage], length)]
        elif stage < halvings + doublings:
            bit = self.extra[stage - halvings]
            length = self.rows >> halvings
            source = self.buffer.at[self.held(self.offsets[-1], length)]
            target = self.landing.at[self.landed(self.lands[-1] + (stage - halvings) * length, length)]
        else:
            step = 2 * halvings + doublings - 1 - stage
            bit = self.order[step]
            length = self.rows >> (step + 1)
            target = self.final(self.offsets[step + 1], length)
            source = target
            if step == halvings - 1:
                source = self.buffer.at[self.held(self.offsets[step + 1], length)]
        return pltpu.make_async_remote_copy(
            src_ref=source,
            dst_ref=target,
            send_sem=self.send_sem,
            recv_sem=self.recv_sems.at[stage],
            device_id=(partner_of(self.me, bit), self.core),
            device_id_type=MESH_ID,
        )

    def advance(self, stage):
        halvings = len(self.order)
        doublings = len(self.extra)
        if stage > 0:
            self.copy(stage - 1).wait()
            if stage <= halvings + doublings:
                step = min(stage, halvings)
                length = self.rows >> step
                if stage <= halvings:
                    land = self.lands[stage - 1]
                else:
                    land = self.lands[-1] + (stage - 1 - halvings) * length
                index = self.held(self.offsets[step], length)
                self.buffer[index] = self.buffer[index] + self.landing[self.landed(land, length)]
            if stage == halvings + doublings:
                self.own_copy().start()
            if stage == halvings + doublings + 1:
                self.own_copy().wait()
        if stage < self.stages:
            self.copy(stage).start()


def chunk_list():
    out, base = [], 0
    for group, (width, count) in enumerate(CHUNKS):
        for at in range(count):
            out.append((group, at, base, width))
            base += width
    return out


def unit_table():
    table = []
    for number, (group, _, base, width) in enumerate(chunk_list()):
        for c in range(3):
            place = (base, 256 * c)
            table.append((("proj", group), place, place, (width, 256), c, ("hidden", number)))
        for c in range(3):
            place = (256 * c, base)
            table.append((("hidden", group), place, place, (256, width), c, ("hidden", number)))
    for c in range(3):
        table.append(("output", (0, 256 * c), (0, 256 * c), (384, 256), c, ("output", 0)))
    for name, col in (("query", 0), ("key", 384), ("value", 0)):
        for c in range(3):
            table.append((name, (256 * c, col), (256 * c, 0), (256, 384), c, ("attend", 0)))
    table.append(("small", (0, 0), (0, 0), (128, 128), 0, ("small", 0)))
    return table


def order_kind(number, kind):
    return kind if kind < 2 else 2 + (number // 3) % 2


def plan_units(size, ticks, table, freed, start):
    orders, extra = orders_of(size)
    bits = dp_bits(size)
    rate, delay, step_cost, add_rate = RATES
    spots = range(4)
    busy = {}

    def messages(number):
        _, _, _, (rows, cols), kind, _ = table[number]
        order = orders[order_kind(number, kind)]
        down = [(bit, (rows >> (step + 1)) * cols * 4) for step, bit in enumerate(order)]
        across = [(bit, (rows >> len(order)) * cols * 4) for bit in extra]
        return down + across + down[::-1], len(down) + len(across)

    def arrival(message, now):
        bit, length = message
        takes, latest = length / rate, now
        for spot in spots:
            if bit == bits[2]:
                path = [(min(spot, spot ^ 1), spot % 2)]
            elif bit == bits[3]:
                path = [(at, 0) for at in range(spot, spot + 2)] if spot < 2 else [
                    (at, 1) for at in range(spot - 1, spot - 3, -1)
                ]
            else:
                path = [(bit, spot)]
            begin = now
            for link in path:
                key = (len(path) == 1 and bit != bits[2], link)
                begin = max(busy.get(key, 0.0), begin)
                busy[key] = begin + takes
                latest = max(latest, begin + takes)
        return latest + delay

    plans = [messages(number) for number in range(len(table))]
    waiting = []

    def take(item, now, steps):
        waiting.remove(item)
        _, number, stage = item
        sent, downs = plans[number]
        now += step_cost
        if 0 < stage <= downs:
            now += sent[stage - 1][1] / add_rate
        steps.append((number, stage))
        if stage < len(sent):
            waiting.append((arrival(sent[stage], now), number, stage + 1))
        return now

    def run_ready(now, steps):
        while True:
            ready = [item for item in waiting if item[0] <= now]
            if not ready:
                return now
            now = take(min(ready, key=urgency), now, steps)

    by_tick = {}
    now = start
    for name, takes in ticks:
        steps = by_tick[name] = []
        now += takes
        waiting.extend((now, number, 0) for number, entry in enumerate(table) if entry[5] == name)
        if name == ("free", 0):
            for item in sorted(waiting):
                while item[1] in freed and item[2] <= 5 + len(extra):
                    now = take(item, max(now, item[0]), steps)
                    item = waiting[-1]
        now = run_ready(now, steps)
    left = []
    while waiting:
        now = run_ready(max(now, min(waiting)[0]), left)
    return by_tick, left, now


def center_of(rows):
    center = rows - jnp.mean(rows, axis=-1, keepdims=True)
    inverse = lax.rsqrt(jnp.mean(center * center, axis=-1, keepdims=True) + eps)
    return center * inverse, inverse


def norm_back(grad_rows, unit_rows, inverse, norm_gain):
    scaled = grad_rows * norm_gain
    return inverse * (
        scaled
        - jnp.mean(scaled, axis=-1, keepdims=True)
        - unit_rows * jnp.mean(scaled * unit_rows, axis=-1, keepdims=True)
    )


def gelu_parts(before):
    normal_cdf = 0.5 * (1.0 + lax.erf(before * (1.0 / math.sqrt(2.0))))
    slope = normal_cdf + before * jnp.exp(-0.5 * before * before) * (1.0 / math.sqrt(2.0 * math.pi))
    return before * normal_cdf, slope


def column_sum(rows):
    return jnp.sum(rows, axis=0, keepdims=True)


def minus_in_three(column, first):
    lane = lax.broadcasted_iota(jnp.int32, (column.shape[0], PAIR), 1)
    high = (-column).astype(jnp.bfloat16).astype(jnp.float32)
    rest = -column - high
    middle = rest.astype(jnp.bfloat16).astype(jnp.float32)
    low = rest - middle
    zero = jnp.zeros((column.shape[0], PAIR), jnp.float32)
    tail = jnp.where(lane == 1, high, jnp.where(lane == 2, middle, jnp.where(lane == 3, low, zero)))
    return jnp.where(lane == 0, first, tail).astype(jnp.bfloat16)


class Row:
    def __init__(self, ref):
        self.ref = ref

    def __getitem__(self, _):
        return self.ref[...].reshape(1, self.ref.shape[0])


SMALL = (("norm1_gain", 0, 768), ("norm1_bias", 1, 768), ("query_bias", 2, 384), ("value_bias", 3, 384),
         ("output_bias", 4, 768), ("norm2_gain", 5, 768), ("norm2_bias", 6, 768), ("hidden_bias", 7, 1536),
         ("proj_bias", 8, 768))
ROW_OF = {name: row for name, row, _ in SMALL}


def unpack_kernel(packed, *vectors):
    at = 0
    for (_, _, count), vector in zip(SMALL, vectors):
        rows = count // 128
        vector[...] = packed[at : at + rows, :].reshape(count)
        at += rows


def layer_kernel(size, length_ref, *refs):
    (
        frames_in, cotangent_in, hidden_weight_in, proj_weight_in,
        gain_one, shift_one, query_bias, value_bias, output_bias, gain_two, shift_two, hidden_bias, proj_bias,
        query_weight_in, key_weight_in, value_weight_in, output_weight_in,
    ) = refs[:17]
    (
        block_out, input_grad, query_sum, key_sum, value_sum, output_sum, proj_sum, hidden_sum, small_sum,
        peer_mlp, peer_two, peer_one,
    ) = refs[17:29]
    gain_one, shift_one, query_bias, value_bias, output_bias, gain_two, shift_two, proj_bias = (
        Row(ref) for ref in (gain_one, shift_one, query_bias, value_bias, output_bias, gain_two, shift_two, proj_bias)
    )
    (
        left, right, resid, second, masked, hidden_w, proj_w, queries, keys, values, lse_terms, attended, key_terms,
        grad_proj, grad_hidden, *land_hidden, land_attend, land_output, land_small,
        fetched, staged, small, packed, query_weight, key_weight, value_weight, output_weight,
        load_sems, fetch_sem, stage_sem, peer_send, peer_recv, unit_send, unit_recv, unit_own,
    ) = refs[29:]
    me, core = lax.axis_index("dp"), lax.axis_index("tensor")
    total_rows = frames_in.shape[0]
    blocks, pieces = total_rows // BLOCK, total_rows // PIECE
    length = length_ref[0]
    orders, extra = orders_of(size)
    chunks = chunk_list()
    table = unit_table()

    pairs = [
        (frames_in.at[pl.ds(block * BLOCK, BLOCK), :], second.at[pl.ds(block * BLOCK, BLOCK), :])
        for block in range(blocks)
    ]
    pairs += [
        (query_weight_in, query_weight), (key_weight_in, key_weight), (value_weight_in, value_weight),
        (output_weight_in, output_weight), (cotangent_in, masked), (hidden_weight_in, hidden_w),
        (proj_weight_in, proj_w), (frames_in, masked),
    ]
    loads = [
        pltpu.make_async_copy(source, target, load_sems.at[at]) for at, (source, target) in enumerate(pairs)
    ]
    first_loads, weight_loads, later_loads = loads[:blocks], loads[blocks : blocks + 3], loads[blocks + 3 : -1]
    for load in first_loads[:1] + weight_loads + first_loads[1:]:
        load.start()
    barrier = pltpu.get_barrier_semaphore()
    for bit in dp_bits(size):
        pl.semaphore_signal(barrier, inc=1, device_id=(partner_of(me, bit), core), device_id_type=MESH_ID)
    pl.semaphore_signal(barrier, inc=1, device_id=(me, 1 - core), device_id_type=MESH_ID)

    held = {
        "output": (resid, output_sum),
        "query": (grad_proj, query_sum), "key": (grad_proj, key_sum),
        "value": (grad_hidden, value_sum), "small": (packed, small_sum),
    }
    lands = {"output": land_output, "small": land_small}
    for group in range(len(CHUNKS)):
        held["proj", group], held["hidden", group] = (grad_proj, proj_sum), (grad_hidden, hidden_sum)
        lands["proj", group], lands["hidden", group] = land_hidden[2 * group : 2 * group + 2]
    used = {}
    units = []
    for number, (name, place, total_place, shape, kind, _) in enumerate(table):
        shelf = lands.get(name, land_attend)
        key = name if name in lands else "attend"
        slot = used.get(key, 0)
        used[key] = slot + 1
        buffer, total = held[name]
        units.append(
            Unit(
                buffer, total, (place, total_place), shape, orders[order_kind(number, kind)], extra, shelf.at[slot],
                (unit_send.at[number], unit_recv.at[number], unit_own.at[number]), me, core,
            )
        )
    ticks = []
    for number, (_, _, _, width) in enumerate(chunks):
        for block in range(blocks):
            name = ("hidden", number) if block == blocks - 1 else ("ffn", (number, block))
            ticks.append((name, FFN_US * width / 512))
    ticks += [(("back", step), BACK_US) for step in range(pieces)] + [(("output", 0), OUTPUT_US)]
    ticks += [(("attn", step), ATTEND_US) for step in range(3 * pieces)] + [(("free", 0), 0.0)]
    ticks += [(("first", step) if step < pieces - 1 else ("attend", 0), FIRST_US) for step in range(pieces)]
    ticks += [(("last", step) if step < pieces - 1 else ("small", 0), LAST_US) for step in range(pieces)]
    freed = [
        at
        for at, (name, (row, col), _, _, _, _) in enumerate(table)
        if (name[0] == "proj" and row < frames_in.shape[1]) or (name[0] == "hidden" and col < 384)
    ]
    by_tick, remaining, _ = plan_units(size, ticks, table, freed, 0.0)

    def run(steps):
        for number, stage in steps:
            units[number].advance(stage)

    def tick(step, count, name_of):
        for at in range(count):
            steps = by_tick[name_of(at)]
            if steps:
                @pl.when(step == at)
                def _(steps=steps):
                    run(steps)

    def to_peer(source, target, at):
        return pltpu.make_async_remote_copy(
            src_ref=source, dst_ref=target, send_sem=peer_send.at[at], recv_sem=peer_recv.at[at],
            device_id=(me, 1 - core), device_id_type=MESH_ID,
        )

    def rows_at(step, count):
        return pl.ds(pl.multiple_of(step * count, count), count)

    lane = lax.broadcasted_iota(jnp.int32, (1, PAIR), 1)
    heads = (lane < HD, lane >= HD)
    small[...] = jnp.zeros_like(small)
    packed[...] = jnp.zeros_like(packed)

    def add_small(name, value, at=0):
        row = ROW_OF[name]
        index = (slice(row, row + 1), pl.ds(at, value.shape[1]))
        small[index] = small[index] + value

    place = lax.broadcasted_iota(jnp.int32, (total_rows, PAIR), 0)
    column = lax.broadcasted_iota(jnp.int32, (total_rows, PAIR), 1)
    key_terms[...] = jnp.where(
        column == 0, jnp.where(place >= length, masked_value, 0.0), jnp.where(column < 4, 1.0, 0.0)
    ).astype(jnp.bfloat16)
    def normed_block(step):
        first_loads[step].wait()
        unit_rows, _ = center_of(second[pl.ds(step * BLOCK, BLOCK), :].astype(jnp.float32))
        return (unit_rows * gain_one[...] + shift_one[...]).astype(jnp.bfloat16)

    upcoming = normed_block(0)
    for load in weight_loads:
        load.wait()
    for step in range(blocks):
        first_in = upcoming
        if step < blocks - 1:
            upcoming = normed_block(step + 1)
        if step == blocks - 2:
            for load in later_loads:
                load.start()
        rows = pl.ds(step * BLOCK, BLOCK)
        queries[rows, :] = ((dot(first_in, query_weight[...]) + query_bias[...]) * score_scale).astype(jnp.bfloat16)
        keys[rows, :] = dot(first_in, key_weight[...]).astype(jnp.bfloat16)
        values[rows, :] = (dot(first_in, value_weight[...]) + value_bias[...]).astype(jnp.bfloat16)

    first_term = jnp.where(lax.broadcasted_iota(jnp.int32, (BLOCK, PAIR), 1) == 0, 1.0, 0.0).astype(jnp.bfloat16)
    ones = jnp.ones((total_rows, PAIR), jnp.bfloat16)
    later_loads[0].wait()
    pl.semaphore_wait(barrier, len(dp_bits(size)) + 1)

    @pl.loop(0, blocks)
    def _(step):
        rows = rows_at(step, BLOCK)

        def scores_of(number):
            cols = pl.ds((number // 2) * PAIR, PAIR)
            query_pair = queries[rows, cols]
            query_one = jnp.where(heads[number % 2], query_pair, jnp.zeros_like(query_pair))
            key_all = jnp.concatenate([keys[:, cols], key_terms[...]], axis=1)
            return dot(jnp.concatenate([query_one, first_term], axis=1), key_all, NT)

        mixed = []
        upcoming = scores_of(0)
        for number in range(6):
            scores = scores_of(number) if extra and number else upcoming
            if number < 5 and not extra:
                upcoming = scores_of(number + 1)
            cols = pl.ds((number // 2) * PAIR, PAIR)
            maxima = jnp.max(scores, axis=1, keepdims=True)
            weights = jnp.exp(scores - maxima).astype(jnp.bfloat16)
            mixture = dot(weights, jnp.concatenate([values[:, cols], ones], axis=1))
            totals = mixture[:, PAIR:]
            mixed.append(mixture[:, :PAIR] / totals)
            lse_terms[rows, pl.ds(number * PAIR, PAIR)] = minus_in_three(maxima + jnp.log(totals), 1.0)
            if number % 2:
                attended[rows, cols] = jnp.where(heads[0], mixed[-2], mixed[-1]).astype(jnp.bfloat16)

        right[rows, :] = dot(attended[rows, :], output_weight[...])
        to_peer(right.at[rows, :], left.at[rows, :], step).start()

    for load in later_loads[1:]:
        load.wait()

    def feed_forward(group, step):
        width, count = CHUNKS[group]
        first = sum(chunk_count for _, chunk_count in CHUNKS[:group])
        base = chunks[first][2]
        chunk, block = first + step // blocks, step % blocks
        rows = rows_at(block, BLOCK)
        units_of = pl.ds(pl.multiple_of(base + (step // blocks) * width, 256), width)

        @pl.when(chunk == 0)
        def _():
            to_peer(right.at[rows, :], left.at[rows, :], block).wait()
            for half in range(BLOCK // PIECE):
                part = pl.ds(pl.multiple_of(block * BLOCK + half * PIECE, PIECE), PIECE)
                total = second[part, :].astype(jnp.float32) + (right[part, :] + left[part, :]) + output_bias[...]
                resid[part, :] = total
                unit_rows, _ = center_of(total)
                second[part, :] = (unit_rows * gain_two[...] + shift_two[...]).astype(jnp.bfloat16)
                live = lax.broadcasted_iota(jnp.int32, (PIECE, 1), 0) + (block * BLOCK + half * PIECE) < length
                grad_raw = masked[part, :]
                grad_f = jnp.where(live, grad_raw.astype(jnp.float32), 0.0)
                masked[part, :] = grad_f.astype(jnp.bfloat16)
                add_small("proj_bias", column_sum(grad_f))

        rows_in = second[rows, :]
        grad_in = masked[rows, :]
        up, down = hidden_w[:, units_of], proj_w[units_of, :]
        active_f, slope = gelu_parts(dot(rows_in, up) + hidden_bias[units_of].reshape(1, width))
        active = active_f.astype(jnp.bfloat16)
        grad_pre = dot(grad_in, down, NT) * slope
        grad_pre_b = grad_pre.astype(jnp.bfloat16)
        bias_at = (slice(ROW_OF["hidden_bias"], ROW_OF["hidden_bias"] + 1), units_of)
        small[bias_at] = small[bias_at] + column_sum(grad_pre)

        @pl.when(chunk == 0)
        def _():
            left[rows, :] = dot(active, down)
            right[rows, :] = dot(grad_pre_b, up, NT)

        @pl.when(chunk > 0)
        def _():
            left[rows, :] = left[rows, :] + dot(active, down)
            right[rows, :] = right[rows, :] + dot(grad_pre_b, up, NT)

        @pl.when(block == 0)
        def _():
            grad_proj[units_of, :] = dot(active, grad_in, TN)
            grad_hidden[:, units_of] = dot(rows_in, grad_pre_b, TN)

        @pl.when(block > 0)
        def _():
            grad_proj[units_of, :] = grad_proj[units_of, :] + dot(active, grad_in, TN)
            grad_hidden[:, units_of] = grad_hidden[:, units_of] + dot(rows_in, grad_pre_b, TN)

        @pl.when(chunk == len(chunks) - 1)
        def _():
            for half in range(BLOCK // PIECE):
                piece = block * (BLOCK // PIECE) + half
                part = rows_at(piece, PIECE)
                to_peer(right.at[part, :], peer_two.at[part, :], blocks + piece).start()
                to_peer(left.at[part, :], peer_mlp.at[part, :], blocks + pieces + piece).start()

        def name_of(at):
            number = first + at // blocks
            return ("hidden", number) if at % blocks == blocks - 1 else ("ffn", (number, at % blocks))

        tick(step, count * blocks, name_of)

    for group, (_, count) in enumerate(CHUNKS):
        pl.loop(0, count * blocks)(functools.partial(feed_forward, group))

    def fetch(source, part, at):
        return pltpu.make_async_copy(source.at[part, :], fetched.at[at], fetch_sem.at[at])

    def store(value, target, part):
        staged[...] = value.astype(jnp.bfloat16)
        copy = pltpu.make_async_copy(staged, target.at[part, :], stage_sem)
        copy.start()
        copy.wait()

    @pl.loop(0, pieces)
    def _(piece):
        part = rows_at(piece, PIECE)
        to_peer(right.at[part, :], peer_two.at[part, :], blocks + piece).wait()
        fetch(peer_two, part, 0).start()
        to_peer(left.at[part, :], peer_mlp.at[part, :], blocks + pieces + piece).wait()
        fetch(peer_mlp, part, 1).start()
        rows_f = resid[part, :]
        unit_rows, inverse = center_of(rows_f)
        fetch(peer_two, part, 0).wait()
        grad_two = right[part, :] + fetched[0]
        grad_rows = masked[part, :].astype(jnp.float32) + norm_back(grad_two, unit_rows, inverse, gain_two[...])
        add_small("norm2_gain", column_sum(grad_two * unit_rows))
        add_small("norm2_bias", column_sum(grad_two))
        add_small("output_bias", column_sum(grad_rows))
        right[part, :] = grad_rows
        grad_b = grad_rows.astype(jnp.bfloat16)
        masked[part, :] = grad_b
        proj_w[part, 0:384] = dot(grad_b, output_weight[...], NT).astype(jnp.bfloat16)
        fetch(peer_mlp, part, 1).wait()
        store(rows_f + (left[part, :] + fetched[1]) + proj_bias[...], block_out, part)
        tick(piece, pieces, lambda at: ("back", at))

    resid[0:384, :] = dot(attended[...], masked[...], TN)
    run(by_tick[("output", 0)])

    again = loads[-1]
    again.start()
    for pair in range(3):
        hidden_w[pair * PAIR : (pair + 1) * PAIR, :] = keys[:, pair * PAIR : (pair + 1) * PAIR].T
    top = lax.broadcasted_iota(jnp.int32, (PAIR, 1), 0) < HD

    @pl.loop(0, 3 * pieces)
    def _(step):
        pair, piece = step // pieces, step % pieces
        part = rows_at(piece, PIECE)
        cols = pl.ds(pl.multiple_of(pair * PAIR, PAIR), PAIR)
        query_pair = queries[part, cols]
        grad_pair = proj_w[part, cols]
        product = grad_pair.astype(jnp.float32) * attended[part, cols].astype(jnp.float32)
        key_all = jnp.concatenate([keys[:, cols], key_terms[...]], axis=1)
        value_all = jnp.concatenate([values[:, cols], ones], axis=1)
        key_rows = hidden_w[cols, :]
        grad_values, grad_keys, grad_queries = 0.0, 0.0, []
        for head in range(2):
            mine = heads[head]
            query_one = jnp.where(mine, query_pair, jnp.zeros_like(query_pair))
            grad_one = jnp.where(mine, grad_pair, jnp.zeros_like(grad_pair))
            delta = jnp.sum(jnp.where(mine, product, 0.0), axis=1, keepdims=True)
            terms = lse_terms[part, pl.ds(pl.multiple_of((2 * pair + head) * PAIR, PAIR), PAIR)]
            probs = jnp.exp(dot(key_all, jnp.concatenate([query_one, terms], axis=1), NT))
            shifted = dot(value_all, jnp.concatenate([grad_one, minus_in_three(delta, 0.0)], axis=1), NT)
            grad_scores = (probs * shifted).astype(jnp.bfloat16)
            grad_values = grad_values + dot(probs.astype(jnp.bfloat16), grad_one)
            grad_keys = grad_keys + dot(grad_scores, query_one)
            grad_queries.append(dot(key_rows, grad_scores))
        grad_query = (jnp.where(top, grad_queries[0], grad_queries[1]) * score_scale).T
        second[part, cols] = grad_query.astype(jnp.bfloat16)
        bias_at = (slice(ROW_OF["query_bias"], ROW_OF["query_bias"] + 1), cols)
        small[bias_at] = small[bias_at] + column_sum(grad_query)

        @pl.when(piece == 0)
        def _():
            left[:, 0:PAIR] = grad_values
            left[:, PAIR : 2 * PAIR] = grad_keys

        @pl.when(piece > 0)
        def _():
            left[:, 0:PAIR] = left[:, 0:PAIR] + grad_values
            left[:, PAIR : 2 * PAIR] = left[:, PAIR : 2 * PAIR] + grad_keys

        @pl.when(piece == pieces - 1)
        def _():
            grad_all = left[:, 0:PAIR]
            bias_at = (slice(ROW_OF["value_bias"], ROW_OF["value_bias"] + 1), cols)
            small[bias_at] = column_sum(grad_all)
            proj_w[:, pl.ds(pl.multiple_of(384 + pair * PAIR, PAIR), PAIR)] = grad_all.astype(jnp.bfloat16)
            second[:, pl.ds(pl.multiple_of(384 + pair * PAIR, PAIR), PAIR)] = left[:, PAIR : 2 * PAIR].astype(
                jnp.bfloat16
            )

        tick(step, 3 * pieces, lambda at: ("attn", at))

    again.wait()
    run(by_tick[("free", 0)])

    @pl.loop(0, pieces)
    def _(piece):
        part = rows_at(piece, PIECE)
        unit_rows, _ = center_of(masked[part, :].astype(jnp.float32))
        first_in = (unit_rows * gain_one[...] + shift_one[...]).astype(jnp.bfloat16)
        grad_query, grad_key = second[part, 0:384], second[part, 384:768]
        grad_value = proj_w[part, 384:768]
        left[part, :] = (
            dot(grad_query, query_weight[...], NT)
            + dot(grad_key, key_weight[...], NT)
            + dot(grad_value, value_weight[...], NT)
        )
        to_peer(left.at[part, :], peer_one.at[part, :], blocks + 2 * pieces + piece).start()
        terms = [dot(first_in, grad, TN) for grad in (grad_query, grad_key, grad_value)]
        width = frames_in.shape[1]
        targets = (
            (grad_proj, (slice(0, width), slice(0, 384))),
            (grad_proj, (slice(0, width), slice(384, 768))),
            (grad_hidden, (slice(0, width), slice(0, 384))),
        )

        @pl.when(piece == 0)
        def _():
            for (ref, index), term in zip(targets, terms):
                ref[index] = term

        @pl.when(piece > 0)
        def _():
            for (ref, index), term in zip(targets, terms):
                ref[index] = ref[index] + term

        tick(piece, pieces, lambda at: ("first", at) if at < pieces - 1 else ("attend", 0))

    @pl.loop(0, pieces)
    def _(piece):
        part = rows_at(piece, PIECE)
        to_peer(left.at[part, :], peer_one.at[part, :], blocks + 2 * pieces + piece).wait()
        fetch(peer_one, part, 0).start()
        unit_rows, inverse = center_of(masked[part, :].astype(jnp.float32))
        fetch(peer_one, part, 0).wait()
        grad_one = left[part, :] + fetched[0]
        add_small("norm1_gain", column_sum(grad_one * unit_rows))
        add_small("norm1_bias", column_sum(grad_one))
        store(right[part, :] + norm_back(grad_one, unit_rows, inverse, gain_one[...]), input_grad, part)

        @pl.when(piece == pieces - 1)
        def _():
            at = 0
            for _, row, count in SMALL:
                for start in range(0, count, 128):
                    packed[at : at + 1, :] = small[row : row + 1, start : start + 128]
                    at += 1

        tick(piece, pieces, lambda at: ("last", at) if at < pieces - 1 else ("small", 0))

    run(remaining)


VMEM_BYTES = 64 * 2**20
FFN_US, BACK_US, OUTPUT_US, ATTEND_US, FIRST_US, LAST_US = 4.0, 1.4, 1.0, 2.5, 2.0, 2.0
RATES = (46e3, 1.0, 0.05, 2e6)


def urgency(item):
    return (item[1], item[0])


def on_device(
    size,
    frames,
    lengths,
    cotangent,
    norm1_gain,
    norm1_bias,
    query_weight,
    query_bias,
    key_weight,
    value_weight,
    value_bias,
    output_weight,
    output_bias,
    norm2_gain,
    norm2_bias,
    hidden_weight,
    hidden_bias,
    proj_weight,
    proj_bias,
):
    rows, width = frames.shape[1:]
    part = query_weight.shape[1]
    hidden = hidden_weight.shape[1]
    f32, bf16 = jnp.float32, jnp.bfloat16
    extra = orders_of(size)[1]
    units = len(unit_table())
    chunk_lands = []
    for chunk, count in CHUNKS:
        chunk_lands.append(pltpu.VMEM((3 * count, landing_rows(chunk, extra), 256), f32))
        chunk_lands.append(pltpu.VMEM((3 * count, landing_rows(256, extra), chunk), f32))
    stages = 8 + len(extra)
    pieces = rows // PIECE
    shape = jax.ShapeDtypeStruct
    anywhere = pl.BlockSpec(memory_space=pl.ANY)
    inside = pl.BlockSpec(memory_space=pltpu.VMEM)
    dma = pltpu.SemaphoreType.DMA
    results = pl.pallas_call(
        functools.partial(layer_kernel, size),
        out_shape=[
            shape((rows, width), bf16), shape((rows, width), bf16),
            shape((width, part), f32), shape((width, part), f32), shape((width, part), f32), shape((part, width), f32),
            shape((hidden, width), f32), shape((width, hidden), f32), shape((128, 128), f32),
            shape((rows, width), f32), shape((rows, width), f32), shape((rows, width), f32),
        ],
        in_specs=[pl.BlockSpec(memory_space=pltpu.SMEM)] + [anywhere] * 4 + [inside] * 9 + [anywhere] * 4,
        out_specs=[anywhere] * 12,
        scratch_shapes=[
            pltpu.VMEM((rows, width), f32), pltpu.VMEM((rows, width), f32), pltpu.VMEM((rows, width), f32),
            pltpu.VMEM((rows, width), bf16), pltpu.VMEM((rows, width), bf16),
            pltpu.VMEM((width, hidden), bf16), pltpu.VMEM((hidden, width), bf16),
            pltpu.VMEM((rows, part), bf16), pltpu.VMEM((rows, part), bf16), pltpu.VMEM((rows, part), bf16),
            pltpu.VMEM((rows, 2 * part), bf16), pltpu.VMEM((rows, part), bf16), pltpu.VMEM((rows, PAIR), bf16),
            pltpu.VMEM((hidden, width), f32), pltpu.VMEM((width, hidden), f32),
            *chunk_lands,
            pltpu.VMEM((9, landing_rows(256, extra), 384), f32),
            pltpu.VMEM((3, landing_rows(384, extra), 256), f32),
            pltpu.VMEM((1, landing_rows(128, extra), 128), f32),
            pltpu.VMEM((2, PIECE, width), f32), pltpu.VMEM((PIECE, width), bf16),
            pltpu.VMEM((16, hidden), f32), pltpu.VMEM((128, 128), f32),
            *[pltpu.VMEM((width, part), bf16)] * 3, pltpu.VMEM((part, width), bf16),
            dma((rows // BLOCK + 8,)), dma((2,)), dma, dma((3 * pieces + rows // BLOCK,)), dma((3 * pieces + rows // BLOCK,)),
            dma((units,)), dma((units, stages)), dma((units,)),
        ],
        compiler_params=pltpu.CompilerParams(
            collective_id=0, has_side_effects=True, vmem_limit_bytes=VMEM_BYTES
        ),
        name="layer",
    )(
        lengths, frames[0], cotangent[0], hidden_weight, proj_weight,
        norm1_gain, norm1_bias, query_bias, value_bias, output_bias,
        norm2_gain, norm2_bias, hidden_bias, proj_bias,
        query_weight, key_weight, value_weight, output_weight,
    )
    block_out, input_grad, query_w, key_w, value_w, output_w, proj_w, hidden_w, packed = results[:9]
    vectors = pl.pallas_call(
        unpack_kernel, out_shape=[shape((count,), f32) for _, _, count in SMALL], name="unpack"
    )(packed)
    small = {name: vector for (name, _, _), vector in zip(SMALL, vectors)}
    return (
        block_out[None], input_grad[None],
        small["norm1_gain"], small["norm1_bias"],
        query_w, small["query_bias"], key_w, value_w, small["value_bias"],
        output_w, small["output_bias"], small["norm2_gain"], small["norm2_bias"],
        hidden_w, small["hidden_bias"], proj_w, small["proj_bias"],
    )


def solution(mesh):
    placed = (
        P("dp", None, None),
        P("dp"),
        P("dp", None, None),
        P(),
        P(),
        P(None, "tensor"),
        P("tensor"),
        P(None, "tensor"),
        P(None, "tensor"),
        P("tensor"),
        P("tensor", None),
        P(),
        P(),
        P(),
        P(None, "tensor"),
        P("tensor"),
        P("tensor", None),
        P(),
    )
    return jax.shard_map(
        functools.partial(on_device, mesh.shape["dp"]),
        mesh=mesh,
        in_specs=placed,
        out_specs=(
            P("dp", None, None),
            P("dp", None, None),
            P(),
            P(),
            P(None, "tensor"),
            P("tensor"),
            P(None, "tensor"),
            P(None, "tensor"),
            P("tensor"),
            P("tensor", None),
            P(),
            P(),
            P(),
            P(None, "tensor"),
            P("tensor"),
            P("tensor", None),
            P(),
        ),
        check_vma=False,
    )
```

```python
import functools
import math

import jax
import jax.numpy as jnp
from jax import lax
from jax.experimental import pallas as pl
from jax.experimental.pallas import tpu as pltpu
from jax.sharding import PartitionSpec as P

HD = 64
PAIR = 2 * HD
CHUNKS = ((256, 2), (512, 2))
BLOCK = 512
PIECE = 256

eps = 1e-05
score_scale = 0.125
masked_value = -1e30

MESH_ID = pl.DeviceIdType.MESH
NN = (((1,), (0,)), ((), ()))
NT = (((1,), (1,)), ((), ()))
TN = (((0,), (0,)), ((), ()))


def dot(left, right, form=NN):
    return lax.dot_general(left, right, form, preferred_element_type=jnp.float32)


def bit_of(index, bit):
    return (index // bit) % 2


def partner_of(index, bit):
    return index + bit - 2 * bit * bit_of(index, bit)


def dp_bits(size):
    return [1 << power for power in range(size.bit_length() - 1)]


def orders_of(size):
    bits = dp_bits(size)
    a, b, c, d = bits[:4]
    orders = [
        [a, b, c, d], [b, a, c, d], [c, a, b, d], [c, b, a, d],
        [a, c, b, d], [b, c, a, d], [c, d, a, b], [c, d, b, a],
    ]
    return orders, bits[4:]


def landing_rows(rows, extra):
    return rows - (rows >> 4) + len(extra) * (rows >> 4)


class Unit:
    def __init__(self, buffer, total, place, shape, order, extra, landing, sems, me, core):
        (self.row, self.col), (self.total_row, self.total_col) = place
        self.rows, self.cols = shape
        self.buffer, self.total, self.landing = buffer, total, landing
        self.order, self.extra = order, extra
        self.send_sem, self.recv_sems, self.own_sem = sems
        self.me, self.core = me, core
        self.offsets = [0]
        self.lands = [0]
        for step, bit in enumerate(order):
            self.offsets.append(self.offsets[-1] + bit_of(me, bit) * (self.rows >> (step + 1)))
            self.lands.append(self.lands[-1] + (self.rows >> (step + 1)))
        self.stages = 2 * len(order) + len(extra)

    def held(self, offset, length):
        return (pl.ds(pl.multiple_of(self.row + offset, 8), length), pl.ds(self.col, self.cols))

    def final(self, offset, length):
        index = (pl.ds(pl.multiple_of(self.total_row + offset, 8), length), pl.ds(self.total_col, self.cols))
        return self.total.at[index]

    def landed(self, start, length):
        return (pl.ds(start, length), pl.ds(0, self.cols))

    def own_copy(self):
        length = self.rows >> len(self.order)
        return pltpu.make_async_copy(
            self.buffer.at[self.held(self.offsets[-1], length)],
            self.final(self.offsets[-1], length),
            self.own_sem,
        )

    def copy(self, stage):
        halvings = len(self.order)
        doublings = len(self.extra)
        if stage < halvings:
            bit = self.order[stage]
            length = self.rows >> (stage + 1)
            away = self.offsets[stage] + (1 - bit_of(self.me, bit)) * length
            source = self.buffer.at[self.held(away, length)]
            target = self.landing.at[self.landed(self.lands[stage], length)]
        elif stage < halvings + doublings:
            bit = self.extra[stage - halvings]
            length = self.rows >> halvings
            source = self.buffer.at[self.held(self.offsets[-1], length)]
            target = self.landing.at[self.landed(self.lands[-1] + (stage - halvings) * length, length)]
        else:
            step = 2 * halvings + doublings - 1 - stage
            bit = self.order[step]
            length = self.rows >> (step + 1)
            target = self.final(self.offsets[step + 1], length)
            source = target
            if step == halvings - 1:
                source = self.buffer.at[self.held(self.offsets[step + 1], length)]
        return pltpu.make_async_remote_copy(
            src_ref=source,
            dst_ref=target,
            send_sem=self.send_sem,
            recv_sem=self.recv_sems.at[stage],
            device_id=(partner_of(self.me, bit), self.core),
            device_id_type=MESH_ID,
        )

    def advance(self, stage):
        halvings = len(self.order)
        doublings = len(self.extra)
        if stage > 0:
            self.copy(stage - 1).wait()
            if stage <= halvings + doublings:
                step = min(stage, halvings)
                length = self.rows >> step
                if stage <= halvings:
                    land = self.lands[stage - 1]
                else:
                    land = self.lands[-1] + (stage - 1 - halvings) * length
                index = self.held(self.offsets[step], length)
                self.buffer[index] = self.buffer[index] + self.landing[self.landed(land, length)]
            if stage == halvings + doublings:
                self.own_copy().start()
            if stage == halvings + doublings + 1:
                self.own_copy().wait()
        if stage < self.stages:
            self.copy(stage).start()


def chunk_list():
    out, base = [], 0
    for group, (width, count) in enumerate(CHUNKS):
        for at in range(count):
            out.append((group, at, base, width))
            base += width
    return out


def unit_table():
    table = []
    for number, (group, _, base, width) in enumerate(chunk_list()):
        for c in range(3):
            place = (base, 256 * c)
            table.append((("proj", group), place, place, (width, 256), ("hidden", number)))
        for c in range(3):
            place = (256 * c, base)
            table.append((("hidden", group), place, place, (256, width), ("hidden", number)))
    for c in range(3):
        table.append(("output", (0, 256 * c), (0, 256 * c), (384, 256), ("output", 0)))
    for name, col in (("query", 0), ("key", 384), ("value", 0)):
        for c in range(3):
            table.append((name, (256 * c, col), (256 * c, 0), (256, 384), ("attend", 0)))
    table.append(("small", (0, 0), (0, 0), (128, 128), ("small", 0)))
    return table


def plan_units(size, ticks, table, freed, start):
    orders, extra = orders_of(size)
    bits = dp_bits(size)
    rate, delay, step_cost, add_rate = RATES
    spots = range(4)
    busy = {}

    def messages(number):
        _, _, _, (rows, cols), _ = table[number]
        order = orders[KINDS[number]]
        down = [(bit, (rows >> (step + 1)) * cols * 4) for step, bit in enumerate(order)]
        across = [(bit, (rows >> len(order)) * cols * 4) for bit in extra]
        return down + across + down[::-1], len(down) + len(across)

    def arrival(message, now):
        bit, length = message
        takes, latest = length / rate, now
        for spot in spots:
            if bit == bits[2]:
                path = [(min(spot, spot ^ 1), spot % 2)]
            elif bit == bits[3]:
                path = [(at, 0) for at in range(spot, spot + 2)] if spot < 2 else [
                    (at, 1) for at in range(spot - 1, spot - 3, -1)
                ]
            else:
                path = [(bit, spot)]
            begin = now
            for link in path:
                key = (len(path) == 1 and bit != bits[2], link)
                begin = max(busy.get(key, 0.0), begin)
                busy[key] = begin + takes
                latest = max(latest, begin + takes)
        return latest + delay

    plans = [messages(number) for number in range(len(table))]
    waiting = []

    def take(item, now, steps):
        waiting.remove(item)
        _, number, stage = item
        sent, downs = plans[number]
        now += step_cost
        if 0 < stage <= downs:
            now += sent[stage - 1][1] / add_rate
        steps.append((number, stage))
        if stage < len(sent):
            waiting.append((arrival(sent[stage], now), number, stage + 1))
        return now

    def run_ready(now, steps):
        while True:
            ready = [item for item in waiting if item[0] <= now]
            if not ready:
                return now
            now = take(min(ready, key=urgency), now, steps)

    by_tick = {}
    now = start
    for name, takes in ticks:
        steps = by_tick[name] = []
        now += takes
        waiting.extend((now, number, 0) for number, entry in enumerate(table) if entry[4] == name)
        if name == ("free", 0):
            for item in sorted(waiting):
                while item[1] in freed and item[2] <= 5 + len(extra):
                    now = take(item, max(now, item[0]), steps)
                    item = waiting[-1]
        now = run_ready(now, steps)
    left = []
    while waiting:
        now = run_ready(max(now, min(waiting)[0]), left)
    return by_tick, left, now


def center_of(rows):
    center = rows - jnp.mean(rows, axis=-1, keepdims=True)
    inverse = lax.rsqrt(jnp.mean(center * center, axis=-1, keepdims=True) + eps)
    return center * inverse, inverse


def norm_back(grad_rows, unit_rows, inverse, norm_gain):
    scaled = grad_rows * norm_gain
    return inverse * (
        scaled
        - jnp.mean(scaled, axis=-1, keepdims=True)
        - unit_rows * jnp.mean(scaled * unit_rows, axis=-1, keepdims=True)
    )


def gelu_parts(before):
    normal_cdf = 0.5 * (1.0 + lax.erf(before * (1.0 / math.sqrt(2.0))))
    slope = normal_cdf + before * jnp.exp(-0.5 * before * before) * (1.0 / math.sqrt(2.0 * math.pi))
    return before * normal_cdf, slope


def column_sum(rows):
    return jnp.sum(rows, axis=0, keepdims=True)


def minus_in_three(column, first):
    lane = lax.broadcasted_iota(jnp.int32, (column.shape[0], PAIR), 1)
    high = (-column).astype(jnp.bfloat16).astype(jnp.float32)
    rest = -column - high
    middle = rest.astype(jnp.bfloat16).astype(jnp.float32)
    low = rest - middle
    zero = jnp.zeros((column.shape[0], PAIR), jnp.float32)
    tail = jnp.where(lane == 1, high, jnp.where(lane == 2, middle, jnp.where(lane == 3, low, zero)))
    return jnp.where(lane == 0, first, tail).astype(jnp.bfloat16)


class Row:
    def __init__(self, ref):
        self.ref = ref

    def __getitem__(self, _):
        return self.ref[...].reshape(1, self.ref.shape[0])


SMALL = (("norm1_gain", 0, 768), ("norm1_bias", 1, 768), ("query_bias", 2, 384), ("value_bias", 3, 384),
         ("output_bias", 4, 768), ("norm2_gain", 5, 768), ("norm2_bias", 6, 768), ("hidden_bias", 7, 1536),
         ("proj_bias", 8, 768))
ROW_OF = {name: row for name, row, _ in SMALL}


def unpack_kernel(packed, *vectors):
    at = 0
    for (_, _, count), vector in zip(SMALL, vectors):
        rows = count // 128
        vector[...] = packed[at : at + rows, :].reshape(count)
        at += rows


def layer_kernel(size, length_ref, *refs):
    (
        frames_in, cotangent_in, hidden_weight_in, proj_weight_in,
        *vectors_in,
        query_weight_in, key_weight_in, value_weight_in, output_weight_in,
    ) = refs[:17]
    vectors = refs[-9:]
    gain_one, shift_one, query_bias, value_bias, output_bias, gain_two, shift_two, hidden_bias, proj_bias = vectors
    (
        block_out, input_grad, query_sum, key_sum, value_sum, output_sum, proj_sum, hidden_sum, small_sum,
        peer_mlp, peer_two, peer_one,
    ) = refs[17:29]
    gain_one, shift_one, query_bias, value_bias, output_bias, gain_two, shift_two, proj_bias = (
        Row(ref) for ref in (gain_one, shift_one, query_bias, value_bias, output_bias, gain_two, shift_two, proj_bias)
    )
    (
        left, right, resid, second, masked, hidden_w, proj_w, queries, keys, values, lse_terms, attended, key_terms,
        grad_proj, grad_hidden, *land_hidden, land_attend, land_output, land_small,
        fetched, staged, small, packed, query_weight, key_weight, value_weight, output_weight,
        load_sems, fetch_sem, stage_sem, peer_send, peer_recv, unit_send, unit_recv, unit_own,
    ) = refs[29:-9]
    me, core = lax.axis_index("dp"), lax.axis_index("tensor")
    total_rows = frames_in.shape[0]
    blocks, pieces = total_rows // BLOCK, total_rows // PIECE
    length = length_ref[0]
    orders, extra = orders_of(size)
    chunks = chunk_list()
    table = unit_table()

    pairs = [
        (frames_in.at[pl.ds(block * BLOCK, BLOCK), :], second.at[pl.ds(block * BLOCK, BLOCK), :])
        for block in range(blocks)
    ]
    pairs += [
        (query_weight_in, query_weight), (key_weight_in, key_weight), (value_weight_in, value_weight),
        (output_weight_in, output_weight), (cotangent_in, masked), (hidden_weight_in, hidden_w),
        (proj_weight_in, proj_w), (frames_in, masked),
    ]
    loads = [
        pltpu.make_async_copy(source, target, load_sems.at[at]) for at, (source, target) in enumerate(pairs)
    ]
    first_loads, weight_loads, later_loads = loads[:blocks], loads[blocks : blocks + 3], loads[blocks + 3 : -1]
    vector_loads = [
        pltpu.make_async_copy(source, target, load_sems.at[len(pairs) + at])
        for at, (source, target) in enumerate(zip(vectors_in, vectors))
    ]
    weight_loads = vector_loads + weight_loads
    for load in vector_loads + first_loads[:1] + weight_loads[9:] + first_loads[1:]:
        load.start()
    barrier = pltpu.get_barrier_semaphore()
    for bit in dp_bits(size):
        pl.semaphore_signal(barrier, inc=1, device_id=(partner_of(me, bit), core), device_id_type=MESH_ID)
    pl.semaphore_signal(barrier, inc=1, device_id=(me, 1 - core), device_id_type=MESH_ID)

    held = {
        "output": (resid, output_sum),
        "query": (grad_proj, query_sum), "key": (grad_proj, key_sum),
        "value": (grad_hidden, value_sum), "small": (packed, small_sum),
    }
    lands = {"output": land_output, "small": land_small}
    for group in range(len(CHUNKS)):
        held["proj", group], held["hidden", group] = (grad_proj, proj_sum), (grad_hidden, hidden_sum)
        lands["proj", group], lands["hidden", group] = land_hidden[2 * group : 2 * group + 2]
    used = {}
    units = []
    for number, (name, place, total_place, shape, _) in enumerate(table):
        shelf = lands.get(name, land_attend)
        key = name if name in lands else "attend"
        slot = used.get(key, 0)
        used[key] = slot + 1
        buffer, total = held[name]
        units.append(
            Unit(
                buffer, total, (place, total_place), shape, orders[KINDS[number]], extra, shelf.at[slot],
                (unit_send.at[number], unit_recv.at[number], unit_own.at[number]), me, core,
            )
        )
    ticks = []
    for number, (_, _, _, width) in enumerate(chunks):
        for block in range(blocks):
            name = ("hidden", number) if block == blocks - 1 else ("ffn", (number, block))
            ticks.append((name, FFN_US if width == 256 else 1.57 * FFN_US))
    ticks += [(("back", step), BACK_US) for step in range(pieces)] + [(("output", 0), OUTPUT_US)]
    ticks += [(("attn", step), ATTEND_US) for step in range(3 * pieces)] + [(("free", 0), 0.0)]
    ticks += [(("first", step) if step < pieces - 1 else ("attend", 0), FIRST_US) for step in range(pieces)]
    ticks += [(("last", step) if step < pieces - 1 else ("small", 0), LAST_US) for step in range(pieces)]
    freed = [
        at
        for at, (name, (row, col), _, _, _) in enumerate(table)
        if (name[0] == "proj" and row < frames_in.shape[1]) or (name[0] == "hidden" and col < 384)
    ]
    by_tick, remaining, _ = plan_units(size, ticks, table, freed, 0.0)

    def run(steps):
        for number, stage in steps:
            units[number].advance(stage)

    def tick(step, count, name_of):
        for at in range(count):
            steps = by_tick[name_of(at)]
            if steps:
                @pl.when(step == at)
                def _(steps=steps):
                    run(steps)

    def to_peer(source, target, at):
        return pltpu.make_async_remote_copy(
            src_ref=source, dst_ref=target, send_sem=peer_send.at[at], recv_sem=peer_recv.at[at],
            device_id=(me, 1 - core), device_id_type=MESH_ID,
        )

    def rows_at(step, count):
        return pl.ds(pl.multiple_of(step * count, count), count)

    lane = lax.broadcasted_iota(jnp.int32, (1, PAIR), 1)
    heads = (lane < HD, lane >= HD)
    small[...] = jnp.zeros_like(small)
    packed[...] = jnp.zeros_like(packed)
    grad_proj[...] = jnp.zeros_like(grad_proj)
    grad_hidden[...] = jnp.zeros_like(grad_hidden)

    def add_small(name, value, at=0):
        row = ROW_OF[name]
        index = (slice(row, row + 1), pl.ds(at, value.shape[1]))
        small[index] = small[index] + value

    place = lax.broadcasted_iota(jnp.int32, (total_rows, PAIR), 0)
    column = lax.broadcasted_iota(jnp.int32, (total_rows, PAIR), 1)
    key_terms[...] = jnp.where(
        column == 0, jnp.where(place >= length, masked_value, 0.0), jnp.where(column < 4, 1.0, 0.0)
    ).astype(jnp.bfloat16)
    def normed_block(step):
        first_loads[step].wait()
        unit_rows, _ = center_of(second[pl.ds(step * BLOCK, BLOCK), :].astype(jnp.float32))
        return (unit_rows * gain_one[...] + shift_one[...]).astype(jnp.bfloat16)

    for load in vector_loads:
        load.wait()
    upcoming = normed_block(0)
    for load in weight_loads[9:]:
        load.wait()
    for step in range(blocks):
        first_in = upcoming
        if step < blocks - 1:
            upcoming = normed_block(step + 1)
        if step == blocks - 2:
            for load in later_loads:
                load.start()
        rows = pl.ds(step * BLOCK, BLOCK)
        queries[rows, :] = ((dot(first_in, query_weight[...]) + query_bias[...]) * score_scale).astype(jnp.bfloat16)
        keys[rows, :] = dot(first_in, key_weight[...]).astype(jnp.bfloat16)
        values[rows, :] = (dot(first_in, value_weight[...]) + value_bias[...]).astype(jnp.bfloat16)

    first_term = jnp.where(lax.broadcasted_iota(jnp.int32, (BLOCK, PAIR), 1) == 0, 1.0, 0.0).astype(jnp.bfloat16)
    ones = jnp.ones((total_rows, PAIR), jnp.bfloat16)
    later_loads[0].wait()
    pl.semaphore_wait(barrier, len(dp_bits(size)) + 1)

    @pl.loop(0, blocks)
    def _(step):
        rows = rows_at(step, BLOCK)

        def scores_of(number):
            cols = pl.ds((number // 2) * PAIR, PAIR)
            query_pair = queries[rows, cols]
            query_one = jnp.where(heads[number % 2], query_pair, jnp.zeros_like(query_pair))
            key_all = jnp.concatenate([keys[:, cols], key_terms[...]], axis=1)
            return dot(jnp.concatenate([query_one, first_term], axis=1), key_all, NT)

        mixed = []
        upcoming = scores_of(0)
        for number in range(6):
            scores = scores_of(number) if extra and number else upcoming
            if number < 5 and not extra:
                upcoming = scores_of(number + 1)
            cols = pl.ds((number // 2) * PAIR, PAIR)
            maxima = jnp.max(scores, axis=1, keepdims=True)
            weights = jnp.exp(scores - maxima).astype(jnp.bfloat16)
            mixture = dot(weights, jnp.concatenate([values[:, cols], ones], axis=1))
            totals = mixture[:, PAIR:]
            mixed.append(mixture[:, :PAIR] / totals)
            lse_terms[rows, pl.ds(number * PAIR, PAIR)] = minus_in_three(maxima + jnp.log(totals), 1.0)
            if number % 2:
                attended[rows, cols] = jnp.where(heads[0], mixed[-2], mixed[-1]).astype(jnp.bfloat16)

        right[rows, :] = dot(attended[rows, :], output_weight[...])
        to_peer(right.at[rows, :], left.at[rows, :], step).start()

    for load in later_loads[1:]:
        load.wait()

    def feed_forward(group, step):
        width, count = CHUNKS[group]
        first = sum(chunk_count for _, chunk_count in CHUNKS[:group])
        base = chunks[first][2]
        chunk, block = first + step // blocks, step % blocks
        rows = rows_at(block, BLOCK)
        units_of = pl.ds(pl.multiple_of(base + (step // blocks) * width, 256), width)

        @pl.when(chunk == 0)
        def _():
            to_peer(right.at[rows, :], left.at[rows, :], block).wait()
            for half in range(BLOCK // PIECE):
                part = pl.ds(pl.multiple_of(block * BLOCK + half * PIECE, PIECE), PIECE)
                total = second[part, :].astype(jnp.float32) + (right[part, :] + left[part, :]) + output_bias[...]
                resid[part, :] = total
                left[part, :] = jnp.zeros((PIECE, left.shape[1]), jnp.float32)
                right[part, :] = jnp.zeros((PIECE, left.shape[1]), jnp.float32)
                unit_rows, _ = center_of(total)
                second[part, :] = (unit_rows * gain_two[...] + shift_two[...]).astype(jnp.bfloat16)
                live = lax.broadcasted_iota(jnp.int32, (PIECE, 1), 0) + (block * BLOCK + half * PIECE) < length
                grad_raw = masked[part, :]
                grad_f = jnp.where(live, grad_raw.astype(jnp.float32), 0.0)
                masked[part, :] = grad_f.astype(jnp.bfloat16)
                add_small("proj_bias", column_sum(grad_f))

        up, down = hidden_w[:, units_of], proj_w[units_of, :]
        bias = hidden_bias[units_of].reshape(1, width)
        halves = [
            pl.ds(pl.multiple_of(block * BLOCK + half * PIECE, PIECE), PIECE) for half in range(BLOCK // PIECE)
        ]
        products = [(dot(second[part, :], up) + bias, dot(masked[part, :], down, NT)) for part in halves]
        actives, grads, bias_grad = [], [], 0.0
        for part, (before, grad_active) in zip(halves, products):
            active_f, slope = gelu_parts(before)
            grad_pre = grad_active * slope
            actives.append(active_f.astype(jnp.bfloat16))
            grads.append(grad_pre.astype(jnp.bfloat16))
            bias_grad = bias_grad + column_sum(grad_pre)
            left[part, :] = left[part, :] + dot(actives[-1], down)
            right[part, :] = right[part, :] + dot(grads[-1], up, NT)
        bias_at = (slice(ROW_OF["hidden_bias"], ROW_OF["hidden_bias"] + 1), units_of)
        small[bias_at] = small[bias_at] + bias_grad
        active, grad_pre_b = jnp.concatenate(actives, axis=0), jnp.concatenate(grads, axis=0)
        grad_proj[units_of, :] = grad_proj[units_of, :] + dot(active, masked[rows, :], TN)
        grad_hidden[:, units_of] = grad_hidden[:, units_of] + dot(second[rows, :], grad_pre_b, TN)

        @pl.when(chunk == len(chunks) - 1)
        def _():
            for half in range(BLOCK // PIECE):
                piece = block * (BLOCK // PIECE) + half
                part = rows_at(piece, PIECE)
                to_peer(right.at[part, :], peer_two.at[part, :], blocks + piece).start()
                to_peer(left.at[part, :], peer_mlp.at[part, :], blocks + pieces + piece).start()

        def name_of(at):
            number = first + at // blocks
            return ("hidden", number) if at % blocks == blocks - 1 else ("ffn", (number, at % blocks))

        tick(step, count * blocks, name_of)

    for group, (_, count) in enumerate(CHUNKS):
        pl.loop(0, count * blocks)(functools.partial(feed_forward, group))

    def fetch(source, part, at):
        return pltpu.make_async_copy(source.at[part, :], fetched.at[at], fetch_sem.at[at])

    def store(value, target, part):
        staged[...] = value.astype(jnp.bfloat16)
        copy = pltpu.make_async_copy(staged, target.at[part, :], stage_sem)
        copy.start()
        copy.wait()

    @pl.loop(0, pieces)
    def _(piece):
        part = rows_at(piece, PIECE)
        to_peer(right.at[part, :], peer_two.at[part, :], blocks + piece).wait()
        fetch(peer_two, part, 0).start()
        to_peer(left.at[part, :], peer_mlp.at[part, :], blocks + pieces + piece).wait()
        fetch(peer_mlp, part, 1).start()
        rows_f = resid[part, :]
        unit_rows, inverse = center_of(rows_f)
        fetch(peer_two, part, 0).wait()
        grad_two = right[part, :] + fetched[0]
        grad_rows = masked[part, :].astype(jnp.float32) + norm_back(grad_two, unit_rows, inverse, gain_two[...])
        add_small("norm2_gain", column_sum(grad_two * unit_rows))
        add_small("norm2_bias", column_sum(grad_two))
        add_small("output_bias", column_sum(grad_rows))
        right[part, :] = grad_rows
        grad_b = grad_rows.astype(jnp.bfloat16)
        masked[part, :] = grad_b
        proj_w[part, 0:384] = dot(grad_b, output_weight[...], NT).astype(jnp.bfloat16)
        fetch(peer_mlp, part, 1).wait()
        store(rows_f + (left[part, :] + fetched[1]) + proj_bias[...], block_out, part)
        tick(piece, pieces, lambda at: ("back", at))

    resid[0:384, :] = dot(attended[...], masked[...], TN)
    run(by_tick[("output", 0)])

    again = loads[-1]
    again.start()
    for pair in range(3):
        hidden_w[pair * PAIR : (pair + 1) * PAIR, :] = keys[:, pair * PAIR : (pair + 1) * PAIR].T
    top = lax.broadcasted_iota(jnp.int32, (PAIR, 1), 0) < HD

    @pl.loop(0, 3 * pieces)
    def _(step):
        pair, piece = step // pieces, step % pieces
        part = rows_at(piece, PIECE)
        cols = pl.ds(pl.multiple_of(pair * PAIR, PAIR), PAIR)
        query_pair = queries[part, cols]
        grad_pair = proj_w[part, cols]
        product = grad_pair.astype(jnp.float32) * attended[part, cols].astype(jnp.float32)
        key_all = jnp.concatenate([keys[:, cols], key_terms[...]], axis=1)
        value_all = jnp.concatenate([values[:, cols], ones], axis=1)
        key_rows = hidden_w[cols, :]
        grad_values, grad_keys, grad_queries = 0.0, 0.0, []
        for head in range(2):
            mine = heads[head]
            query_one = jnp.where(mine, query_pair, jnp.zeros_like(query_pair))
            grad_one = jnp.where(mine, grad_pair, jnp.zeros_like(grad_pair))
            delta = jnp.sum(jnp.where(mine, product, 0.0), axis=1, keepdims=True)
            terms = lse_terms[part, pl.ds(pl.multiple_of((2 * pair + head) * PAIR, PAIR), PAIR)]
            probs = jnp.exp(dot(key_all, jnp.concatenate([query_one, terms], axis=1), NT))
            shifted = dot(value_all, jnp.concatenate([grad_one, minus_in_three(delta, 0.0)], axis=1), NT)
            grad_scores = (probs * shifted).astype(jnp.bfloat16)
            grad_values = grad_values + dot(probs.astype(jnp.bfloat16), grad_one)
            grad_keys = grad_keys + dot(grad_scores, query_one)
            grad_queries.append(dot(key_rows, grad_scores))
        grad_query = (jnp.where(top, grad_queries[0], grad_queries[1]) * score_scale).T
        second[part, cols] = grad_query.astype(jnp.bfloat16)
        bias_at = (slice(ROW_OF["query_bias"], ROW_OF["query_bias"] + 1), cols)
        small[bias_at] = small[bias_at] + column_sum(grad_query)

        @pl.when(piece == 0)
        def _():
            left[:, 0:PAIR] = grad_values
            left[:, PAIR : 2 * PAIR] = grad_keys

        @pl.when(piece > 0)
        def _():
            left[:, 0:PAIR] = left[:, 0:PAIR] + grad_values
            left[:, PAIR : 2 * PAIR] = left[:, PAIR : 2 * PAIR] + grad_keys

        @pl.when(piece == pieces - 1)
        def _():
            grad_all = left[:, 0:PAIR]
            bias_at = (slice(ROW_OF["value_bias"], ROW_OF["value_bias"] + 1), cols)
            small[bias_at] = column_sum(grad_all)
            proj_w[:, pl.ds(pl.multiple_of(384 + pair * PAIR, PAIR), PAIR)] = grad_all.astype(jnp.bfloat16)
            second[:, pl.ds(pl.multiple_of(384 + pair * PAIR, PAIR), PAIR)] = left[:, PAIR : 2 * PAIR].astype(
                jnp.bfloat16
            )

        tick(step, 3 * pieces, lambda at: ("attn", at))

    again.wait()
    run(by_tick[("free", 0)])

    @pl.loop(0, pieces)
    def _(piece):
        part = rows_at(piece, PIECE)
        unit_rows, _ = center_of(masked[part, :].astype(jnp.float32))
        first_in = (unit_rows * gain_one[...] + shift_one[...]).astype(jnp.bfloat16)
        grad_query, grad_key = second[part, 0:384], second[part, 384:768]
        grad_value = proj_w[part, 384:768]
        left[part, :] = (
            dot(grad_query, query_weight[...], NT)
            + dot(grad_key, key_weight[...], NT)
            + dot(grad_value, value_weight[...], NT)
        )
        to_peer(left.at[part, :], peer_one.at[part, :], blocks + 2 * pieces + piece).start()
        terms = [dot(first_in, grad, TN) for grad in (grad_query, grad_key, grad_value)]
        width = frames_in.shape[1]
        targets = (
            (grad_proj, (slice(0, width), slice(0, 384))),
            (grad_proj, (slice(0, width), slice(384, 768))),
            (grad_hidden, (slice(0, width), slice(0, 384))),
        )

        @pl.when(piece == 0)
        def _():
            for (ref, index), term in zip(targets, terms):
                ref[index] = term

        @pl.when(piece > 0)
        def _():
            for (ref, index), term in zip(targets, terms):
                ref[index] = ref[index] + term

        tick(piece, pieces, lambda at: ("first", at) if at < pieces - 1 else ("attend", 0))

    @pl.loop(0, pieces)
    def _(piece):
        part = rows_at(piece, PIECE)
        to_peer(left.at[part, :], peer_one.at[part, :], blocks + 2 * pieces + piece).wait()
        fetch(peer_one, part, 0).start()
        unit_rows, inverse = center_of(masked[part, :].astype(jnp.float32))
        fetch(peer_one, part, 0).wait()
        grad_one = left[part, :] + fetched[0]
        add_small("norm1_gain", column_sum(grad_one * unit_rows))
        add_small("norm1_bias", column_sum(grad_one))
        store(right[part, :] + norm_back(grad_one, unit_rows, inverse, gain_one[...]), input_grad, part)

        @pl.when(piece == pieces - 1)
        def _():
            at = 0
            for _, row, count in SMALL:
                for start in range(0, count, 128):
                    packed[at : at + 1, :] = small[row : row + 1, start : start + 128]
                    at += 1

        tick(piece, pieces, lambda at: ("last", at) if at < pieces - 1 else ("small", 0))

    run(remaining)


VMEM_BYTES = 64 * 2**20
FFN_US, BACK_US, OUTPUT_US, ATTEND_US, FIRST_US, LAST_US = 1.823, 1.279, 0.874, 2.702, 2.067, 2.001
RATES = (47489.6, 2.462, 0.1, 4e6)


KINDS = (0, 1, 2, 0, 1, 3, 0, 1, 2, 0, 1, 3, 0, 1, 2, 0, 1, 3, 0, 1, 2, 0, 1, 3, 0, 1, 2, 0, 1, 3, 0, 1, 2, 0, 1, 3, 0)
LATER = (0, 0, 0, 0, 0, 2, 0, 0, 0, -1, 0, 0, -2, 0, 0, -2, 0, 0, -1, -2, 0, -2, 0, -2, 3, 8, 5, 7, -6, -7, -9, -4, -4, -6, 2, -2, 2)


def urgency(item):
    return (item[1] - (-3) * item[2] + LATER[item[1]], item[0])


def on_device(
    size,
    frames,
    lengths,
    cotangent,
    norm1_gain,
    norm1_bias,
    query_weight,
    query_bias,
    key_weight,
    value_weight,
    value_bias,
    output_weight,
    output_bias,
    norm2_gain,
    norm2_bias,
    hidden_weight,
    hidden_bias,
    proj_weight,
    proj_bias,
):
    rows, width = frames.shape[1:]
    part = query_weight.shape[1]
    hidden = hidden_weight.shape[1]
    f32, bf16 = jnp.float32, jnp.bfloat16
    extra = orders_of(size)[1]
    units = len(unit_table())
    chunk_lands = []
    for chunk, count in CHUNKS:
        chunk_lands.append(pltpu.VMEM((3 * count, landing_rows(chunk, extra), 256), f32))
        chunk_lands.append(pltpu.VMEM((3 * count, landing_rows(256, extra), chunk), f32))
    stages = 8 + len(extra)
    pieces = rows // PIECE
    shape = jax.ShapeDtypeStruct
    anywhere = pl.BlockSpec(memory_space=pl.ANY)
    inside = pl.BlockSpec(memory_space=pltpu.VMEM)
    dma = pltpu.SemaphoreType.DMA
    results = pl.pallas_call(
        functools.partial(layer_kernel, size),
        out_shape=[
            shape((rows, width), bf16), shape((rows, width), bf16),
            shape((width, part), f32), shape((width, part), f32), shape((width, part), f32), shape((part, width), f32),
            shape((hidden, width), f32), shape((width, hidden), f32), shape((128, 128), f32),
            shape((rows, width), f32), shape((rows, width), f32), shape((rows, width), f32),
        ],
        in_specs=[pl.BlockSpec(memory_space=pltpu.SMEM)] + [anywhere] * 17,
        out_specs=[anywhere] * 12,
        scratch_shapes=[
            pltpu.VMEM((rows, width), f32), pltpu.VMEM((rows, width), f32), pltpu.VMEM((rows, width), f32),
            pltpu.VMEM((rows, width), bf16), pltpu.VMEM((rows, width), bf16),
            pltpu.VMEM((width, hidden), bf16), pltpu.VMEM((hidden, width), bf16),
            pltpu.VMEM((rows, part), bf16), pltpu.VMEM((rows, part), bf16), pltpu.VMEM((rows, part), bf16),
            pltpu.VMEM((rows, 2 * part), bf16), pltpu.VMEM((rows, part), bf16), pltpu.VMEM((rows, PAIR), bf16),
            pltpu.VMEM((hidden, width), f32), pltpu.VMEM((width, hidden), f32),
            *chunk_lands,
            pltpu.VMEM((9, landing_rows(256, extra), 384), f32),
            pltpu.VMEM((3, landing_rows(384, extra), 256), f32),
            pltpu.VMEM((1, landing_rows(128, extra), 128), f32),
            pltpu.VMEM((2, PIECE, width), f32), pltpu.VMEM((PIECE, width), bf16),
            pltpu.VMEM((16, hidden), f32), pltpu.VMEM((128, 128), f32),
            *[pltpu.VMEM((width, part), bf16)] * 3, pltpu.VMEM((part, width), bf16),
            dma((rows // BLOCK + 17,)), dma((2,)), dma, dma((3 * pieces + rows // BLOCK,)), dma((3 * pieces + rows // BLOCK,)),
            dma((units,)), dma((units, stages)), dma((units,)),
            *[pltpu.VMEM((count,), f32) for count in (width, width, part, part, width, width, width, hidden, width)],
        ],
        compiler_params=pltpu.CompilerParams(
            collective_id=0, has_side_effects=True, vmem_limit_bytes=VMEM_BYTES
        ),
        name="layer",
    )(
        lengths, frames[0], cotangent[0], hidden_weight, proj_weight,
        norm1_gain, norm1_bias, query_bias, value_bias, output_bias,
        norm2_gain, norm2_bias, hidden_bias, proj_bias,
        query_weight, key_weight, value_weight, output_weight,
    )
    block_out, input_grad, query_w, key_w, value_w, output_w, proj_w, hidden_w, packed = results[:9]
    vectors = pl.pallas_call(
        unpack_kernel, out_shape=[shape((count,), f32) for _, _, count in SMALL], name="unpack"
    )(packed)
    small = {name: vector for (name, _, _), vector in zip(SMALL, vectors)}
    return (
        block_out[None], input_grad[None],
        small["norm1_gain"], small["norm1_bias"],
        query_w, small["query_bias"], key_w, value_w, small["value_bias"],
        output_w, small["output_bias"], small["norm2_gain"], small["norm2_bias"],
        hidden_w, small["hidden_bias"], proj_w, small["proj_bias"],
    )


def solution(mesh):
    placed = (
        P("dp", None, None),
        P("dp"),
        P("dp", None, None),
        P(),
        P(),
        P(None, "tensor"),
        P("tensor"),
        P(None, "tensor"),
        P(None, "tensor"),
        P("tensor"),
        P("tensor", None),
        P(),
        P(),
        P(),
        P(None, "tensor"),
        P("tensor"),
        P("tensor", None),
        P(),
    )
    return jax.shard_map(
        functools.partial(on_device, mesh.shape["dp"]),
        mesh=mesh,
        in_specs=placed,
        out_specs=(
            P("dp", None, None),
            P("dp", None, None),
            P(),
            P(),
            P(None, "tensor"),
            P("tensor"),
            P(None, "tensor"),
            P(None, "tensor"),
            P("tensor"),
            P("tensor", None),
            P(),
            P(),
            P(),
            P(None, "tensor"),
            P("tensor"),
            P("tensor", None),
            P(),
        ),
        check_vma=False,
    )
```

```python
import functools
import math

import jax
import jax.numpy as jnp
from jax import lax
from jax.experimental import pallas as pl
from jax.experimental.pallas import tpu as pltpu
from jax.sharding import PartitionSpec as P

HD = 64
PAIR = 2 * HD
CHUNKS = ((256, 2), (512, 2))
BLOCK = 512
PIECE = 256

eps = 1e-05
score_scale = 0.125
masked_value = -1e30

MESH_ID = pl.DeviceIdType.MESH
NN = (((1,), (0,)), ((), ()))
NT = (((1,), (1,)), ((), ()))
TN = (((0,), (0,)), ((), ()))


def dot(left, right, form=NN):
    return lax.dot_general(left, right, form, preferred_element_type=jnp.float32)


def bit_of(index, bit):
    return (index // bit) % 2


def partner_of(index, bit):
    return index + bit - 2 * bit * bit_of(index, bit)


def dp_bits(size):
    return [1 << power for power in range(size.bit_length() - 1)]


def orders_of(size):
    bits = dp_bits(size)
    a, b, c, d = bits[:4]
    orders = [
        [a, b, c, d], [b, a, c, d], [c, a, b, d], [c, b, a, d],
        [a, c, b, d], [b, c, a, d], [c, d, a, b], [c, d, b, a],
    ]
    return orders, bits[4:]


def landing_rows(rows, extra):
    return rows - (rows >> 4) + len(extra) * (rows >> 4)


class Unit:
    def __init__(self, buffer, total, place, shape, order, extra, landing, sems, me, core):
        (self.row, self.col), (self.total_row, self.total_col) = place
        self.rows, self.cols = shape
        self.buffer, self.total, self.landing = buffer, total, landing
        self.order, self.extra = order, extra
        self.send_sem, self.recv_sems, self.own_sem = sems
        self.me, self.core = me, core
        self.offsets = [0]
        self.lands = [0]
        for step, bit in enumerate(order):
            self.offsets.append(self.offsets[-1] + bit_of(me, bit) * (self.rows >> (step + 1)))
            self.lands.append(self.lands[-1] + (self.rows >> (step + 1)))
        self.stages = 2 * len(order) + len(extra)

    def held(self, offset, length):
        return (pl.ds(pl.multiple_of(self.row + offset, 8), length), pl.ds(self.col, self.cols))

    def final(self, offset, length):
        index = (pl.ds(pl.multiple_of(self.total_row + offset, 8), length), pl.ds(self.total_col, self.cols))
        return self.total.at[index]

    def landed(self, start, length):
        return (pl.ds(start, length), pl.ds(0, self.cols))

    def own_copy(self):
        length = self.rows >> len(self.order)
        return pltpu.make_async_copy(
            self.buffer.at[self.held(self.offsets[-1], length)],
            self.final(self.offsets[-1], length),
            self.own_sem,
        )

    def copy(self, stage):
        halvings = len(self.order)
        doublings = len(self.extra)
        if stage < halvings:
            bit = self.order[stage]
            length = self.rows >> (stage + 1)
            away = self.offsets[stage] + (1 - bit_of(self.me, bit)) * length
            source = self.buffer.at[self.held(away, length)]
            target = self.landing.at[self.landed(self.lands[stage], length)]
        elif stage < halvings + doublings:
            bit = self.extra[stage - halvings]
            length = self.rows >> halvings
            source = self.buffer.at[self.held(self.offsets[-1], length)]
            target = self.landing.at[self.landed(self.lands[-1] + (stage - halvings) * length, length)]
        else:
            step = 2 * halvings + doublings - 1 - stage
            bit = self.order[step]
            length = self.rows >> (step + 1)
            target = self.final(self.offsets[step + 1], length)
            source = target
            if step == halvings - 1:
                source = self.buffer.at[self.held(self.offsets[step + 1], length)]
        return pltpu.make_async_remote_copy(
            src_ref=source,
            dst_ref=target,
            send_sem=self.send_sem,
            recv_sem=self.recv_sems.at[stage],
            device_id=(partner_of(self.me, bit), self.core),
            device_id_type=MESH_ID,
        )

    def advance(self, stage):
        halvings = len(self.order)
        doublings = len(self.extra)
        if stage > 0:
            self.copy(stage - 1).wait()
            if stage <= halvings + doublings:
                step = min(stage, halvings)
                length = self.rows >> step
                if stage <= halvings:
                    land = self.lands[stage - 1]
                else:
                    land = self.lands[-1] + (stage - 1 - halvings) * length
                index = self.held(self.offsets[step], length)
                self.buffer[index] = self.buffer[index] + self.landing[self.landed(land, length)]
            if stage == halvings + doublings:
                self.own_copy().start()
            if stage == halvings + doublings + 1:
                self.own_copy().wait()
        if stage < self.stages:
            self.copy(stage).start()


def chunk_list():
    out, base = [], 0
    for group, (width, count) in enumerate(CHUNKS):
        for at in range(count):
            out.append((group, at, base, width))
            base += width
    return out


def unit_table():
    table = []
    for number, (group, _, base, width) in enumerate(chunk_list()):
        for c in range(3):
            place = (base, 256 * c)
            table.append((("proj", group), place, place, (width, 256), ("hidden", number)))
        for c in range(3):
            place = (256 * c, base)
            table.append((("hidden", group), place, place, (256, width), ("hidden", number)))
    for c in range(3):
        table.append(("output", (0, 256 * c), (0, 256 * c), (384, 256), ("output", 0)))
    for name, col in (("query", 0), ("key", 384), ("value", 0)):
        for c in range(3):
            table.append((name, (256 * c, col), (256 * c, 0), (256, 384), ("attend", 0)))
    table.append(("small", (0, 0), (0, 0), (128, 128), ("small", 0)))
    return table


def plan_units(size, ticks, table, freed, start):
    orders, extra = orders_of(size)
    bits = dp_bits(size)
    rate, delay, step_cost, add_rate = RATES
    spots = range(4)
    busy = {}

    def messages(number):
        _, _, _, (rows, cols), _ = table[number]
        order = orders[KINDS[number]]
        down = [(bit, (rows >> (step + 1)) * cols * 4) for step, bit in enumerate(order)]
        across = [(bit, (rows >> len(order)) * cols * 4) for bit in extra]
        return down + across + down[::-1], len(down) + len(across)

    def arrival(message, now):
        bit, length = message
        takes, latest = length / rate, now
        for spot in spots:
            if bit == bits[2]:
                path = [(min(spot, spot ^ 1), spot % 2)]
            elif bit == bits[3]:
                path = [(at, 0) for at in range(spot, spot + 2)] if spot < 2 else [
                    (at, 1) for at in range(spot - 1, spot - 3, -1)
                ]
            else:
                path = [(bit, spot)]
            begin = now
            for link in path:
                key = (len(path) == 1 and bit != bits[2], link)
                begin = max(busy.get(key, 0.0), begin)
                busy[key] = begin + takes
                latest = max(latest, begin + takes)
        return latest + delay

    plans = [messages(number) for number in range(len(table))]
    waiting = []

    def take(item, now, steps):
        waiting.remove(item)
        _, number, stage = item
        sent, downs = plans[number]
        now += step_cost
        if 0 < stage <= downs:
            now += sent[stage - 1][1] / add_rate
        steps.append((number, stage))
        if stage < len(sent):
            waiting.append((arrival(sent[stage], now), number, stage + 1))
        return now

    def run_ready(now, steps):
        while True:
            ready = [item for item in waiting if item[0] <= now]
            if not ready:
                return now
            now = take(min(ready, key=urgency), now, steps)

    by_tick = {}
    now = start
    for name, takes in ticks:
        steps = by_tick[name] = []
        now += takes
        waiting.extend((now, number, 0) for number, entry in enumerate(table) if entry[4] == name)
        if name == ("free", 0):
            for item in sorted(waiting):
                while item[1] in freed and item[2] <= 5 + len(extra):
                    now = take(item, max(now, item[0]), steps)
                    item = waiting[-1]
        now = run_ready(now, steps)
    left = []
    while waiting:
        now = run_ready(max(now, min(waiting)[0]), left)
    return by_tick, left, now


def center_of(rows):
    center = rows - jnp.mean(rows, axis=-1, keepdims=True)
    inverse = lax.rsqrt(jnp.mean(center * center, axis=-1, keepdims=True) + eps)
    return center * inverse, inverse


def norm_back(grad_rows, unit_rows, inverse, norm_gain):
    scaled = grad_rows * norm_gain
    return inverse * (
        scaled
        - jnp.mean(scaled, axis=-1, keepdims=True)
        - unit_rows * jnp.mean(scaled * unit_rows, axis=-1, keepdims=True)
    )


def gelu_parts(before):
    normal_cdf = 0.5 * (1.0 + lax.erf(before * (1.0 / math.sqrt(2.0))))
    slope = normal_cdf + before * jnp.exp(-0.5 * before * before) * (1.0 / math.sqrt(2.0 * math.pi))
    return before * normal_cdf, slope


def column_sum(rows):
    return jnp.sum(rows, axis=0, keepdims=True)


def minus_in_three(column, first):
    lane = lax.broadcasted_iota(jnp.int32, (column.shape[0], PAIR), 1)
    high = (-column).astype(jnp.bfloat16).astype(jnp.float32)
    rest = -column - high
    middle = rest.astype(jnp.bfloat16).astype(jnp.float32)
    low = rest - middle
    zero = jnp.zeros((column.shape[0], PAIR), jnp.float32)
    tail = jnp.where(lane == 1, high, jnp.where(lane == 2, middle, jnp.where(lane == 3, low, zero)))
    return jnp.where(lane == 0, first, tail).astype(jnp.bfloat16)


class Row:
    def __init__(self, ref):
        self.ref = ref

    def __getitem__(self, _):
        return self.ref[...].reshape(1, self.ref.shape[0])


SMALL = (("norm1_gain", 0, 768), ("norm1_bias", 1, 768), ("query_bias", 2, 384), ("value_bias", 3, 384),
         ("output_bias", 4, 768), ("norm2_gain", 5, 768), ("norm2_bias", 6, 768), ("hidden_bias", 7, 1536),
         ("proj_bias", 8, 768))
ROW_OF = {name: row for name, row, _ in SMALL}


def unpack_kernel(packed, *vectors):
    at = 0
    for (_, _, count), vector in zip(SMALL, vectors):
        rows = count // 128
        vector[...] = packed[at : at + rows, :].reshape(count)
        at += rows


def layer_kernel(size, length_ref, *refs):
    (
        frames_in, cotangent_in, hidden_weight_in, proj_weight_in,
        *vectors_in,
        query_weight_in, key_weight_in, value_weight_in, output_weight_in,
    ) = refs[:17]
    vectors = refs[-9:]
    gain_one, shift_one, query_bias, value_bias, output_bias, gain_two, shift_two, hidden_bias, proj_bias = vectors
    (
        block_out, input_grad, query_sum, key_sum, value_sum, output_sum, proj_sum, hidden_sum, small_sum,
        peer_mlp, peer_two, peer_one,
    ) = refs[17:29]
    gain_one, shift_one, query_bias, value_bias, output_bias, gain_two, shift_two, proj_bias = (
        Row(ref) for ref in (gain_one, shift_one, query_bias, value_bias, output_bias, gain_two, shift_two, proj_bias)
    )
    (
        left, right, resid, second, masked, hidden_w, proj_w, queries, keys, values, log_sums, attended, key_terms,
        grad_proj, grad_hidden, *land_hidden, land_attend, land_output, land_small,
        fetched, staged, small, packed, query_weight, key_weight, value_weight, output_weight,
        load_sems, fetch_sem, stage_sem, peer_send, peer_recv, unit_send, unit_recv, unit_own,
    ) = refs[29:-9]
    me, core = lax.axis_index("dp"), lax.axis_index("tensor")
    total_rows = frames_in.shape[0]
    blocks, pieces = total_rows // BLOCK, total_rows // PIECE
    length = length_ref[0]
    orders, extra = orders_of(size)
    chunks = chunk_list()
    table = unit_table()

    pairs = [
        (frames_in.at[pl.ds(block * BLOCK, BLOCK), :], second.at[pl.ds(block * BLOCK, BLOCK), :])
        for block in range(blocks)
    ]
    pairs += [
        (query_weight_in, query_weight), (key_weight_in, key_weight), (value_weight_in, value_weight),
        (output_weight_in, output_weight), (cotangent_in, masked), (hidden_weight_in, hidden_w),
        (proj_weight_in, proj_w), (frames_in, masked),
    ]
    loads = [
        pltpu.make_async_copy(source, target, load_sems.at[at]) for at, (source, target) in enumerate(pairs)
    ]
    first_loads, weight_loads, later_loads = loads[:blocks], loads[blocks : blocks + 3], loads[blocks + 3 : -1]
    vector_loads = [
        pltpu.make_async_copy(source, target, load_sems.at[len(pairs) + at])
        for at, (source, target) in enumerate(zip(vectors_in, vectors))
    ]
    weight_loads = vector_loads + weight_loads
    for load in vector_loads + first_loads[:1] + weight_loads[9:] + first_loads[1:]:
        load.start()
    barrier = pltpu.get_barrier_semaphore()
    for bit in dp_bits(size):
        pl.semaphore_signal(barrier, inc=1, device_id=(partner_of(me, bit), core), device_id_type=MESH_ID)
    pl.semaphore_signal(barrier, inc=1, device_id=(me, 1 - core), device_id_type=MESH_ID)

    held = {
        "output": (resid, output_sum),
        "query": (grad_proj, query_sum), "key": (grad_proj, key_sum),
        "value": (grad_hidden, value_sum), "small": (packed, small_sum),
    }
    lands = {"output": land_output, "small": land_small}
    for group in range(len(CHUNKS)):
        held["proj", group], held["hidden", group] = (grad_proj, proj_sum), (grad_hidden, hidden_sum)
        lands["proj", group], lands["hidden", group] = land_hidden[2 * group : 2 * group + 2]
    used = {}
    units = []
    for number, (name, place, total_place, shape, _) in enumerate(table):
        shelf = lands.get(name, land_attend)
        key = name if name in lands else "attend"
        slot = used.get(key, 0)
        used[key] = slot + 1
        buffer, total = held[name]
        units.append(
            Unit(
                buffer, total, (place, total_place), shape, orders[KINDS[number]], extra, shelf.at[slot],
                (unit_send.at[number], unit_recv.at[number], unit_own.at[number]), me, core,
            )
        )
    ticks = []
    for number, (_, _, _, width) in enumerate(chunks):
        for block in range(blocks):
            name = ("hidden", number) if block == blocks - 1 else ("ffn", (number, block))
            ticks.append((name, FFN_US if width == 256 else 1.57 * FFN_US))
    ticks += [(("back", step), BACK_US) for step in range(pieces)] + [(("output", 0), OUTPUT_US)]
    ticks += [(("attn", step), ATTEND_US) for step in range(3 * pieces)] + [(("free", 0), 0.0)]
    ticks += [(("first", step) if step < pieces - 1 else ("attend", 0), FIRST_US) for step in range(pieces)]
    ticks += [(("last", step) if step < pieces - 1 else ("small", 0), LAST_US) for step in range(pieces)]
    freed = [
        at
        for at, (name, (row, col), _, _, _) in enumerate(table)
        if (name[0] == "proj" and row < frames_in.shape[1]) or (name[0] == "hidden" and col < 384)
    ]
    by_tick, remaining, _ = plan_units(size, ticks, table, freed, 0.0)

    def run(steps):
        for number, stage in steps:
            units[number].advance(stage)

    def tick(step, count, name_of):
        for at in range(count):
            steps = by_tick[name_of(at)]
            if steps:
                @pl.when(step == at)
                def _(steps=steps):
                    run(steps)

    def to_peer(source, target, at):
        return pltpu.make_async_remote_copy(
            src_ref=source, dst_ref=target, send_sem=peer_send.at[at], recv_sem=peer_recv.at[at],
            device_id=(me, 1 - core), device_id_type=MESH_ID,
        )

    def rows_at(step, count):
        return pl.ds(pl.multiple_of(step * count, count), count)

    lane = lax.broadcasted_iota(jnp.int32, (1, PAIR), 1)
    heads = (lane < HD, lane >= HD)
    small[...] = jnp.zeros_like(small)
    packed[...] = jnp.zeros_like(packed)
    grad_proj[...] = jnp.zeros_like(grad_proj)
    grad_hidden[...] = jnp.zeros_like(grad_hidden)

    def add_small(name, value, at=0):
        row = ROW_OF[name]
        index = (slice(row, row + 1), pl.ds(at, value.shape[1]))
        small[index] = small[index] + value

    place = lax.broadcasted_iota(jnp.int32, (total_rows, PAIR), 0)
    column = lax.broadcasted_iota(jnp.int32, (total_rows, PAIR), 1)
    key_terms[...] = jnp.where(
        column == 0, jnp.where(place >= length, masked_value, 0.0), jnp.where(column < 4, 1.0, 0.0)
    ).astype(jnp.bfloat16)
    def normed_block(step):
        first_loads[step].wait()
        unit_rows, _ = center_of(second[pl.ds(step * BLOCK, BLOCK), :].astype(jnp.float32))
        return (unit_rows * gain_one[...] + shift_one[...]).astype(jnp.bfloat16)

    for load in vector_loads:
        load.wait()
    upcoming = normed_block(0)
    for load in weight_loads[9:]:
        load.wait()
    for step in range(blocks):
        first_in = upcoming
        if step < blocks - 1:
            upcoming = normed_block(step + 1)
        if step == blocks - 2:
            for load in later_loads:
                load.start()
        rows = pl.ds(step * BLOCK, BLOCK)
        queries[rows, :] = ((dot(first_in, query_weight[...]) + query_bias[...]) * score_scale).astype(jnp.bfloat16)
        keys[rows, :] = dot(first_in, key_weight[...]).astype(jnp.bfloat16)
        values[rows, :] = (dot(first_in, value_weight[...]) + value_bias[...]).astype(jnp.bfloat16)

    first_term = jnp.where(lax.broadcasted_iota(jnp.int32, (BLOCK, PAIR), 1) == 0, 1.0, 0.0).astype(jnp.bfloat16)
    ones = jnp.ones((total_rows, PAIR), jnp.bfloat16)
    later_loads[0].wait()
    pl.semaphore_wait(barrier, len(dp_bits(size)) + 1)

    @pl.loop(0, blocks)
    def _(step):
        rows = rows_at(step, BLOCK)

        def scores_of(number):
            cols = pl.ds((number // 2) * PAIR, PAIR)
            query_pair = queries[rows, cols]
            query_one = jnp.where(heads[number % 2], query_pair, jnp.zeros_like(query_pair))
            key_all = jnp.concatenate([keys[:, cols], key_terms[...]], axis=1)
            return dot(jnp.concatenate([query_one, first_term], axis=1), key_all, NT)

        mixed = []
        all_maxima = jnp.zeros((BLOCK, PAIR), jnp.float32)
        all_totals = jnp.ones((BLOCK, PAIR), jnp.float32)
        upcoming = scores_of(0)
        for number in range(6):
            scores = scores_of(number) if extra and number else upcoming
            if number < 5 and not extra:
                upcoming = scores_of(number + 1)
            cols = pl.ds((number // 2) * PAIR, PAIR)
            maxima = jnp.max(scores, axis=1, keepdims=True)
            weights = jnp.exp(scores - maxima).astype(jnp.bfloat16)
            mixture = dot(weights, jnp.concatenate([values[:, cols], ones], axis=1))
            totals = mixture[:, PAIR:]
            mixed.append(mixture[:, :PAIR] / totals)
            all_maxima = jnp.where(lane == number, maxima, all_maxima)
            all_totals = jnp.where(lane == number, totals, all_totals)
            if number % 2:
                attended[rows, cols] = jnp.where(heads[0], mixed[-2], mixed[-1]).astype(jnp.bfloat16)

        log_sums[rows, :] = all_maxima + jnp.log(all_totals)
        right[rows, :] = dot(attended[rows, :], output_weight[...])
        to_peer(right.at[rows, :], left.at[rows, :], step).start()

    for load in later_loads[1:]:
        load.wait()

    def feed_forward(group, step):
        width, count = CHUNKS[group]
        first = sum(chunk_count for _, chunk_count in CHUNKS[:group])
        base = chunks[first][2]
        chunk, block = first + step // blocks, step % blocks
        rows = rows_at(block, BLOCK)
        units_of = pl.ds(pl.multiple_of(base + (step // blocks) * width, 256), width)

        @pl.when(chunk == 0)
        def _():
            to_peer(right.at[rows, :], left.at[rows, :], block).wait()
            for half in range(BLOCK // PIECE):
                part = pl.ds(pl.multiple_of(block * BLOCK + half * PIECE, PIECE), PIECE)
                total = second[part, :].astype(jnp.float32) + (right[part, :] + left[part, :]) + output_bias[...]
                resid[part, :] = total
                left[part, :] = jnp.zeros((PIECE, left.shape[1]), jnp.float32)
                right[part, :] = jnp.zeros((PIECE, left.shape[1]), jnp.float32)
                unit_rows, _ = center_of(total)
                second[part, :] = (unit_rows * gain_two[...] + shift_two[...]).astype(jnp.bfloat16)
                live = lax.broadcasted_iota(jnp.int32, (PIECE, 1), 0) + (block * BLOCK + half * PIECE) < length
                grad_raw = masked[part, :]
                grad_f = jnp.where(live, grad_raw.astype(jnp.float32), 0.0)
                masked[part, :] = grad_f.astype(jnp.bfloat16)
                add_small("proj_bias", column_sum(grad_f))

        up, down = hidden_w[:, units_of], proj_w[units_of, :]
        bias = hidden_bias[units_of].reshape(1, width)
        halves = [
            pl.ds(pl.multiple_of(block * BLOCK + half * PIECE, PIECE), PIECE) for half in range(BLOCK // PIECE)
        ]
        products = [(dot(second[part, :], up) + bias, dot(masked[part, :], down, NT)) for part in halves]
        actives, grads, bias_grad = [], [], 0.0
        for part, (before, grad_active) in zip(halves, products):
            active_f, slope = gelu_parts(before)
            grad_pre = grad_active * slope
            actives.append(active_f.astype(jnp.bfloat16))
            grads.append(grad_pre.astype(jnp.bfloat16))
            bias_grad = bias_grad + column_sum(grad_pre)
            left[part, :] = left[part, :] + dot(actives[-1], down)
            right[part, :] = right[part, :] + dot(grads[-1], up, NT)
        bias_at = (slice(ROW_OF["hidden_bias"], ROW_OF["hidden_bias"] + 1), units_of)
        small[bias_at] = small[bias_at] + bias_grad
        active, grad_pre_b = jnp.concatenate(actives, axis=0), jnp.concatenate(grads, axis=0)
        grad_proj[units_of, :] = grad_proj[units_of, :] + dot(active, masked[rows, :], TN)
        grad_hidden[:, units_of] = grad_hidden[:, units_of] + dot(second[rows, :], grad_pre_b, TN)

        @pl.when(chunk == len(chunks) - 1)
        def _():
            for half in range(BLOCK // PIECE):
                piece = block * (BLOCK // PIECE) + half
                part = rows_at(piece, PIECE)
                to_peer(right.at[part, :], peer_two.at[part, :], blocks + piece).start()
                to_peer(left.at[part, :], peer_mlp.at[part, :], blocks + pieces + piece).start()

        def name_of(at):
            number = first + at // blocks
            return ("hidden", number) if at % blocks == blocks - 1 else ("ffn", (number, at % blocks))

        tick(step, count * blocks, name_of)

    for group, (_, count) in enumerate(CHUNKS):
        pl.loop(0, count * blocks)(functools.partial(feed_forward, group))

    def fetch(source, part, at):
        return pltpu.make_async_copy(source.at[part, :], fetched.at[at], fetch_sem.at[at])

    def store(value, target, part):
        staged[...] = value.astype(jnp.bfloat16)
        copy = pltpu.make_async_copy(staged, target.at[part, :], stage_sem)
        copy.start()
        copy.wait()

    @pl.loop(0, pieces)
    def _(piece):
        part = rows_at(piece, PIECE)
        to_peer(right.at[part, :], peer_two.at[part, :], blocks + piece).wait()
        fetch(peer_two, part, 0).start()
        to_peer(left.at[part, :], peer_mlp.at[part, :], blocks + pieces + piece).wait()
        fetch(peer_mlp, part, 1).start()
        rows_f = resid[part, :]
        unit_rows, inverse = center_of(rows_f)
        fetch(peer_two, part, 0).wait()
        grad_two = right[part, :] + fetched[0]
        grad_rows = masked[part, :].astype(jnp.float32) + norm_back(grad_two, unit_rows, inverse, gain_two[...])
        add_small("norm2_gain", column_sum(grad_two * unit_rows))
        add_small("norm2_bias", column_sum(grad_two))
        add_small("output_bias", column_sum(grad_rows))
        right[part, :] = grad_rows
        grad_b = grad_rows.astype(jnp.bfloat16)
        masked[part, :] = grad_b
        proj_w[part, 0:384] = dot(grad_b, output_weight[...], NT).astype(jnp.bfloat16)
        fetch(peer_mlp, part, 1).wait()
        store(rows_f + (left[part, :] + fetched[1]) + proj_bias[...], block_out, part)
        tick(piece, pieces, lambda at: ("back", at))

    resid[0:384, :] = dot(attended[...], masked[...], TN)
    run(by_tick[("output", 0)])

    again = loads[-1]
    again.start()
    for pair in range(3):
        hidden_w[pair * PAIR : (pair + 1) * PAIR, :] = keys[:, pair * PAIR : (pair + 1) * PAIR].T
    top = lax.broadcasted_iota(jnp.int32, (PAIR, 1), 0) < HD

    @pl.loop(0, 3 * pieces)
    def _(step):
        pair, piece = step // pieces, step % pieces
        part = rows_at(piece, PIECE)
        cols = pl.ds(pl.multiple_of(pair * PAIR, PAIR), PAIR)
        query_pair = queries[part, cols]
        grad_pair = proj_w[part, cols]
        product = grad_pair.astype(jnp.float32) * attended[part, cols].astype(jnp.float32)
        key_all = jnp.concatenate([keys[:, cols], key_terms[...]], axis=1)
        value_all = jnp.concatenate([values[:, cols], ones], axis=1)
        key_rows = hidden_w[cols, :]
        grad_values, grad_keys, grad_queries = 0.0, 0.0, []
        for head in range(2):
            mine = heads[head]
            query_one = jnp.where(mine, query_pair, jnp.zeros_like(query_pair))
            grad_one = jnp.where(mine, grad_pair, jnp.zeros_like(grad_pair))
            delta = jnp.sum(jnp.where(mine, product, 0.0), axis=1, keepdims=True)
            log_sum = jnp.sum(jnp.where(lane == 2 * pair + head, log_sums[part, :], 0.0), axis=1, keepdims=True)
            terms = minus_in_three(log_sum, 1.0)
            probs = jnp.exp(dot(key_all, jnp.concatenate([query_one, terms], axis=1), NT))
            shifted = dot(value_all, jnp.concatenate([grad_one, minus_in_three(delta, 0.0)], axis=1), NT)
            grad_scores = (probs * shifted).astype(jnp.bfloat16)
            grad_values = grad_values + dot(probs.astype(jnp.bfloat16), grad_one)
            grad_keys = grad_keys + dot(grad_scores, query_one)
            grad_queries.append(dot(key_rows, grad_scores))
        grad_query = (jnp.where(top, grad_queries[0], grad_queries[1]) * score_scale).T
        second[part, cols] = grad_query.astype(jnp.bfloat16)
        bias_at = (slice(ROW_OF["query_bias"], ROW_OF["query_bias"] + 1), cols)
        small[bias_at] = small[bias_at] + column_sum(grad_query)

        @pl.when(piece == 0)
        def _():
            left[:, 0:PAIR] = grad_values
            left[:, PAIR : 2 * PAIR] = grad_keys

        @pl.when(piece > 0)
        def _():
            left[:, 0:PAIR] = left[:, 0:PAIR] + grad_values
            left[:, PAIR : 2 * PAIR] = left[:, PAIR : 2 * PAIR] + grad_keys

        @pl.when(piece == pieces - 1)
        def _():
            grad_all = left[:, 0:PAIR]
            bias_at = (slice(ROW_OF["value_bias"], ROW_OF["value_bias"] + 1), cols)
            small[bias_at] = column_sum(grad_all)
            proj_w[:, pl.ds(pl.multiple_of(384 + pair * PAIR, PAIR), PAIR)] = grad_all.astype(jnp.bfloat16)
            second[:, pl.ds(pl.multiple_of(384 + pair * PAIR, PAIR), PAIR)] = left[:, PAIR : 2 * PAIR].astype(
                jnp.bfloat16
            )

        tick(step, 3 * pieces, lambda at: ("attn", at))

    again.wait()
    run(by_tick[("free", 0)])

    @pl.loop(0, pieces)
    def _(piece):
        part = rows_at(piece, PIECE)
        unit_rows, _ = center_of(masked[part, :].astype(jnp.float32))
        first_in = (unit_rows * gain_one[...] + shift_one[...]).astype(jnp.bfloat16)
        grad_query, grad_key = second[part, 0:384], second[part, 384:768]
        grad_value = proj_w[part, 384:768]
        left[part, :] = (
            dot(grad_query, query_weight[...], NT)
            + dot(grad_key, key_weight[...], NT)
            + dot(grad_value, value_weight[...], NT)
        )
        to_peer(left.at[part, :], peer_one.at[part, :], blocks + 2 * pieces + piece).start()
        terms = [dot(first_in, grad, TN) for grad in (grad_query, grad_key, grad_value)]
        width = frames_in.shape[1]
        targets = (
            (grad_proj, (slice(0, width), slice(0, 384))),
            (grad_proj, (slice(0, width), slice(384, 768))),
            (grad_hidden, (slice(0, width), slice(0, 384))),
        )

        @pl.when(piece == 0)
        def _():
            for (ref, index), term in zip(targets, terms):
                ref[index] = term

        @pl.when(piece > 0)
        def _():
            for (ref, index), term in zip(targets, terms):
                ref[index] = ref[index] + term

        tick(piece, pieces, lambda at: ("first", at) if at < pieces - 1 else ("attend", 0))

    @pl.loop(0, pieces)
    def _(piece):
        part = rows_at(piece, PIECE)
        to_peer(left.at[part, :], peer_one.at[part, :], blocks + 2 * pieces + piece).wait()
        fetch(peer_one, part, 0).start()
        unit_rows, inverse = center_of(masked[part, :].astype(jnp.float32))
        fetch(peer_one, part, 0).wait()
        grad_one = left[part, :] + fetched[0]
        add_small("norm1_gain", column_sum(grad_one * unit_rows))
        add_small("norm1_bias", column_sum(grad_one))
        store(right[part, :] + norm_back(grad_one, unit_rows, inverse, gain_one[...]), input_grad, part)

        @pl.when(piece == pieces - 1)
        def _():
            at = 0
            for _, row, count in SMALL:
                for start in range(0, count, 128):
                    packed[at : at + 1, :] = small[row : row + 1, start : start + 128]
                    at += 1

        tick(piece, pieces, lambda at: ("last", at) if at < pieces - 1 else ("small", 0))

    run(remaining)


VMEM_BYTES = 64 * 2**20
FFN_US, BACK_US, OUTPUT_US, ATTEND_US, FIRST_US, LAST_US = 1.812, 1.279, 0.871, 2.702, 2.118, 2.117
RATES = (47496.7, 2.386, 0.1, 4e6)


KINDS = (0, 1, 2, 0, 1, 3, 0, 1, 2, 0, 1, 3, 0, 1, 2, 0, 1, 3, 0, 1, 2, 0, 1, 3, 0, 1, 2, 0, 1, 3, 0, 1, 2, 0, 1, 3, 0)
LATER = (0, -1, 0, 0, -3, 3, 0, 0, 3, -1, 0, 0, -2, 0, 0, -2, 0, 0, 1, 0, 0, -2, 1, 3, 1, 1, 0, 7, -3, -1, -6, 5, -4, -8, 8, -4, 0)


def urgency(item):
    return (item[1] - (-3) * item[2] + LATER[item[1]], item[0])


def on_device(
    size,
    frames,
    lengths,
    cotangent,
    norm1_gain,
    norm1_bias,
    query_weight,
    query_bias,
    key_weight,
    value_weight,
    value_bias,
    output_weight,
    output_bias,
    norm2_gain,
    norm2_bias,
    hidden_weight,
    hidden_bias,
    proj_weight,
    proj_bias,
):
    rows, width = frames.shape[1:]
    part = query_weight.shape[1]
    hidden = hidden_weight.shape[1]
    f32, bf16 = jnp.float32, jnp.bfloat16
    extra = orders_of(size)[1]
    units = len(unit_table())
    chunk_lands = []
    for chunk, count in CHUNKS:
        chunk_lands.append(pltpu.VMEM((3 * count, landing_rows(chunk, extra), 256), f32))
        chunk_lands.append(pltpu.VMEM((3 * count, landing_rows(256, extra), chunk), f32))
    stages = 8 + len(extra)
    pieces = rows // PIECE
    shape = jax.ShapeDtypeStruct
    anywhere = pl.BlockSpec(memory_space=pl.ANY)
    inside = pl.BlockSpec(memory_space=pltpu.VMEM)
    dma = pltpu.SemaphoreType.DMA
    results = pl.pallas_call(
        functools.partial(layer_kernel, size),
        out_shape=[
            shape((rows, width), bf16), shape((rows, width), bf16),
            shape((width, part), f32), shape((width, part), f32), shape((width, part), f32), shape((part, width), f32),
            shape((hidden, width), f32), shape((width, hidden), f32), shape((128, 128), f32),
            shape((rows, width), f32), shape((rows, width), f32), shape((rows, width), f32),
        ],
        in_specs=[pl.BlockSpec(memory_space=pltpu.SMEM)] + [anywhere] * 17,
        out_specs=[anywhere] * 12,
        scratch_shapes=[
            pltpu.VMEM((rows, width), f32), pltpu.VMEM((rows, width), f32), pltpu.VMEM((rows, width), f32),
            pltpu.VMEM((rows, width), bf16), pltpu.VMEM((rows, width), bf16),
            pltpu.VMEM((width, hidden), bf16), pltpu.VMEM((hidden, width), bf16),
            pltpu.VMEM((rows, part), bf16), pltpu.VMEM((rows, part), bf16), pltpu.VMEM((rows, part), bf16),
            pltpu.VMEM((rows, PAIR), f32), pltpu.VMEM((rows, part), bf16), pltpu.VMEM((rows, PAIR), bf16),
            pltpu.VMEM((hidden, width), f32), pltpu.VMEM((width, hidden), f32),
            *chunk_lands,
            pltpu.VMEM((9, landing_rows(256, extra), 384), f32),
            pltpu.VMEM((3, landing_rows(384, extra), 256), f32),
            pltpu.VMEM((1, landing_rows(128, extra), 128), f32),
            pltpu.VMEM((2, PIECE, width), f32), pltpu.VMEM((PIECE, width), bf16),
            pltpu.VMEM((16, hidden), f32), pltpu.VMEM((128, 128), f32),
            *[pltpu.VMEM((width, part), bf16)] * 3, pltpu.VMEM((part, width), bf16),
            dma((rows // BLOCK + 17,)), dma((2,)), dma, dma((3 * pieces + rows // BLOCK,)), dma((3 * pieces + rows // BLOCK,)),
            dma((units,)), dma((units, stages)), dma((units,)),
            *[pltpu.VMEM((count,), f32) for count in (width, width, part, part, width, width, width, hidden, width)],
        ],
        compiler_params=pltpu.CompilerParams(
            collective_id=0, has_side_effects=True, vmem_limit_bytes=VMEM_BYTES
        ),
        name="layer",
    )(
        lengths, frames[0], cotangent[0], hidden_weight, proj_weight,
        norm1_gain, norm1_bias, query_bias, value_bias, output_bias,
        norm2_gain, norm2_bias, hidden_bias, proj_bias,
        query_weight, key_weight, value_weight, output_weight,
    )
    block_out, input_grad, query_w, key_w, value_w, output_w, proj_w, hidden_w, packed = results[:9]
    vectors = pl.pallas_call(
        unpack_kernel, out_shape=[shape((count,), f32) for _, _, count in SMALL], name="unpack"
    )(packed)
    small = {name: vector for (name, _, _), vector in zip(SMALL, vectors)}
    return (
        block_out[None], input_grad[None],
        small["norm1_gain"], small["norm1_bias"],
        query_w, small["query_bias"], key_w, value_w, small["value_bias"],
        output_w, small["output_bias"], small["norm2_gain"], small["norm2_bias"],
        hidden_w, small["hidden_bias"], proj_w, small["proj_bias"],
    )


def solution(mesh):
    placed = (
        P("dp", None, None),
        P("dp"),
        P("dp", None, None),
        P(),
        P(),
        P(None, "tensor"),
        P("tensor"),
        P(None, "tensor"),
        P(None, "tensor"),
        P("tensor"),
        P("tensor", None),
        P(),
        P(),
        P(),
        P(None, "tensor"),
        P("tensor"),
        P("tensor", None),
        P(),
    )
    return jax.shard_map(
        functools.partial(on_device, mesh.shape["dp"]),
        mesh=mesh,
        in_specs=placed,
        out_specs=(
            P("dp", None, None),
            P("dp", None, None),
            P(),
            P(),
            P(None, "tensor"),
            P("tensor"),
            P(None, "tensor"),
            P(None, "tensor"),
            P("tensor"),
            P("tensor", None),
            P(),
            P(),
            P(),
            P(None, "tensor"),
            P("tensor"),
            P("tensor", None),
            P(),
        ),
        check_vma=False,
    )
```
